512 devices in a mesh: row: 16 (over x, y), col: 32 (over z, core).
Axes of the slice: x: 4, y: 4, z: 16, core: 2. Of those that a mesh axis runs over, the one named last changes fastest.
Arguments:
- object_field: float32 [2, 4096, 8192], P(None, 'row', 'col')
- probe_field: float32 [2, 256, 256], replicated, may hold values from -6 to 6
- object_dir_prev: float32 [2, 4096, 8192], P(None, 'row', 'col')
- probe_dir_prev: float32 [2, 256, 256], replicated, may hold values from -6 to 6
- prev_norm: float32 [], replicated, may hold values from 33554432 to 134217728
- intensities: bfloat16 [16, 32, 4, 256, 256], P('row', 'col'), may hold values from 0 to 1.5
- positions: int32 [16, 32, 4, 2], P('row', 'col'), may hold values from 0 to 8191, as said below
- counts: int32 [16, 32], P('row'), may hold values from 0 to 4, as said below
Outputs:
- object_new: float32 [2, 4096, 8192], P(None, 'row', 'col')
- probe_new: float32 [2, 256, 256], replicated
- object_direction: float32 [2, 4096, 8192], P(None, 'row', 'col')
- probe_direction: float32 [2, 256, 256], replicated
- grad_norm: float32 [], replicated
- frame_curvature: float32 [16, 32, 4], P('row', 'col')
The draws below stay inside these ranges and needn't reach their ends.
Inputs may be any that keep to these rules, and one draw needn't show every extreme that they name: positions[i, j] lie in tile (i, j): rows i * 256 to (i + 1) * 256 - 1 and columns j * 256 to (j + 1) * 256 - 1. The devices of column indices 2 k and 2 k + 1 of one row hold at most 4 live frames together; a device's live slots are its first counts[i, j].
All inputs are finite; a program needn't handle non-finite values.
Results may differ from the reference program's by a relative error of at most 0.0003.
Values sent between devices are 32-bit elements; how exact they have to be, the bound alone decides.
No kernel may reach another device: no remote copies, remote signals or barrier semaphores. Data moves between devices by JAX's collectives and lax.ppermute only.
A program may use at most 64 MiB of HBM per device.

```python
import math
import jax
import jax.numpy as jnp
from jax import lax

WIN = 256
TR = 256
TC = 256
CAP = 4
TILES_R = 16
TILES_C = 32
NR = 4096
NC = 8192
FRAMES = 2048


def ramp_scale(steepness):
    rows_f = lax.broadcasted_iota(jnp.float32, (NR, NC), 0) / NR
    cols_f = lax.broadcasted_iota(jnp.float32, (NR, NC), 1) / NC
    return jnp.exp(steepness * (rows_f - 0.5)) * jnp.exp(steepness * (cols_f - 0.5))


def draw_object_field(key, part):
    key = jax.random.fold_in(key, 11)
    values = 0.5 * jax.random.normal(key, (2, NR, NC), jnp.float32)
    return values * ramp_scale(0.5 * math.log(10.0))[None]


def draw_object_dir_prev(key, part):
    key = jax.random.fold_in(key, 12)
    values = 0.5 * jax.random.normal(key, (2, NR, NC), jnp.float32)
    return values * ramp_scale(0.5 * math.log(10.0))[None]


def draw_positions(key, part):
    key = jax.random.fold_in(key, 13)
    first_key, second_key = jax.random.split(key)
    rows_off = jax.random.randint(first_key, (TILES_R, TILES_C, CAP), 0, TR)
    cols_off = jax.random.randint(second_key, (TILES_R, TILES_C, CAP), 0, TC)
    tile_ids_r = lax.broadcasted_iota(jnp.int32, (TILES_R, TILES_C, CAP), 0)
    tile_ids_c = lax.broadcasted_iota(jnp.int32, (TILES_R, TILES_C, CAP), 1)
    slot_ids = lax.broadcasted_iota(jnp.int32, (TILES_R, TILES_C, CAP), 2)
    first_slot = jnp.logical_and(jnp.logical_and(tile_ids_r == 0, tile_ids_c == 0), slot_ids == 0)
    last_slot = jnp.logical_and(jnp.logical_and(tile_ids_r == TILES_R - 1, tile_ids_c == TILES_C - 1), slot_ids == CAP - 1)
    rows_off = jnp.where(first_slot, 0, jnp.where(last_slot, TR - 1, rows_off))
    cols_off = jnp.where(first_slot, 0, jnp.where(last_slot, TC - 1, cols_off))
    return jnp.stack([rows_off + tile_ids_r * TR, cols_off + tile_ids_c * TC], axis=-1).astype(jnp.int32)


def draw_counts(key, part):
    key = jax.random.fold_in(key, 14)
    keys = jax.random.split(key, 5)
    pairs_row = TILES_C // 2
    totals = jax.random.randint(keys[0], (TILES_R, pairs_row), CAP - 1, CAP + 1)
    firsts = jax.random.randint(keys[1], (TILES_R, pairs_row), 0, totals + 1)
    full_row = jax.random.randint(keys[2], (), 0, TILES_R)
    full_pair = jax.random.randint(keys[3], (), 0, pairs_row)
    flipped = jax.random.randint(keys[4], (), 0, 2)
    row_ids = lax.broadcasted_iota(jnp.int32, (TILES_R, pairs_row), 0)
    pair_ids = lax.broadcasted_iota(jnp.int32, (TILES_R, pairs_row), 1)
    chosen = jnp.logical_and(row_ids == full_row, pair_ids == full_pair)
    totals = jnp.where(chosen, CAP, totals)
    firsts = jnp.where(chosen, flipped * CAP, firsts)
    return jnp.stack([firsts, totals - firsts], axis=-1).reshape(TILES_R, TILES_C).astype(jnp.int32)


def block_levels(key, dims, cuts, smallest, high):
    factor_of, own = 1.0, jax.random.fold_in(key, 6)
    for dim, shards_of in cuts:
        heights = jnp.exp(jax.random.uniform(jax.random.fold_in(own, dim), (shards_of,), jnp.float32, smallest / len(cuts), high / len(cuts)))
        factor_of = factor_of * jnp.repeat(heights, dims[dim] // shards_of).reshape([-1 if axis == dim else 1 for axis in range(len(dims))])
    return factor_of


def gaussian(key, dims, scale, most, held_as=jnp.bfloat16):
    return jnp.clip(scale * jax.random.normal(key, dims, jnp.float32), -most, most).astype(held_as)


def setup_inputs(seed: int = 0) -> dict:
    key_list = jax.random.split(jax.random.key(seed), 9)
    object_field = draw_object_field(jax.random.fold_in(key_list[8], 71), 0)
    probe_field = gaussian(key_list[1], (2, WIN, WIN), 0.7, 6.0, jnp.float32)
    object_dir_prev = draw_object_dir_prev(jax.random.fold_in(key_list[8], 71), 0)
    probe_dir_prev = gaussian(key_list[3], (2, WIN, WIN), 0.5, 6.0, jnp.float32)
    prev_norm = jnp.clip(jnp.exp(jax.random.uniform(key_list[4], (), jnp.float32, math.log(33554432), math.log(134217728))), 33554432, 134217728)
    intensities = jnp.clip(1.5 * jax.random.uniform(key_list[5], (TILES_R, TILES_C, CAP, WIN, WIN), jnp.float32) ** block_levels(key_list[5], (TILES_R, TILES_C, CAP, WIN, WIN), ((0, 16), (1, 32)), -0.2, 0.2), 0.0, 1.5).astype(jnp.bfloat16)
    positions = draw_positions(jax.random.fold_in(key_list[8], 71), 0)
    counts = draw_counts(jax.random.fold_in(key_list[8], 71), 0)
    return {"object_field": object_field, "probe_field": probe_field, "object_dir_prev": object_dir_prev, "probe_dir_prev": probe_dir_prev, "prev_norm": prev_norm, "intensities": intensities, "positions": positions, "counts": counts}


def unitary_transform(real_part, imag_part, inverse):
    joined = lax.complex(real_part, imag_part)
    if inverse:
        result = jnp.fft.ifft2(joined) * WIN
    else:
        result = jnp.fft.fft2(joined) / WIN
    return (jnp.real(result), jnp.imag(result))

def reference(object_field, probe_field, object_dir_prev, probe_dir_prev, prev_norm, intensities, positions, counts):
    real_type = object_field.dtype
    probe_scale = 1.0 / math.sqrt(FRAMES)
    padded = jnp.pad(object_field, ((0, 0), (0, WIN), (0, WIN)))
    corners = positions.reshape(-1, 2)
    measured = intensities.reshape(-1, WIN, WIN)
    slot_ids = jnp.arange(CAP, dtype=jnp.int32)
    live_mask = (slot_ids[None, None, :] < counts[:, :, None]).reshape(-1)

    def window(source, corner):
        return lax.dynamic_slice(source, (jnp.int32(0), corner[0], corner[1]), (2, WIN, WIN))

    def exit_wave(corner, keep_slot):
        patches = window(padded, corner)
        wave_r = jnp.where(keep_slot, probe_field[0] * patches[0] - probe_field[1] * patches[1], 0.0)
        wave_i = jnp.where(keep_slot, probe_field[0] * patches[1] + probe_field[1] * patches[0], 0.0)
        return (patches, wave_r, wave_i)

    def grad_step(carried, record):
        grad_pad, probe_acc = carried
        corner, measure, keep_slot = record
        patches, wave_r, wave_i = exit_wave(corner, keep_slot)
        far_r, far_i = unitary_transform(wave_r, wave_i, False)
        residue = far_r * far_r + far_i * far_i - jnp.where(keep_slot, measure.astype(far_r.dtype), 0.0)
        back_r, back_i = unitary_transform(residue * far_r, residue * far_i, True)
        obj_r = probe_field[0] * back_r + probe_field[1] * back_i
        obj_i = probe_field[0] * back_i - probe_field[1] * back_r
        anchor = (jnp.int32(0), corner[0], corner[1])
        before = lax.dynamic_slice(grad_pad, anchor, (2, WIN, WIN))
        grad_pad = lax.dynamic_update_slice(grad_pad, before + jnp.stack([obj_r, obj_i]), anchor)
        probe_r = patches[0] * back_r + patches[1] * back_i
        probe_i = patches[0] * back_i - patches[1] * back_r
        return ((grad_pad, probe_acc + jnp.stack([probe_r, probe_i])), None)
    initial = (jnp.zeros_like(padded), jnp.zeros_like(probe_field))
    (grad_pad, probe_acc), unused = lax.scan(grad_step, initial, (corners, measured, live_mask))
    object_grad = grad_pad[:, :NR, :NC]
    probe_grad = probe_acc * probe_scale
    grad_norm = jnp.sum(object_grad * object_grad) + jnp.sum(probe_grad * probe_grad)
    along_prev = jnp.sum(object_grad * object_dir_prev) + jnp.sum(probe_grad * probe_dir_prev)
    conj_ratio = grad_norm / prev_norm
    object_direction = -object_grad + conj_ratio * object_dir_prev
    probe_direction = -probe_grad + conj_ratio * probe_dir_prev
    descent = grad_norm - conj_ratio * along_prev
    dir_pad = jnp.pad(object_direction, ((0, 0), (0, WIN), (0, WIN)))

    def curve_step(running, record):
        corner, keep_slot = record
        patches, wave_r, wave_i = exit_wave(corner, keep_slot)
        dir_patch = window(dir_pad, corner)
        step_r = probe_field[0] * dir_patch[0] - probe_field[1] * dir_patch[1] + probe_direction[0] * patches[0] - probe_direction[1] * patches[1]
        step_i = probe_field[0] * dir_patch[1] + probe_field[1] * dir_patch[0] + probe_direction[0] * patches[1] + probe_direction[1] * patches[0]
        step_r = jnp.where(keep_slot, step_r, 0.0)
        step_i = jnp.where(keep_slot, step_i, 0.0)
        far_r, far_i = unitary_transform(wave_r, wave_i, False)
        dfar_r, dfar_i = unitary_transform(step_r, step_i, False)
        quad_term = 2.0 * (far_r * dfar_r + far_i * dfar_i)
        frame_sum = jnp.sum(quad_term * quad_term)
        return (running + frame_sum, frame_sum)
    curvature, frame_sums = lax.scan(curve_step, jnp.zeros((), real_type), (corners, live_mask))
    frame_curvature = (frame_sums / (WIN * WIN)).reshape(TILES_R, TILES_C, CAP)
    step_size = descent / (0.5 * curvature + 1e-06)
    return (object_field + step_size * object_direction, probe_field + step_size * probe_direction, object_direction, probe_direction, grad_norm, frame_curvature)
```

```python
import math

import jax
import jax.numpy as jnp
from jax import lax
from jax.sharding import PartitionSpec as P


def passed_along(shard, axis, by):
    count = lax.axis_size(axis)
    pairs = [(i, i + by) for i in range(count) if 0 <= i + by < count]
    return lax.ppermute(shard, axis, pairs)


def summed_pieces(whole, axis):
    count = lax.axis_size(axis)
    pieces = whole.reshape((count, whole.shape[0] // count) + whole.shape[1:])
    return jnp.sum(lax.all_to_all(pieces, axis, 0, 0), axis=0)


def gathered_pieces(piece, axis):
    count = lax.axis_size(axis)
    copies = jnp.broadcast_to(piece[None], (count,) + piece.shape)
    return lax.all_to_all(copies, axis, 0, 0)


def summed_scalars(values):
    row = jnp.zeros((1, 128), jnp.float32)
    for at, value in enumerate(values):
        row = row.at[0, at].set(value)
    row = jnp.sum(gathered_pieces(row, "row"), axis=0)
    row = jnp.sum(gathered_pieces(row, "col"), axis=0)
    return [row[0, at] for at in range(len(values))]


def summed_probe(part):
    flat = part.reshape(-1, part.shape[-1])
    piece = summed_pieces(summed_pieces(flat, "row"), "col")
    piece = gathered_pieces(piece, "col").reshape(-1, part.shape[-1])
    return gathered_pieces(piece, "row").reshape(part.shape)


def dft_tables(frame_width):
    rows_i = lax.broadcasted_iota(jnp.int32, (frame_width, frame_width), 0)
    cols_i = lax.broadcasted_iota(jnp.int32, (frame_width, frame_width), 1)
    phases = (rows_i * cols_i % frame_width).astype(jnp.float32) * (2.0 * math.pi / frame_width)
    factor = 1.0 / math.sqrt(frame_width)
    return (jnp.cos(phases) * factor, jnp.sin(phases) * factor)


def unitary_dft(frames, cosine, sine_table, orient):
    precise = lax.Precision.HIGHEST
    left_c = jnp.einsum("jk,bckl->bcjl", cosine, frames, precision=precise)
    left_s = jnp.einsum("jk,bckl->bcjl", sine_table, frames, precision=precise)
    middle = jnp.stack(
        [left_c[:, 0] + orient * left_s[:, 1], left_c[:, 1] - orient * left_s[:, 0]], axis=1
    )
    right_c = jnp.einsum("bcjk,kl->bcjl", middle, cosine, precision=precise)
    right_s = jnp.einsum("bcjk,kl->bcjl", middle, sine_table, precision=precise)
    return jnp.stack(
        [right_c[:, 0] + orient * right_s[:, 1], right_c[:, 1] - orient * right_s[:, 0]], axis=1
    )


def complex_times(left, right):
    real_out = left[..., 0, :, :] * right[..., 0, :, :] - left[..., 1, :, :] * right[..., 1, :, :]
    imag_out = left[..., 0, :, :] * right[..., 1, :, :] + left[..., 1, :, :] * right[..., 0, :, :]
    return jnp.stack([real_out, imag_out], axis=-3)


def conj_times(left, right):
    real_out = left[..., 0, :, :] * right[..., 0, :, :] + left[..., 1, :, :] * right[..., 1, :, :]
    imag_out = left[..., 0, :, :] * right[..., 1, :, :] - left[..., 1, :, :] * right[..., 0, :, :]
    return jnp.stack([real_out, imag_out], axis=-3)


def extend_object(tile_vals):
    lower_rim = passed_along(tile_vals, "row", -1)
    stacked = jnp.concatenate([tile_vals, lower_rim], axis=1)
    right_rim = passed_along(stacked, "col", -1)
    return jnp.concatenate([stacked, right_rim], axis=2)


def extend_direction(tile_vals):
    lower_rim = passed_along(tile_vals, "row", -1)
    stacked = jnp.concatenate([tile_vals, lower_rim], axis=1)
    right_rim = passed_along(stacked, "col", -1)
    return jnp.concatenate([stacked, right_rim], axis=2)


def fold_back(spread, tile_rows, tile_cols, frame_width):
    from_left = passed_along(spread[:, :, tile_cols:], "col", 1)
    owned = spread[:, :, :tile_cols].at[:, :, :frame_width].add(from_left)
    from_above = passed_along(owned[:, tile_rows:, :], "row", 1)
    return owned[:, :tile_rows, :].at[:, :frame_width, :].add(from_above)


def cut_patches(extended, offsets_r, offsets_c, frame_width):

    def one_patch(row_off, col_off):
        return lax.dynamic_slice(extended, (0, row_off, col_off), (2, frame_width, frame_width))

    return jax.vmap(one_patch)(offsets_r, offsets_c)


def accumulate(contrib, offsets_r, offsets_c, grid_shape):

    def add_one(slot_at, grid):
        piece = contrib[slot_at]
        anchor = (0, offsets_r[slot_at], offsets_c[slot_at])
        current = lax.dynamic_slice(grid, anchor, piece.shape)
        return lax.dynamic_update_slice(grid, current + piece, anchor)

    return lax.fori_loop(0, contrib.shape[0], add_one, jnp.zeros(grid_shape, jnp.float32))


def gradient_frames(waves, measure, cosine, sine_table):
    far_field = unitary_dft(waves, cosine, sine_table, 1.0)
    residue = far_field[:, 0] * far_field[:, 0] + far_field[:, 1] * far_field[:, 1] - measure
    backward = unitary_dft(far_field * residue[:, None], cosine, sine_table, -1.0)
    return (backward, far_field)


def per_device(
    object_field,
    probe_field,
    object_dir_prev,
    probe_dir_prev,
    prev_norm,
    intensities,
    positions,
    counts,
):
    tile_rows = object_field.shape[1]
    tile_cols = object_field.shape[2]
    frame_width = probe_field.shape[-1]
    slot_count = positions.shape[2]
    row_at = lax.axis_index("row")
    col_at = lax.axis_index("col")
    cosine, sine_table = dft_tables(frame_width)
    offsets_r = positions[0, 0, :, 0] - row_at * tile_rows
    offsets_c = positions[0, 0, :, 1] - col_at * tile_cols
    row_counts = counts[0]
    own_count = lax.dynamic_index_in_dim(row_counts, col_at, 0, keepdims=False)
    slot_ids = jnp.arange(slot_count, dtype=jnp.int32)
    live_mask = (slot_ids < own_count).astype(jnp.float32)
    extended = extend_object(object_field)
    patches = cut_patches(extended, offsets_r, offsets_c, frame_width)
    waves = complex_times(probe_field, patches) * live_mask[:, None, None, None]
    measure = intensities[0, 0].astype(jnp.float32) * live_mask[:, None, None]
    backward, far_kept = gradient_frames(waves, measure, cosine, sine_table)
    grid_shape = (2, tile_rows + frame_width, tile_cols + frame_width)
    spread = accumulate(conj_times(probe_field, backward), offsets_r, offsets_c, grid_shape)
    object_grad = fold_back(spread, tile_rows, tile_cols, frame_width)
    probe_part = jnp.sum(conj_times(patches, backward), axis=0)
    scale_probe = 1.0 / math.sqrt(slot_count * lax.axis_size("row") * lax.axis_size("col"))
    obj_square = jnp.sum(object_grad * object_grad)
    obj_along = jnp.sum(object_grad * object_dir_prev)
    probe_total = summed_probe(probe_part)
    products = summed_scalars([obj_square, obj_along])
    probe_grad = probe_total * scale_probe
    grad_norm = products[0] + jnp.sum(probe_grad * probe_grad)
    along_prev = products[1] + jnp.sum(probe_grad * probe_dir_prev)
    conj_ratio = grad_norm / prev_norm
    probe_direction = -probe_grad + conj_ratio * probe_dir_prev
    object_direction = -object_grad + conj_ratio * object_dir_prev
    descent = grad_norm - conj_ratio * along_prev
    dir_extended = extend_direction(object_direction)
    dir_patches = cut_patches(dir_extended, offsets_r, offsets_c, frame_width)
    step_waves = (
        complex_times(probe_field, dir_patches) + complex_times(probe_direction, patches)
    ) * live_mask[:, None, None, None]
    step_far = unitary_dft(step_waves, cosine, sine_table, 1.0)
    quad_term = 2.0 * (far_kept[:, 0] * step_far[:, 0] + far_kept[:, 1] * step_far[:, 1])
    frame_sums = jnp.sum(quad_term * quad_term, axis=(1, 2))
    curvature = summed_scalars([jnp.sum(frame_sums)])[0]
    step_size = descent / (0.5 * curvature + 1e-06)
    frame_curvature = (frame_sums / (frame_width * frame_width)).reshape(1, 1, slot_count)
    return (
        object_field + step_size * object_direction,
        probe_field + step_size * probe_direction,
        object_direction,
        probe_direction,
        grad_norm,
        frame_curvature,
    )


def solution(mesh):
    return jax.shard_map(
        per_device,
        mesh=mesh,
        in_specs=(
            P(None, "row", "col"),
            P(),
            P(None, "row", "col"),
            P(),
            P(),
            P("row", "col", None, None, None),
            P("row", "col", None, None),
            P("row", None),
        ),
        out_specs=(
            P(None, "row", "col"),
            P(),
            P(None, "row", "col"),
            P(),
            P(),
            P("row", "col", None),
        ),
        check_vma=False,
    )
```

```python
import functools
import math

import jax
import jax.numpy as jnp
import numpy as np
from jax import lax
from jax.experimental import pallas as pl
from jax.experimental.pallas import tpu as pltpu
from jax.sharding import PartitionSpec as P

VMEM_BYTES = 48 * 1024 * 1024


def dft_blocks(width):
    at = np.arange(width)
    angle = (np.outer(at, at) % width) * (2.0 * math.pi / width)
    cosine = (np.cos(angle) / math.sqrt(width)).astype(np.float32)
    sine = (np.sin(angle) / math.sqrt(width)).astype(np.float32)

    def thrice(table):
        high = table.astype(jnp.bfloat16)
        low = (table - high.astype(np.float32)).astype(jnp.bfloat16)
        return np.concatenate([high, low, high], axis=1)

    real_rows = np.concatenate([thrice(cosine), thrice(sine)], axis=1)
    imag_rows = np.concatenate([thrice(-sine), thrice(cosine)], axis=1)
    left = np.concatenate([real_rows, imag_rows], axis=0)
    return left, np.ascontiguousarray(left.T)


def split_halves(value):
    high = value.astype(jnp.bfloat16)
    low = (value - high.astype(jnp.float32)).astype(jnp.bfloat16)
    return high, low


def dft_pair(first, second, left_ref, right_ref, tall_ref, wide_ref):
    width = first.shape[0]
    for at, part in enumerate((first, second)):
        high, low = split_halves(part)
        base = 3 * at * width
        tall_ref[base : base + width, :] = high
        tall_ref[base + width : base + 2 * width, :] = high
        tall_ref[base + 2 * width : base + 3 * width, :] = low
    middle = jnp.dot(left_ref[...], tall_ref[...], preferred_element_type=jnp.float32)
    for at in range(2):
        high, low = split_halves(middle[at * width : (at + 1) * width])
        base = 3 * at * width
        wide_ref[:, base : base + width] = high
        wide_ref[:, base + width : base + 2 * width] = high
        wide_ref[:, base + 2 * width : base + 3 * width] = low
    done = jnp.dot(wide_ref[...], right_ref[...], preferred_element_type=jnp.float32)
    return done[:, :width], done[:, width:]


def rolled(value, row, col):
    return pltpu.roll(pltpu.roll(value, row, 0), col, 1)


def wrapped(own, below, right, diag, upper, nearer):
    return jnp.where(nearer, jnp.where(upper, own, below), jnp.where(upper, right, diag))


def masks(row, col, width):
    upper = lax.broadcasted_iota(jnp.int32, (width, width), 0) >= row
    nearer = lax.broadcasted_iota(jnp.int32, (width, width), 1) >= col
    return upper, nearer


def gradient_kernel(
    positions_ref,
    counts_ref,
    own_ref,
    below_ref,
    right_ref,
    diag_ref,
    probe_ref,
    measured_ref,
    dft_left_ref,
    dft_right_ref,
    near_ref,
    side_ref,
    probe_part_ref,
    patch_ref,
    moved_ref,
    far_ref,
    tall_ref,
    wide_ref,
):
    width = probe_ref.shape[-1]
    near_ref[...] = jnp.zeros_like(near_ref)
    side_ref[...] = jnp.zeros_like(side_ref)
    probe_part_ref[...] = jnp.zeros_like(probe_part_ref)

    def frame(slot, carry):
        row = lax.rem(positions_ref[0, 0, slot, 0], width)
        col = lax.rem(positions_ref[0, 0, slot, 1], width)
        upper, nearer = masks(row, col, width)
        for part in range(2):
            patch_ref[slot, part] = wrapped(
                own_ref[part], below_ref[part], right_ref[part], diag_ref[part], upper, nearer
            )
            moved_ref[slot, part] = rolled(probe_ref[part], row, col)
        patch_r, patch_i = patch_ref[slot, 0], patch_ref[slot, 1]
        probe_r, probe_i = moved_ref[slot, 0], moved_ref[slot, 1]
        wave_r = probe_r * patch_r - probe_i * patch_i
        wave_i = probe_r * patch_i + probe_i * patch_r
        far_r, far_i = dft_pair(wave_r, wave_i, dft_left_ref, dft_right_ref, tall_ref, wide_ref)
        far_ref[slot, 0] = far_r
        far_ref[slot, 1] = far_i
        residue = far_r * far_r + far_i * far_i - measured_ref[0, 0, slot].astype(jnp.float32)
        back_i, back_r = dft_pair(
            residue * far_i, residue * far_r, dft_left_ref, dft_right_ref, tall_ref, wide_ref
        )
        patch_r, patch_i = patch_ref[slot, 0], patch_ref[slot, 1]
        probe_r, probe_i = moved_ref[slot, 0], moved_ref[slot, 1]
        back_row = lax.rem(width - row, width)
        back_col = lax.rem(width - col, width)
        probe_part_ref[0] += rolled(patch_r * back_r + patch_i * back_i, back_row, back_col)
        probe_part_ref[1] += rolled(patch_r * back_i - patch_i * back_r, back_row, back_col)
        terms = (probe_r * back_r + probe_i * back_i, probe_r * back_i - probe_i * back_r)
        for part, term in enumerate(terms):
            close = jnp.where(nearer, term, 0.0)
            beyond = term - close
            near_ref[part, :width, :] += jnp.where(upper, close, 0.0)
            near_ref[part, width:, :] += jnp.where(upper, 0.0, close)
            side_ref[part, :width, :] += jnp.where(upper, beyond, 0.0)
            side_ref[part, width:, :] += jnp.where(upper, 0.0, beyond)
        return carry

    lax.fori_loop(0, counts_ref[0, lax.axis_index("col")], frame, 0)


def curvature_kernel(
    positions_ref,
    counts_ref,
    prev_norm_ref,
    gathered_ref,
    g_own_ref,
    g_below_ref,
    g_right_ref,
    d_own_ref,
    d_below_ref,
    d_right_ref,
    probe_prev_ref,
    patch_ref,
    moved_ref,
    far_ref,
    dft_left_ref,
    dft_right_ref,
    direction_ref,
    probe_direction_ref,
    row_ref,
    below_ref,
    right_ref,
    tall_ref,
    wide_ref,
    *,
    probe_scale,
):
    width = gathered_ref.shape[-1]
    depth = gathered_ref.shape[1] - 1
    probe_grad = gathered_ref[:, :depth, :].reshape(probe_prev_ref.shape) * probe_scale
    probe_prev = probe_prev_ref[...]
    products = jnp.sum(gathered_ref[:, depth:, :], axis=0)
    at = lax.broadcasted_iota(jnp.int32, products.shape, 1)
    grad_norm = jnp.sum(jnp.where(at == 0, products, 0.0)) + jnp.sum(probe_grad * probe_grad)
    along_prev = jnp.sum(jnp.where(at == 1, products, 0.0)) + jnp.sum(probe_grad * probe_prev)
    ratio = grad_norm / prev_norm_ref[0]
    descent = grad_norm - ratio * along_prev
    probe_direction_ref[...] = ratio * probe_prev - probe_grad
    direction_ref[...] = ratio * d_own_ref[...] - g_own_ref[...]
    below_ref[...] = ratio * d_below_ref[...] - g_below_ref[...]
    right_ref[...] = ratio * d_right_ref[...] - g_right_ref[...]
    lane = lax.broadcasted_iota(jnp.int32, (1, 128), 1)

    def frame(slot, carry):
        row = lax.rem(positions_ref[0, 0, slot, 0], width)
        col = lax.rem(positions_ref[0, 0, slot, 1], width)
        upper, nearer = masks(row, col, width)
        step_r, step_i = [
            wrapped(
                direction_ref[part],
                below_ref[part],
                right_ref[part, :width],
                right_ref[part, width:],
                upper,
                nearer,
            )
            for part in range(2)
        ]
        patch_r, patch_i = patch_ref[slot, 0], patch_ref[slot, 1]
        probe_r, probe_i = moved_ref[slot, 0], moved_ref[slot, 1]
        change_r = rolled(probe_direction_ref[0], row, col)
        change_i = rolled(probe_direction_ref[1], row, col)
        wave_r = probe_r * step_r - probe_i * step_i + change_r * patch_r - change_i * patch_i
        wave_i = probe_r * step_i + probe_i * step_r + change_r * patch_i + change_i * patch_r
        far_r, far_i = dft_pair(wave_r, wave_i, dft_left_ref, dft_right_ref, tall_ref, wide_ref)
        quad = 2.0 * (far_ref[slot, 0] * far_r + far_ref[slot, 1] * far_i)
        frame_sum = jnp.sum(quad * quad)
        return carry + jnp.where((lane == 0) | (lane == slot + 1), frame_sum, 0.0)

    row = lax.fori_loop(0, counts_ref[0, lax.axis_index("col")], frame, jnp.zeros((1, 128), jnp.float32))
    row_ref[...] = jnp.where(lane == 5, grad_norm, jnp.where(lane == 6, descent, row))


def shaped(*dims):
    return jax.ShapeDtypeStruct(dims, jnp.float32)


def in_vmem(count):
    return [pl.BlockSpec(memory_space=pltpu.VMEM)] * count


def in_smem(count):
    return [pl.BlockSpec(memory_space=pltpu.SMEM)] * count


def scratch_for(width):
    return [
        pltpu.VMEM((6 * width, width), jnp.bfloat16),
        pltpu.VMEM((width, 6 * width), jnp.bfloat16),
    ]


def gradient_call(positions, counts, tiles, probe, measured, tables):
    width = probe.shape[-1]
    slots = measured.shape[2]
    return pl.pallas_call(
        gradient_kernel,
        out_shape=(
            shaped(2, 2 * width, width),
            shaped(2, 2 * width, width),
            shaped(2, width, width),
            shaped(slots, 2, width, width),
            shaped(slots, 2, width, width),
            shaped(slots, 2, width, width),
        ),
        in_specs=in_smem(2) + in_vmem(8),
        out_specs=tuple(in_vmem(6)),
        scratch_shapes=scratch_for(width),
        compiler_params=pltpu.CompilerParams(vmem_limit_bytes=VMEM_BYTES),
        cost_estimate=pl.CostEstimate(flops=10**10, bytes_accessed=10**7, transcendentals=0),
        name="gradient_frames",
    )(positions, counts, *tiles, probe, measured, *tables)


def curvature_call(positions, counts, prev_norm, gathered, tiles, probe_prev, kept, tables, probe_scale):
    width = gathered.shape[-1]
    return pl.pallas_call(
        functools.partial(curvature_kernel, probe_scale=probe_scale),
        out_shape=(shaped(2, width, width), shaped(2, width, width), shaped(1, 128)),
        in_specs=in_smem(3) + in_vmem(13),
        out_specs=tuple(in_vmem(3)),
        scratch_shapes=[
            pltpu.VMEM((2, width, width), jnp.float32),
            pltpu.VMEM((2, 2 * width, width), jnp.float32),
        ]
        + scratch_for(width),
        compiler_params=pltpu.CompilerParams(vmem_limit_bytes=VMEM_BYTES),
        cost_estimate=pl.CostEstimate(flops=5 * 10**9, bytes_accessed=10**7, transcendentals=0),
        name="curvature_frames",
    )(positions, counts, prev_norm, gathered, *tiles, probe_prev, *kept, *tables)


def passed_along(shard, axis, by):
    count = lax.axis_size(axis)
    pairs = [(i, i + by) for i in range(count) if 0 <= i + by < count]
    return lax.ppermute(shard, axis, pairs)


def summed_pieces(whole, axis):
    count = lax.axis_size(axis)
    pieces = whole.reshape((count, whole.shape[0] // count) + whole.shape[1:])
    return jnp.sum(lax.all_to_all(pieces, axis, 0, 0), axis=0)


def gathered_pieces(piece, axis):
    count = lax.axis_size(axis)
    copies = jnp.broadcast_to(piece[None], (count,) + piece.shape)
    return lax.all_to_all(copies, axis, 0, 0)


def held(value, *others):
    return lax.optimization_barrier((value,) + others)[0]


def stacked_rows(upper, lower):
    return jnp.concatenate([upper, lower], axis=1)


def per_device(
    object_field,
    probe_field,
    object_dir_prev,
    probe_dir_prev,
    prev_norm,
    intensities,
    positions,
    counts,
):
    width = probe_field.shape[-1]
    slots = positions.shape[2]
    tables = dft_blocks(width)
    probe_scale = 1.0 / math.sqrt(slots * lax.axis_size("row") * lax.axis_size("col"))

    below = passed_along(object_field, "row", -1)
    right = passed_along(object_field, "col", -1)
    below = held(below, right)
    diag = passed_along(below, "col", -1)
    prev_below = passed_along(held(object_dir_prev, below), "row", -1)
    diag = held(diag, prev_below)
    prev_right = passed_along(stacked_rows(object_dir_prev, prev_below), "col", -1)

    near, side, probe_part, *kept = gradient_call(
        positions, counts, (object_field, below, right, diag), probe_field, intensities, tables
    )
    probe_part = held(probe_part, prev_right)
    from_left = passed_along(side, "col", 1)
    piece = summed_pieces(probe_part.reshape(-1, width), "row")
    owned = near + held(from_left, piece)
    from_above = passed_along(owned[:, width:], "row", 1)
    piece = summed_pieces(held(piece, owned), "col")
    object_grad = owned[:, :width] + held(from_above, piece)
    grad_below = passed_along(object_grad, "row", -1)
    lane = lax.broadcasted_iota(jnp.int32, (1, width), 1)
    square = jnp.sum(object_grad * object_grad)
    along = jnp.sum(object_grad * object_dir_prev)
    products = jnp.where(lane == 0, square, jnp.where(lane == 1, along, 0.0))
    pieces = gathered_pieces(jnp.concatenate([piece, products], axis=0), "col")
    products = jnp.sum(pieces[:, 1], axis=0)[None]
    grad_column = stacked_rows(object_grad, held(grad_below, pieces))
    grad_right = passed_along(grad_column, "col", -1)
    piece = jnp.concatenate([pieces[:, 0], products], axis=0)
    gathered = gathered_pieces(held(piece, grad_column), "row")
    grad_right = held(grad_right, gathered)

    object_direction, probe_direction, row = curvature_call(
        positions,
        counts,
        prev_norm.reshape(1),
        gathered,
        (object_grad, grad_below, grad_right, object_dir_prev, prev_below, prev_right),
        probe_dir_prev,
        kept,
        tables,
        probe_scale,
    )
    across = jnp.sum(gathered_pieces(row, "row"), axis=0)
    across = jnp.sum(gathered_pieces(across, "col"), axis=0)
    step_size = row[0, 6] / (0.5 * across[0, 0] + 1e-06)
    frame_curvature = (row[0, 1 : 1 + slots] / (width * width)).reshape(1, 1, slots)
    return (
        object_field + step_size * object_direction,
        probe_field + step_size * probe_direction,
        object_direction,
        probe_direction,
        row[0, 5],
        frame_curvature,
    )


def solution(mesh):
    return jax.shard_map(
        per_device,
        mesh=mesh,
        in_specs=(
            P(None, "row", "col"),
            P(),
            P(None, "row", "col"),
            P(),
            P(),
            P("row", "col", None, None, None),
            P("row", "col", None, None),
            P("row", None),
        ),
        out_specs=(
            P(None, "row", "col"),
            P(),
            P(None, "row", "col"),
            P(),
            P(),
            P("row", "col", None),
        ),
        check_vma=False,
    )
```

```python
import functools
import math

import jax
import jax.numpy as jnp
import numpy as np
from jax import lax
from jax.experimental import pallas as pl
from jax.experimental.pallas import tpu as pltpu
from jax.sharding import PartitionSpec as P

VMEM_BYTES = 60 * 1024 * 1024


def dft_blocks(width):
    at = np.arange(width)
    angle = (np.outer(at, at) % width) * (2.0 * math.pi / width)
    cosine = (np.cos(angle) / math.sqrt(width)).astype(np.float32)
    sine = (np.sin(angle) / math.sqrt(width)).astype(np.float32)

    def thrice(table):
        high = table.astype(jnp.bfloat16)
        low = (table - high.astype(np.float32)).astype(jnp.bfloat16)
        return np.concatenate([high, low, high], axis=1)

    real_rows = np.concatenate([thrice(cosine), thrice(sine)], axis=1)
    imag_rows = np.concatenate([thrice(-sine), thrice(cosine)], axis=1)
    left = np.concatenate([real_rows, imag_rows], axis=0)
    return left, np.ascontiguousarray(left.T)


def split_halves(value):
    high = value.astype(jnp.bfloat16)
    low = (value - high.astype(jnp.float32)).astype(jnp.bfloat16)
    return high, low


def dft_pairs(pairs, tables, scratch):
    left_ref, right_ref = tables
    tall_ref, wide_ref = scratch
    width = pairs[0][0].shape[0]
    for which, pair in enumerate(pairs):
        for at, part in enumerate(pair):
            high, low = split_halves(part)
            base = 3 * at * width
            tall_ref[which, base : base + width, :] = high
            tall_ref[which, base + width : base + 2 * width, :] = high
            tall_ref[which, base + 2 * width : base + 3 * width, :] = low
    results = []
    left_ref = left_ref()
    for which in range(len(pairs)):
        middle = jnp.dot(left_ref[...], tall_ref[which], preferred_element_type=jnp.float32)
        for at in range(2):
            high, low = split_halves(middle[at * width : (at + 1) * width])
            base = 3 * at * width
            wide_ref[which, :, base : base + width] = high
            wide_ref[which, :, base + width : base + 2 * width] = high
            wide_ref[which, :, base + 2 * width : base + 3 * width] = low
    right_ref = right_ref()
    for which in range(len(pairs)):
        done = jnp.dot(wide_ref[which], right_ref[...], preferred_element_type=jnp.float32)
        results.append((done[:, :width], done[:, width:]))
    return results


def rolled(value, row, col):
    return pltpu.roll(pltpu.roll(value, row, 0), col, 1)


def wrapped(own, below, right, diag, upper, nearer):
    return jnp.where(nearer, jnp.where(upper, own, below), jnp.where(upper, right, diag))


def masks(row, col, width):
    upper = lax.broadcasted_iota(jnp.int32, (width, width), 0) >= row
    nearer = lax.broadcasted_iota(jnp.int32, (width, width), 1) >= col
    return upper, nearer


def corner(positions_ref, slot, width):
    row = lax.rem(positions_ref[0, 0, slot, 0], width)
    col = lax.rem(positions_ref[0, 0, slot, 1], width)
    return row, col


def live_count(counts_ref):
    return counts_ref[0, lax.axis_index("col")]


class Incoming:
    def __init__(self, source, target, semaphore):
        self.target = target
        self.copy = pltpu.make_async_copy(source, target, semaphore)
        self.copy.start()
        self.waiting = True

    def __call__(self):
        if self.waiting:
            self.copy.wait()
            self.waiting = False
        return self.target


def incoming(sources, targets, semaphores):
    return [
        Incoming(source, target, semaphores.at[at])
        for at, (source, target) in enumerate(zip(sources, targets))
    ]


def outgoing(sources, targets, semaphores, first=0):
    sent = [
        pltpu.make_async_copy(source, target, semaphores.at[first + at])
        for at, (source, target) in enumerate(zip(sources, targets))
    ]
    for copy in sent:
        copy.start()
    return sent


def gradient_kernel(
    positions_ref,
    counts_ref,
    own_any,
    below_any,
    right_any,
    diag_any,
    probe_any,
    measured_any,
    left_any,
    right_table_any,
    own_grad_any,
    below_grad_any,
    right_grad_any,
    diag_grad_any,
    probe_grad_any,
    patch_any,
    moved_any,
    far_any,
    tiles_ref,
    probe_ref,
    measured_ref,
    left_ref,
    right_ref,
    grads_ref,
    patch_ref,
    moved_ref,
    far_ref,
    tall_ref,
    wide_ref,
    in_sems,
    out_sems,
):
    width = probe_ref.shape[-1]
    live = live_count(counts_ref)
    *ready, left, measured, right = incoming(
        [own_any, below_any, right_any, diag_any, probe_any]
        + [left_any, measured_any.at[0, 0], right_table_any],
        [tiles_ref.at[at] for at in range(4)] + [probe_ref, left_ref, measured_ref, right_ref],
        in_sems,
    )
    for arrival in ready:
        arrival()

    def both(first):
        slots = (first, first + 1)
        spots = [corner(positions_ref, slot, width) for slot in slots]
        waves = []
        for slot, (row, col) in zip(slots, spots):
            upper, nearer = masks(row, col, width)
            for part in range(2):
                patch_ref[slot, part] = wrapped(
                    *[tiles_ref[at, part] for at in range(4)], upper, nearer
                )
                moved_ref[slot, part] = rolled(probe_ref[part], row, col)
            patch_r, patch_i = patch_ref[slot, 0], patch_ref[slot, 1]
            probe_r, probe_i = moved_ref[slot, 0], moved_ref[slot, 1]
            kept = slot < live
            waves.append(
                (
                    jnp.where(kept, probe_r * patch_r - probe_i * patch_i, 0.0),
                    jnp.where(kept, probe_r * patch_i + probe_i * patch_r, 0.0),
                )
            )
        span = pl.ds(first, 2)
        sent = outgoing(
            [patch_ref.at[span], moved_ref.at[span]],
            [patch_any.at[span], moved_any.at[span]],
            out_sems,
            5 + 3 * (first // 2),
        )
        fars = dft_pairs(waves, (left, right), (tall_ref, wide_ref))
        turned = []
        measured()
        for slot, (far_r, far_i) in zip(slots, fars):
            far_ref[slot, 0] = far_r
            far_ref[slot, 1] = far_i
            residue = far_r * far_r + far_i * far_i - measured_ref[slot].astype(jnp.float32)
            turned.append((residue * far_i, residue * far_r))
        sent += outgoing(
            [far_ref.at[span]], [far_any.at[span]], out_sems, 7 + 3 * (first // 2)
        )
        backs = dft_pairs(turned, (left, right), (tall_ref, wide_ref))
        pieces = []
        for slot, (row, col), (back_i, back_r) in zip(slots, spots, backs):
            patch_r, patch_i = patch_ref[slot, 0], patch_ref[slot, 1]
            back_row = lax.rem(width - row, width)
            back_col = lax.rem(width - col, width)
            pieces.append(
                (
                    rolled(patch_r * back_r + patch_i * back_i, back_row, back_col),
                    rolled(patch_r * back_i - patch_i * back_r, back_row, back_col),
                )
            )
        for part in range(2):
            total = pieces[0][part] + pieces[1][part]
            grads_ref[4, part] = total if first == 0 else grads_ref[4, part] + total
        for part in range(2):
            sums = [0.0, 0.0, 0.0, 0.0]
            for slot, (row, col), (back_i, back_r) in zip(slots, spots, backs):
                upper, nearer = masks(row, col, width)
                probe_r, probe_i = moved_ref[slot, 0], moved_ref[slot, 1]
                if part == 0:
                    term = probe_r * back_r + probe_i * back_i
                else:
                    term = probe_r * back_i - probe_i * back_r
                close = jnp.where(nearer, term, 0.0)
                beyond = term - close
                for at, side in enumerate((close, beyond)):
                    top = jnp.where(upper, side, 0.0)
                    sums[2 * at] = sums[2 * at] + top
                    sums[2 * at + 1] = sums[2 * at + 1] + (side - top)
            for at, total in enumerate(sums):
                grads_ref[at, part] = total if first == 0 else grads_ref[at, part] + total
        for copy in sent:
            copy.wait()

    both(0)
    pl.when(live > 2)(lambda: both(2))
    outs = [own_grad_any, below_grad_any, right_grad_any, diag_grad_any, probe_grad_any]
    for copy in outgoing([grads_ref.at[at] for at in range(5)], outs, out_sems):
        copy.wait()


def linear_frames(positions_ref, live, tiles, change, kept, tables, scratch, finish):
    own_ref, below_ref, right_ref, diag_ref = [tile() for tile in tiles]
    change_ref = change()
    width = own_ref.shape[-1]

    def both(first, patches, moves, fars):
        slots = (first, first + 1)
        patch_ref, moved_ref = patches(), moves()
        waves = []
        for at, slot in enumerate(slots):
            row, col = corner(positions_ref, slot, width)
            upper, nearer = masks(row, col, width)
            step_r, step_i = [
                wrapped(own_ref[part], below_ref[part], right_ref[part], diag_ref[part], upper, nearer)
                for part in range(2)
            ]
            patch_r, patch_i = patch_ref[at, 0], patch_ref[at, 1]
            probe_r, probe_i = moved_ref[at, 0], moved_ref[at, 1]
            change_r = rolled(change_ref[0], row, col)
            change_i = rolled(change_ref[1], row, col)
            waves.append(
                (
                    probe_r * step_r - probe_i * step_i + change_r * patch_r - change_i * patch_i,
                    probe_r * step_i + probe_i * step_r + change_r * patch_i + change_i * patch_r,
                )
            )
        steps = dft_pairs(waves, tables, scratch)
        far_ref = fars()
        quads = [
            2.0 * (far_ref[at, 0] * step_r + far_ref[at, 1] * step_i)
            for at, (step_r, step_i) in enumerate(steps)
        ]
        finish(slots, quads)

    both(0, *kept[0])
    for arrival in kept[1]:
        arrival()
    pl.when(live > 2)(lambda: both(2, *kept[1]))


def halves(array, ref):
    return [(array.at[pl.ds(first, 2)], ref.at[pl.ds(first, 2)]) for first in (0, 2)]


def previous_kernel(
    positions_ref,
    counts_ref,
    own_any,
    below_any,
    right_any,
    diag_any,
    change_any,
    patch_any,
    moved_any,
    far_any,
    left_any,
    right_table_any,
    quad_any,
    sums_ref,
    tiles_ref,
    change_ref,
    patch_ref,
    moved_ref,
    far_ref,
    left_ref,
    right_ref,
    quad_ref,
    tall_ref,
    wide_ref,
    in_sems,
    out_sem,
):
    live = live_count(counts_ref)
    kept = [
        halves(patch_any, patch_ref),
        halves(moved_any, moved_ref),
        halves(far_any, far_ref),
    ]
    moves = [(change_any, change_ref)]
    moves += [
        (tile, tiles_ref.at[at]) for at, tile in enumerate((own_any, below_any, right_any, diag_any))
    ]
    moves += [kept[0][0], kept[1][0], (left_any, left_ref), (right_table_any, right_ref), kept[2][0]]
    moves += [kept[0][1], kept[1][1], kept[2][1]]
    change, *arrivals = incoming(*zip(*moves), in_sems)
    tiles, (patch, moved, left, right, far), later = arrivals[:4], arrivals[4:9], arrivals[9:]
    lane = lax.broadcasted_iota(jnp.int32, (1, 128), 1)
    sums_ref[...] = jnp.zeros_like(sums_ref)

    def finish(slots, quads):
        row = sums_ref[...]
        for slot, quad in zip(slots, quads):
            quad_ref[slot] = quad
            square = jnp.sum(quad * quad)
            row = row + jnp.where((lane == 2) | (lane == 16 + slot), square, 0.0)
        sums_ref[...] = row

    linear_frames(
        positions_ref,
        live,
        tiles,
        change,
        ((patch, moved, far), later),
        (left, right),
        (tall_ref, wide_ref),
        finish,
    )
    copy = pltpu.make_async_copy(quad_ref, quad_any, out_sem)
    copy.start()
    copy.wait()


def curvature_kernel(
    positions_ref,
    counts_ref,
    own_any,
    below_any,
    right_any,
    diag_any,
    total_any,
    patch_any,
    moved_any,
    far_any,
    left_any,
    right_table_any,
    prev_any,
    quad_any,
    prev_sums_ref,
    prev_probe_any,
    sums_ref,
    change_any,
    tiles_ref,
    total_ref,
    change_ref,
    patch_ref,
    moved_ref,
    far_ref,
    left_ref,
    right_ref,
    quad_ref,
    prev_ref,
    prev_probe_ref,
    tall_ref,
    wide_ref,
    in_sems,
    out_sem,
    *,
    probe_scale,
):
    live = live_count(counts_ref)
    kept = [
        halves(patch_any, patch_ref),
        halves(moved_any, moved_ref),
        halves(far_any, far_ref),
    ]
    moves = [(total_any, total_ref)]
    moves += [
        (tile, tiles_ref.at[at]) for at, tile in enumerate((own_any, below_any, right_any, diag_any))
    ]
    moves += [kept[0][0], kept[1][0], (left_any, left_ref), (right_table_any, right_ref), kept[2][0]]
    moves += [kept[0][1], kept[1][1], kept[2][1]]
    moves += [(quad_any, quad_ref), (prev_any, prev_ref), (prev_probe_any, prev_probe_ref)]
    total, *arrivals = incoming(*zip(*moves), in_sems)
    tiles, (patch, moved, left, right, far), later = arrivals[:4], arrivals[4:9], arrivals[9:12]
    quad_in, prev, prev_probe = arrivals[12:]
    change_ref[...] = total()[...].reshape(change_ref.shape) * probe_scale
    copy = pltpu.make_async_copy(change_ref, change_any, out_sem)
    copy.start()
    lane = lax.broadcasted_iota(jnp.int32, (1, 128), 1)
    sums_ref[...] = prev_sums_ref[...]

    def finish(slots, quads):
        quad_in()
        row = sums_ref[...]
        for slot, quad in zip(slots, quads):
            square = jnp.sum(quad * quad)
            cross = jnp.sum(quad * quad_ref[slot])
            row = row + jnp.where((lane == 0) | (lane == 8 + slot), square, 0.0)
            row = row + jnp.where((lane == 1) | (lane == 12 + slot), cross, 0.0)
        sums_ref[...] = row

    linear_frames(
        positions_ref,
        live,
        tiles,
        lambda: change_ref,
        ((patch, moved, far), later),
        (left, right),
        (tall_ref, wide_ref),
        finish,
    )
    prev()
    prev_probe()
    own = tiles_ref[0]
    probe_grad = change_ref[...]
    values = [
        (3, jnp.sum(own * own)),
        (4, jnp.sum(own * prev_ref[...])),
        (20, jnp.sum(probe_grad * probe_grad)),
        (21, jnp.sum(probe_grad * prev_probe_ref[...])),
    ]
    row = sums_ref[...]
    for at, value in values:
        row = jnp.where(lane == at, value, row)
    sums_ref[...] = row
    copy.wait()


def update_kernel(
    prev_norm_ref,
    gathered_ref,
    sums_ref,
    object_any,
    object_grad_any,
    object_prev_any,
    probe_any,
    probe_grad_any,
    probe_prev_any,
    object_new_any,
    probe_new_any,
    object_direction_any,
    probe_direction_any,
    row_ref,
    held_ref,
    made_ref,
    in_sems,
    out_sems,
):
    sources = [object_prev_any, object_grad_any, object_any]
    sources += [probe_prev_any, probe_grad_any, probe_any]
    arrivals = incoming(sources, [held_ref.at[at] for at in range(6)], in_sems)
    total = jnp.sum(gathered_ref[...], axis=0)
    local = sums_ref[...]
    lane = lax.broadcasted_iota(jnp.int32, (1, 128), 1)

    def pick(row, at):
        return jnp.sum(jnp.where(lane == at, row, 0.0))

    grad_norm = pick(total, 3) + pick(local, 20)
    along_prev = pick(total, 4) + pick(local, 21)
    ratio = grad_norm / prev_norm_ref[0]
    descent = grad_norm - ratio * along_prev
    curvature = pick(total, 0) - 2.0 * ratio * pick(total, 1) + ratio * ratio * pick(total, 2)
    step_size = descent / (0.5 * curvature + 1e-06)
    outs = [object_direction_any, object_new_any, probe_direction_any, probe_new_any]
    sent = []
    for first in (0, 3):
        at = 2 * (first // 3)
        prev, grad, field = [arrival()[...] for arrival in arrivals[first : first + 3]]
        direction = ratio * prev - grad
        made_ref[at] = direction
        made_ref[at + 1] = field + step_size * direction
        span = range(at, at + 2)
        sent += outgoing([made_ref.at[i] for i in span], [outs[i] for i in span], out_sems, at)
    pixels = held_ref.shape[-1] * held_ref.shape[-2]
    row = jnp.where(lane == 4, grad_norm, 0.0)
    for slot in range(4):
        frame_sum = (
            pick(local, 8 + slot)
            - 2.0 * ratio * pick(local, 12 + slot)
            + ratio * ratio * pick(local, 16 + slot)
        )
        row = jnp.where(lane == slot, frame_sum / pixels, row)
    row_ref[...] = row
    for copy in sent:
        copy.wait()


def shaped(*dims):
    return jax.ShapeDtypeStruct(dims, jnp.float32)


def buffer(*dims, dtype=jnp.float32):
    return pltpu.VMEM(dims, dtype)


def arrivals_of(count):
    return pltpu.SemaphoreType.DMA((count,))


def anywhere(count):
    return [pl.BlockSpec(memory_space=pl.ANY)] * count


def in_hbm(count):
    return [pl.BlockSpec(memory_space=pltpu.HBM)] * count


def in_vmem(count):
    return [pl.BlockSpec(memory_space=pltpu.VMEM)] * count


def in_smem(count):
    return [pl.BlockSpec(memory_space=pltpu.SMEM)] * count


def table_buffers(width):
    return [
        buffer(2 * width, 6 * width, dtype=jnp.bfloat16),
        buffer(6 * width, 2 * width, dtype=jnp.bfloat16),
    ]


def dft_scratch(width):
    return [
        buffer(2, 6 * width, width, dtype=jnp.bfloat16),
        buffer(2, width, 6 * width, dtype=jnp.bfloat16),
    ]


def costing(flops):
    return {
        "compiler_params": pltpu.CompilerParams(vmem_limit_bytes=VMEM_BYTES),
        "cost_estimate": pl.CostEstimate(flops=flops, bytes_accessed=10**7, transcendentals=0),
    }


def gradient_call(positions, counts, tiles, probe, measured, tables):
    width = probe.shape[-1]
    slots = measured.shape[2]
    frames = buffer(slots, 2, width, width)
    return pl.pallas_call(
        gradient_kernel,
        out_shape=(shaped(2, width, width),) * 5 + (shaped(slots, 2, width, width),) * 3,
        in_specs=in_smem(2) + anywhere(4) + in_hbm(4),
        out_specs=(*anywhere(5), *in_hbm(3)),
        scratch_shapes=[
            buffer(4, 2, width, width),
            buffer(2, width, width),
            buffer(slots, width, width, dtype=measured.dtype),
            *table_buffers(width),
            buffer(5, 2, width, width),
            frames,
            frames,
            frames,
            *dft_scratch(width),
            arrivals_of(8),
            arrivals_of(11),
        ],
        name="gradient_frames",
        **costing(10**10),
    )(positions, counts, *tiles, probe, measured, *tables)


def previous_call(positions, counts, tiles, probe_prev, kept, tables):
    width = probe_prev.shape[-1]
    slots = kept[0].shape[0]
    frames = buffer(slots, 2, width, width)
    return pl.pallas_call(
        previous_kernel,
        out_shape=(shaped(slots, width, width), shaped(1, 128)),
        in_specs=in_smem(2) + anywhere(4) + in_hbm(6),
        out_specs=(*in_hbm(1), *in_vmem(1)),
        scratch_shapes=[
            buffer(4, 2, width, width),
            buffer(2, width, width),
            frames,
            frames,
            frames,
            *table_buffers(width),
            buffer(slots, width, width),
            *dft_scratch(width),
            arrivals_of(13),
            pltpu.SemaphoreType.DMA,
        ],
        name="previous_frames",
        **costing(5 * 10**9),
    )(positions, counts, *tiles, probe_prev, *kept, *tables)


def curvature_call(positions, counts, tiles, total, kept, tables, previous, probe_scale):
    width = tiles[0].shape[-1]
    slots = kept[0].shape[0]
    frames = buffer(slots, 2, width, width)
    return pl.pallas_call(
        functools.partial(curvature_kernel, probe_scale=probe_scale),
        out_shape=(shaped(1, 128), shaped(2, width, width)),
        in_specs=in_smem(2) + anywhere(5) + in_hbm(7) + in_vmem(1) + in_hbm(1),
        out_specs=(*in_vmem(1), *in_hbm(1)),
        scratch_shapes=[
            buffer(4, 2, width, width),
            buffer(*total.shape),
            buffer(2, width, width),
            frames,
            frames,
            frames,
            *table_buffers(width),
            buffer(slots, width, width),
            buffer(2, width, width),
            buffer(2, width, width),
            *dft_scratch(width),
            arrivals_of(16),
            pltpu.SemaphoreType.DMA,
        ],
        name="curvature_frames",
        **costing(5 * 10**9),
    )(positions, counts, *tiles, total, *kept, *tables, *previous)


def update_call(prev_norm, gathered, sums, arrays):
    shape = arrays[0].shape
    return pl.pallas_call(
        update_kernel,
        out_shape=(shaped(*shape),) * 4 + (shaped(1, 128),),
        in_specs=in_smem(1) + in_vmem(2) + in_hbm(6),
        out_specs=(*in_hbm(4), *in_vmem(1)),
        scratch_shapes=[buffer(6, *shape), buffer(4, *shape), arrivals_of(6), arrivals_of(4)],
        name="update",
        **costing(10**6),
    )(prev_norm, gathered, sums, *arrays)


def passed_along(shard, axis, by):
    count = lax.axis_size(axis)
    pairs = [(i, i + by) for i in range(count) if 0 <= i + by < count]
    return lax.ppermute(shard, axis, pairs)


def device_groups(block):
    rows, cols = lax.axis_size("row"), lax.axis_size("col")
    near = [
        [row * cols + first + at for row in range(rows) for at in range(block)]
        for first in range(0, cols, block)
    ]
    return near, [list(members) for members in zip(*near)]


def exchanged(pieces, groups):
    return lax.all_to_all(pieces, ("row", "col"), 0, 0, axis_index_groups=groups)


def copies(piece, groups):
    return jnp.broadcast_to(piece[None], (len(groups[0]),) + piece.shape)


def held(value, *others):
    return lax.optimization_barrier((value,) + others)[0]


def per_device(
    object_field,
    probe_field,
    object_dir_prev,
    probe_dir_prev,
    prev_norm,
    intensities,
    positions,
    counts,
):
    width = probe_field.shape[-1]
    slots = positions.shape[2]
    tables = dft_blocks(width)
    probe_scale = 1.0 / math.sqrt(slots * lax.axis_size("row") * lax.axis_size("col"))
    near, apart = device_groups(4)

    right = passed_along(object_field, "col", -1)
    below = passed_along(object_field, "row", -1)
    diag = passed_along(held(below, right), "col", -1)
    prev_below = passed_along(held(object_dir_prev, below), "row", -1)
    prev_diag = passed_along(held(prev_below, diag), "col", -1)

    own_grad, below_grad, right_grad, diag_grad, probe_part, *kept = gradient_call(
        positions,
        counts,
        (object_field, below, right, held(diag, prev_below)),
        probe_field,
        intensities,
        tables,
    )
    probe_part = held(probe_part, prev_diag)
    from_left_diag = passed_along(diag_grad, "col", 1)
    prev_right = passed_along(held(object_dir_prev, diag_grad), "col", -1)
    pieces = exchanged(probe_part.reshape((len(near[0]), -1, width)), near)
    pieces, from_left_diag = lax.optimization_barrier((pieces, from_left_diag))
    piece = copies(jnp.sum(pieces, axis=0), apart)
    piece, below_sum = lax.optimization_barrier((piece, below_grad + from_left_diag))
    from_above = passed_along(below_sum, "row", 1)
    from_left = passed_along(right_grad, "col", 1)
    pieces = exchanged(piece, apart)
    pieces, from_above, from_left = lax.optimization_barrier((pieces, from_above, from_left))
    piece = copies(jnp.sum(pieces, axis=0), near)
    object_grad = own_grad + from_left + from_above
    piece, object_grad, prev_right = lax.optimization_barrier((piece, object_grad, prev_right))
    grad_below = passed_along(object_grad, "row", -1)
    grad_right = passed_along(object_grad, "col", -1)
    grad_diag = passed_along(grad_below, "col", -1)
    total = exchanged(piece, near)
    prev_tiles = (object_dir_prev, prev_below, prev_right, prev_diag)
    previous = previous_call(positions, counts, prev_tiles, probe_dir_prev, kept, tables)
    total = held(total, grad_right, grad_diag, *previous)
    sums, probe_grad = curvature_call(
        positions,
        counts,
        (object_grad, grad_below, grad_right, grad_diag),
        total,
        kept,
        tables,
        (object_dir_prev, *previous, probe_dir_prev),
        probe_scale,
    )
    near, apart = device_groups(2)
    across = jnp.sum(exchanged(copies(sums, near), near), axis=0)
    across = exchanged(copies(across, apart), apart)
    arrays = (object_field, object_grad, object_dir_prev, probe_field, probe_grad, probe_dir_prev)
    object_new, probe_new, object_direction, probe_direction, row = update_call(
        prev_norm.reshape(1), across, sums, arrays
    )
    return (
        object_new,
        probe_new,
        object_direction,
        probe_direction,
        row[0, slots],
        row[0, :slots].reshape(1, 1, slots),
    )


def solution(mesh):
    return jax.shard_map(
        per_device,
        mesh=mesh,
        in_specs=(
            P(None, "row", "col"),
            P(),
            P(None, "row", "col"),
            P(),
            P(),
            P("row", "col", None, None, None),
            P("row", "col", None, None),
            P("row", None),
        ),
        out_specs=(
            P(None, "row", "col"),
            P(),
            P(None, "row", "col"),
            P(),
            P(),
            P("row", "col", None),
        ),
        check_vma=False,
    )
```

```python
import functools
import math

import jax
import jax.numpy as jnp
import numpy as np
from jax import lax
from jax.experimental import pallas as pl
from jax.experimental.pallas import tpu as pltpu
from jax.sharding import PartitionSpec as P

VMEM_BYTES = 60 * 1024 * 1024


def dft_blocks(width):
    at = np.arange(width)
    angle = (np.outer(at, at) % width) * (2.0 * math.pi / width)
    cosine = (np.cos(angle) / math.sqrt(width)).astype(np.float32)
    sine = (np.sin(angle) / math.sqrt(width)).astype(np.float32)

    def thrice(table):
        high = table.astype(jnp.bfloat16)
        low = (table - high.astype(np.float32)).astype(jnp.bfloat16)
        return np.concatenate([high, low, high], axis=1)

    real_rows = np.concatenate([thrice(cosine), thrice(sine)], axis=1)
    imag_rows = np.concatenate([thrice(-sine), thrice(cosine)], axis=1)
    left = np.concatenate([real_rows, imag_rows], axis=0)
    return left, np.ascontiguousarray(left.T)


def split_halves(value):
    high = value.astype(jnp.bfloat16)
    low = (value - high.astype(jnp.float32)).astype(jnp.bfloat16)
    return high, low


def dft_pairs(pairs, tables, scratch):
    left_ref, right_ref = tables
    tall_ref, wide_ref = scratch
    width = pairs[0][0].shape[0]
    for which, pair in enumerate(pairs):
        for at, part in enumerate(pair):
            high, low = split_halves(part)
            base = 3 * at * width
            tall_ref[which, base : base + width, :] = high
            tall_ref[which, base + width : base + 2 * width, :] = high
            tall_ref[which, base + 2 * width : base + 3 * width, :] = low
    results = []
    left_ref = left_ref()
    for which in range(len(pairs)):
        middle = jnp.dot(left_ref[...], tall_ref[which], preferred_element_type=jnp.float32)
        for at in range(2):
            high, low = split_halves(middle[at * width : (at + 1) * width])
            base = 3 * at * width
            wide_ref[which, :, base : base + width] = high
            wide_ref[which, :, base + width : base + 2 * width] = high
            wide_ref[which, :, base + 2 * width : base + 3 * width] = low
    right_ref = right_ref()
    for which in range(len(pairs)):
        done = jnp.dot(wide_ref[which], right_ref[...], preferred_element_type=jnp.float32)
        results.append((done[:, :width], done[:, width:]))
    return results


def rolled(value, row, col):
    return pltpu.roll(pltpu.roll(value, row, 0), col, 1)


def wrapped(own, below, right, diag, upper, nearer):
    return jnp.where(nearer, jnp.where(upper, own, below), jnp.where(upper, right, diag))


def masks(row, col, width):
    upper = lax.broadcasted_iota(jnp.int32, (width, width), 0) >= row
    nearer = lax.broadcasted_iota(jnp.int32, (width, width), 1) >= col
    return upper, nearer


def corner(positions_ref, slot, width):
    row = lax.rem(positions_ref[0, 0, slot, 0], width)
    col = lax.rem(positions_ref[0, 0, slot, 1], width)
    return row, col


def live_count(counts_ref):
    return counts_ref[0, lax.axis_index("col")]


class Incoming:
    def __init__(self, source, target, semaphore):
        self.target = target
        self.copy = pltpu.make_async_copy(source, target, semaphore)
        self.copy.start()
        self.waiting = True

    def __call__(self):
        if self.waiting:
            self.copy.wait()
            self.waiting = False
        return self.target


def incoming(sources, targets, semaphores):
    return [
        Incoming(source, target, semaphores.at[at])
        for at, (source, target) in enumerate(zip(sources, targets))
    ]


def outgoing(sources, targets, semaphores, first=0):
    sent = [
        pltpu.make_async_copy(source, target, semaphores.at[first + at])
        for at, (source, target) in enumerate(zip(sources, targets))
    ]
    for copy in sent:
        copy.start()
    return sent


def gradient_kernel(
    positions_ref,
    counts_ref,
    own_any,
    below_any,
    right_any,
    diag_any,
    probe_any,
    measured_any,
    left_any,
    right_table_any,
    own_grad_any,
    below_grad_any,
    right_grad_any,
    diag_grad_any,
    probe_grad_any,
    patch_any,
    moved_any,
    far_any,
    tiles_ref,
    probe_ref,
    measured_ref,
    left_ref,
    right_ref,
    grads_ref,
    probe_sum_ref,
    patch_ref,
    moved_ref,
    far_ref,
    tall_ref,
    wide_ref,
    in_sems,
    out_sems,
):
    width = probe_ref.shape[-1]
    live = live_count(counts_ref)
    *ready, left, measured, right = incoming(
        [own_any, below_any, right_any, diag_any, probe_any]
        + [left_any, measured_any.at[0, 0], right_table_any],
        [tiles_ref.at[at] for at in range(4)] + [probe_ref, left_ref, measured_ref, right_ref],
        in_sems,
    )
    for arrival in ready:
        arrival()

    def both(first):
        slots = (first, first + 1)
        spots = [corner(positions_ref, slot, width) for slot in slots]
        waves = []
        for slot, (row, col) in zip(slots, spots):
            upper, nearer = masks(row, col, width)
            for part in range(2):
                patch_ref[slot, part] = wrapped(
                    *[tiles_ref[at, part] for at in range(4)], upper, nearer
                )
                moved_ref[slot, part] = rolled(probe_ref[part], row, col)
            patch_r, patch_i = patch_ref[slot, 0], patch_ref[slot, 1]
            probe_r, probe_i = moved_ref[slot, 0], moved_ref[slot, 1]
            kept = slot < live
            waves.append(
                (
                    jnp.where(kept, probe_r * patch_r - probe_i * patch_i, 0.0),
                    jnp.where(kept, probe_r * patch_i + probe_i * patch_r, 0.0),
                )
            )
        span = pl.ds(first, 2)
        sent = outgoing(
            [patch_ref.at[span], moved_ref.at[span]],
            [patch_any.at[span], moved_any.at[span]],
            out_sems,
            5 + 3 * (first // 2),
        )
        fars = dft_pairs(waves, (left, right), (tall_ref, wide_ref))
        turned = []
        measured()
        for slot, (far_r, far_i) in zip(slots, fars):
            far_ref[slot, 0] = far_r
            far_ref[slot, 1] = far_i
            residue = far_r * far_r + far_i * far_i - measured_ref[slot].astype(jnp.float32)
            turned.append((residue * far_i, residue * far_r))
        sent += outgoing(
            [far_ref.at[span]], [far_any.at[span]], out_sems, 7 + 3 * (first // 2)
        )
        backs = dft_pairs(turned, (left, right), (tall_ref, wide_ref))
        pieces = []
        for slot, (row, col), (back_i, back_r) in zip(slots, spots, backs):
            patch_r, patch_i = patch_ref[slot, 0], patch_ref[slot, 1]
            back_row = lax.rem(width - row, width)
            back_col = lax.rem(width - col, width)
            pieces.append(
                (
                    rolled(patch_r * back_r + patch_i * back_i, back_row, back_col),
                    rolled(patch_r * back_i - patch_i * back_r, back_row, back_col),
                )
            )
        for part in range(2):
            total = pieces[0][part] + pieces[1][part]
            for half in range(2):
                rows = pl.ds((2 * part + half) * width, width)
                side = total[:, half * (width // 2) : (half + 1) * (width // 2)]
                probe_sum_ref[rows, :] = side if first == 0 else probe_sum_ref[rows, :] + side
        for part in range(2):
            sums = [0.0, 0.0, 0.0, 0.0]
            for slot, (row, col), (back_i, back_r) in zip(slots, spots, backs):
                upper, nearer = masks(row, col, width)
                probe_r, probe_i = moved_ref[slot, 0], moved_ref[slot, 1]
                if part == 0:
                    term = probe_r * back_r + probe_i * back_i
                else:
                    term = probe_r * back_i - probe_i * back_r
                close = jnp.where(nearer, term, 0.0)
                beyond = term - close
                for at, side in enumerate((close, beyond)):
                    top = jnp.where(upper, side, 0.0)
                    sums[2 * at] = sums[2 * at] + top
                    sums[2 * at + 1] = sums[2 * at + 1] + (side - top)
            for at, total in enumerate(sums):
                grads_ref[at, part] = total if first == 0 else grads_ref[at, part] + total
        for copy in sent:
            copy.wait()

    both(0)
    pl.when(live > 2)(lambda: both(2))
    outs = [own_grad_any, below_grad_any, right_grad_any, diag_grad_any, probe_grad_any]
    made = [grads_ref.at[at] for at in range(4)] + [probe_sum_ref]
    for copy in outgoing(made, outs, out_sems):
        copy.wait()


def linear_frames(positions_ref, live, tiles, change, kept, tables, scratch, finish):
    own_ref, below_ref, right_ref, diag_ref = [tile() for tile in tiles]
    change_ref = change()
    width = own_ref.shape[-1]

    def both(first, patches, moves, fars):
        slots = (first, first + 1)
        patch_ref, moved_ref = patches(), moves()
        waves = []
        for at, slot in enumerate(slots):
            row, col = corner(positions_ref, slot, width)
            upper, nearer = masks(row, col, width)
            step_r, step_i = [
                wrapped(own_ref[part], below_ref[part], right_ref[part], diag_ref[part], upper, nearer)
                for part in range(2)
            ]
            patch_r, patch_i = patch_ref[at, 0], patch_ref[at, 1]
            probe_r, probe_i = moved_ref[at, 0], moved_ref[at, 1]
            change_r = rolled(change_ref[0], row, col)
            change_i = rolled(change_ref[1], row, col)
            waves.append(
                (
                    probe_r * step_r - probe_i * step_i + change_r * patch_r - change_i * patch_i,
                    probe_r * step_i + probe_i * step_r + change_r * patch_i + change_i * patch_r,
                )
            )
        steps = dft_pairs(waves, tables, scratch)
        far_ref = fars()
        quads = [
            2.0 * (far_ref[at, 0] * step_r + far_ref[at, 1] * step_i)
            for at, (step_r, step_i) in enumerate(steps)
        ]
        finish(slots, quads)

    both(0, *kept[0])
    for arrival in kept[1]:
        arrival()
    pl.when(live > 2)(lambda: both(2, *kept[1]))


def halves(array, ref):
    return [(array.at[pl.ds(first, 2)], ref.at[pl.ds(first, 2)]) for first in (0, 2)]


def fold_kernel(
    own_any,
    left_any,
    above_any,
    prev_any,
    pieces_any,
    grad_any,
    payload_ref,
    held_ref,
    pieces_ref,
    grad_ref,
    in_sems,
    out_sem,
):
    sources = [own_any, left_any, above_any, prev_any, pieces_any]
    targets = [held_ref.at[at] for at in range(4)] + [pieces_ref]
    own, left, above, prev, pieces = incoming(sources, targets, in_sems)
    grad_ref[...] = own()[...] + left()[...] + above()[...]
    copy = pltpu.make_async_copy(grad_ref, grad_any, out_sem)
    copy.start()
    square = jnp.sum(grad_ref[...] * grad_ref[...])
    along = jnp.sum(grad_ref[...] * prev()[...])
    piece = jnp.sum(pieces()[...], axis=0)
    depth = piece.shape[0]
    lanes = lax.broadcasted_iota(jnp.int32, (1, payload_ref.shape[2]), 1)
    extra = jnp.where(lanes == 0, square, jnp.where(lanes == 1, along, 0.0))
    for at in range(payload_ref.shape[0]):
        payload_ref[at, :depth] = piece
        payload_ref[at, depth:] = extra
    copy.wait()


def curvature_kernel(
    positions_ref,
    counts_ref,
    prev_norm_ref,
    own_any,
    below_any,
    right_any,
    diag_any,
    prev_own_any,
    prev_below_any,
    prev_right_any,
    prev_diag_any,
    total_any,
    patch_any,
    moved_any,
    far_any,
    left_any,
    right_table_any,
    prev_probe_any,
    direction_any,
    probe_direction_any,
    sums_ref,
    tiles_ref,
    prev_tiles_ref,
    total_ref,
    change_ref,
    patch_ref,
    moved_ref,
    far_ref,
    left_ref,
    right_ref,
    prev_probe_ref,
    tall_ref,
    wide_ref,
    in_sems,
    out_sems,
    *,
    probe_scale,
    pieces,
):
    live = live_count(counts_ref)
    width = change_ref.shape[-1]
    kept = [
        halves(patch_any, patch_ref),
        halves(moved_any, moved_ref),
        halves(far_any, far_ref),
    ]
    moves = [(total_any, total_ref), (prev_probe_any, prev_probe_ref)]
    for group, target in (
        ((own_any, below_any, right_any, diag_any), tiles_ref),
        ((prev_own_any, prev_below_any, prev_right_any, prev_diag_any), prev_tiles_ref),
    ):
        moves += [(tile, target.at[at]) for at, tile in enumerate(group)]
    moves += [kept[0][0], kept[1][0], (left_any, left_ref), (right_table_any, right_ref), kept[2][0]]
    moves += [kept[0][1], kept[1][1], kept[2][1]]
    total, prev_probe, *arrivals = incoming(*zip(*moves), in_sems)
    tiles, prev_tiles = arrivals[:4], arrivals[4:8]
    (patch, moved, left, right, far), later = arrivals[8:13], arrivals[13:]

    total()
    depth = 4 * width // pieces
    products = jnp.zeros((1, total_ref.shape[-1]), jnp.float32)
    for piece in range(pieces):
        base = piece * (depth + 1)
        part, rest = divmod(piece * depth, 2 * width)
        half, first = divmod(rest, width)
        lanes = slice(half * (width // 2), (half + 1) * (width // 2))
        change_ref[part, first : first + depth, lanes] = (
            total_ref[base : base + depth, :] * probe_scale
        )
        products = products + total_ref[base + depth : base + depth + 1, :]
    lane = lax.broadcasted_iota(jnp.int32, (1, 128), 1)
    probe_grad = change_ref[...]
    prev_probe()
    grad_norm = jnp.sum(jnp.where(lane == 0, products, 0.0)) + jnp.sum(probe_grad * probe_grad)
    along_prev = jnp.sum(jnp.where(lane == 1, products, 0.0))
    along_prev = along_prev + jnp.sum(probe_grad * prev_probe_ref[...])
    ratio = grad_norm / prev_norm_ref[0]
    descent = grad_norm - ratio * along_prev
    change_ref[...] = ratio * prev_probe_ref[...] - change_ref[...]
    for at, (tile, prev) in enumerate(zip(tiles, prev_tiles)):
        tile()
        prev()
        tiles_ref[at] = ratio * prev_tiles_ref[at] - tiles_ref[at]
    sent = outgoing(
        [tiles_ref.at[0], change_ref], [direction_any, probe_direction_any], out_sems
    )
    row = jnp.where(lane == 5, grad_norm, jnp.where(lane == 6, descent, 0.0))
    sums_ref[...] = row

    def finish(slots, quads):
        row = sums_ref[...]
        for slot, quad in zip(slots, quads):
            square = jnp.sum(quad * quad)
            row = row + jnp.where((lane == 0) | (lane == 1 + slot), square, 0.0)
        sums_ref[...] = row

    linear_frames(
        positions_ref,
        live,
        [(lambda at=at: tiles_ref.at[at]) for at in range(4)],
        lambda: change_ref,
        ((patch, moved, far), later),
        (left, right),
        (tall_ref, wide_ref),
        finish,
    )
    for copy in sent:
        copy.wait()


def update_kernel(
    gathered_ref,
    sums_ref,
    object_any,
    direction_any,
    probe_any,
    probe_direction_any,
    object_new_any,
    probe_new_any,
    norm_ref,
    frames_ref,
    held_ref,
    in_sems,
    out_sems,
):
    sources = [object_any, direction_any, probe_any, probe_direction_any]
    arrivals = incoming(sources, [held_ref.at[at] for at in range(4)], in_sems)
    total = jnp.sum(gathered_ref[...], axis=0)
    local = sums_ref[...]
    lane = lax.broadcasted_iota(jnp.int32, (1, 128), 1)

    def pick(row, at):
        return jnp.sum(jnp.where(lane == at, row, 0.0))

    curvature = pick(total, 0)
    step_size = pick(local, 6) / (0.5 * curvature + 1e-06)
    outs = [object_new_any, probe_new_any]
    sent = []
    for which in range(2):
        field, direction = [arrival() for arrival in arrivals[2 * which : 2 * which + 2]]
        field[...] = field[...] + step_size * direction[...]
        sent += outgoing([field], [outs[which]], out_sems, which)
    norm_ref[0, 0] = pick(local, 5)
    pixels = held_ref.shape[-1] * held_ref.shape[-2]
    for slot in range(frames_ref.shape[-1]):
        frames_ref[0, 0, slot] = pick(local, 1 + slot) / pixels
    for copy in sent:
        copy.wait()


def shaped(*dims):
    return jax.ShapeDtypeStruct(dims, jnp.float32)


def buffer(*dims, dtype=jnp.float32):
    return pltpu.VMEM(dims, dtype)


def arrivals_of(count):
    return pltpu.SemaphoreType.DMA((count,))


def anywhere(count):
    return [pl.BlockSpec(memory_space=pl.ANY)] * count


def in_hbm(count):
    return [pl.BlockSpec(memory_space=pltpu.HBM)] * count


def in_vmem(count):
    return [pl.BlockSpec(memory_space=pltpu.VMEM)] * count


def in_smem(count):
    return [pl.BlockSpec(memory_space=pltpu.SMEM)] * count


def table_buffers(width):
    return [
        buffer(2 * width, 6 * width, dtype=jnp.bfloat16),
        buffer(6 * width, 2 * width, dtype=jnp.bfloat16),
    ]


def dft_scratch(width):
    return [
        buffer(2, 6 * width, width, dtype=jnp.bfloat16),
        buffer(2, width, 6 * width, dtype=jnp.bfloat16),
    ]


def costing(flops):
    return {
        "compiler_params": pltpu.CompilerParams(vmem_limit_bytes=VMEM_BYTES),
        "cost_estimate": pl.CostEstimate(flops=flops, bytes_accessed=10**7, transcendentals=0),
    }


def gradient_call(positions, counts, tiles, probe, measured, tables):
    width = probe.shape[-1]
    slots = measured.shape[2]
    frames = buffer(slots, 2, width, width)
    return pl.pallas_call(
        gradient_kernel,
        out_shape=(shaped(2, width, width),) * 4
        + (shaped(4 * width, width // 2),)
        + (shaped(slots, 2, width, width),) * 3,
        in_specs=in_smem(2) + anywhere(4) + in_hbm(4),
        out_specs=(*anywhere(5), *in_hbm(3)),
        scratch_shapes=[
            buffer(4, 2, width, width),
            buffer(2, width, width),
            buffer(slots, width, width, dtype=measured.dtype),
            *table_buffers(width),
            buffer(4, 2, width, width),
            buffer(4 * width, width // 2),
            frames,
            frames,
            frames,
            *dft_scratch(width),
            arrivals_of(8),
            arrivals_of(11),
        ],
        name="gradient_frames",
        **costing(10**10),
    )(positions, counts, *tiles, probe, measured, *tables)


def fold_call(parts, prev, pieces, targets):
    shape = prev.shape
    depth = pieces.shape[1]
    return pl.pallas_call(
        fold_kernel,
        out_shape=(shaped(*shape), shaped(targets, depth + 1, pieces.shape[2])),
        in_specs=anywhere(5),
        out_specs=(*anywhere(1), *in_vmem(1)),
        scratch_shapes=[
            buffer(4, *shape),
            buffer(*pieces.shape),
            buffer(*shape),
            arrivals_of(5),
            pltpu.SemaphoreType.DMA,
        ],
        name="fold",
        **costing(10**6),
    )(*parts, prev, pieces)


def curvature_call(positions, counts, prev_norm, tiles, total, pieces, kept, tables, probe_prev, scale):
    width = tiles[0].shape[-1]
    slots = kept[0].shape[0]
    frames = buffer(slots, 2, width, width)
    return pl.pallas_call(
        functools.partial(curvature_kernel, probe_scale=scale, pieces=pieces),
        out_shape=(shaped(2, width, width), shaped(2, width, width), shaped(1, 128)),
        in_specs=in_smem(3) + anywhere(9) + in_hbm(6),
        out_specs=(*in_hbm(2), *in_vmem(1)),
        scratch_shapes=[
            buffer(4, 2, width, width),
            buffer(4, 2, width, width),
            buffer(*total.shape),
            buffer(2, width, width),
            frames,
            frames,
            frames,
            *table_buffers(width),
            buffer(2, width, width),
            *dft_scratch(width),
            arrivals_of(18),
            arrivals_of(2),
        ],
        name="curvature_frames",
        **costing(5 * 10**9),
    )(positions, counts, prev_norm, *tiles, total, *kept, *tables, probe_prev)


def update_call(gathered, sums, arrays, slots):
    shape = arrays[0].shape
    return pl.pallas_call(
        update_kernel,
        out_shape=(shaped(*shape),) * 2 + (shaped(1, 1), shaped(1, 1, slots)),
        in_specs=in_vmem(2) + in_hbm(4),
        out_specs=(*in_hbm(2), *in_smem(2)),
        scratch_shapes=[buffer(4, *shape), arrivals_of(4), arrivals_of(2)],
        name="update",
        **costing(10**6),
    )(gathered, sums, *arrays)


def passed_along(shard, axis, by):
    count = lax.axis_size(axis)
    pairs = [(i, i + by) for i in range(count) if 0 <= i + by < count]
    return lax.ppermute(shard, axis, pairs)


def device_groups(block):
    rows, cols = lax.axis_size("row"), lax.axis_size("col")
    near = [
        [row * cols + first + at for row in range(rows) for at in range(block)]
        for first in range(0, cols, block)
    ]
    return near, [list(members) for members in zip(*near)]


def exchanged(pieces, groups):
    return lax.all_to_all(pieces, ("row", "col"), 0, 0, axis_index_groups=groups)


def copies(piece, groups):
    return jnp.broadcast_to(piece[None], (len(groups[0]),) + piece.shape)


def held(value, *others):
    return lax.optimization_barrier((value,) + others)[0]


def per_device(
    object_field,
    probe_field,
    object_dir_prev,
    probe_dir_prev,
    prev_norm,
    intensities,
    positions,
    counts,
):
    width = probe_field.shape[-1]
    slots = positions.shape[2]
    tables = dft_blocks(width)
    probe_scale = 1.0 / math.sqrt(slots * lax.axis_size("row") * lax.axis_size("col"))
    near, apart = device_groups(4)

    right = passed_along(object_field, "col", -1)
    below = passed_along(object_field, "row", -1)
    diag = passed_along(held(below, right), "col", -1)
    prev_below = passed_along(held(object_dir_prev, below), "row", -1)
    prev_right = passed_along(held(object_dir_prev, below), "col", -1)

    own_grad, below_grad, right_grad, diag_grad, probe_part, *kept = gradient_call(
        positions,
        counts,
        (object_field, below, right, diag),
        probe_field,
        intensities,
        tables,
    )
    probe_part, prev_below, prev_right = lax.optimization_barrier(
        (probe_part, prev_below, prev_right)
    )
    from_left_diag = passed_along(diag_grad, "col", 1)
    pieces = exchanged(probe_part.reshape((len(near[0]), -1, width // 2)), near)
    from_above = passed_along(below_grad + from_left_diag, "row", 1)
    from_left = passed_along(right_grad, "col", 1)
    prev_diag = passed_along(held(prev_below, diag_grad), "col", -1)
    from_above = held(from_above, prev_diag)
    object_grad, payload = fold_call(
        (own_grad, from_left, from_above), object_dir_prev, pieces, len(apart[0])
    )
    grad_below = passed_along(object_grad, "row", -1)
    grad_right = passed_along(object_grad, "col", -1)
    payload, grad_below, grad_right = lax.optimization_barrier(
        (exchanged(payload, apart), grad_below, grad_right)
    )
    payload = jnp.sum(payload, axis=0)[:, None, :]
    grad_diag = passed_along(grad_below, "col", -1)
    total = exchanged(copies(payload, near), near)
    total = held(total, grad_diag)
    object_direction, probe_direction, sums = curvature_call(
        positions,
        counts,
        prev_norm.reshape(1),
        (object_grad, grad_below, grad_right, grad_diag)
        + (object_dir_prev, prev_below, prev_right, prev_diag),
        total.reshape(-1, width // 2),
        len(near[0]),
        kept,
        tables,
        probe_dir_prev,
        probe_scale,
    )
    near, apart = device_groups(2)
    across = jnp.sum(exchanged(copies(sums, near), near), axis=0)
    across = exchanged(copies(across, apart), apart)
    object_new, probe_new, norm, frame_curvature = update_call(
        across, sums, (object_field, object_direction, probe_field, probe_direction), slots
    )
    return (
        object_new,
        probe_new,
        object_direction,
        probe_direction,
        norm.reshape(()),
        frame_curvature,
    )


def solution(mesh):
    return jax.shard_map(
        per_device,
        mesh=mesh,
        in_specs=(
            P(None, "row", "col"),
            P(),
            P(None, "row", "col"),
            P(),
            P(),
            P("row", "col", None, None, None),
            P("row", "col", None, None),
            P("row", None),
        ),
        out_specs=(
            P(None, "row", "col"),
            P(),
            P(None, "row", "col"),
            P(),
            P(),
            P("row", "col", None),
        ),
        check_vma=False,
    )
```

```python
import functools
import math

import jax
import jax.numpy as jnp
import numpy as np
from jax import lax
from jax.experimental import pallas as pl
from jax.experimental.pallas import tpu as pltpu
from jax.sharding import PartitionSpec as P

VMEM_BYTES = 60 * 1024 * 1024

FOLD_FLOPS = 2 * 10**10


def dft_blocks(width):
    at = np.arange(width)
    angle = (np.outer(at, at) % width) * (2.0 * math.pi / width)
    cosine = (np.cos(angle) / math.sqrt(width)).astype(np.float32)
    sine = (np.sin(angle) / math.sqrt(width)).astype(np.float32)

    def thrice(table):
        high = table.astype(jnp.bfloat16)
        low = (table - high.astype(np.float32)).astype(jnp.bfloat16)
        return np.concatenate([high, low, high], axis=1)

    real_rows = np.concatenate([thrice(cosine), thrice(sine)], axis=1)
    imag_rows = np.concatenate([thrice(-sine), thrice(cosine)], axis=1)
    left = np.concatenate([real_rows, imag_rows], axis=0)
    return left, np.ascontiguousarray(left.T)


def split_halves(value):
    high = value.astype(jnp.bfloat16)
    low = (value - high.astype(jnp.float32)).astype(jnp.bfloat16)
    return high, low


def dft_pairs(pairs, tables, scratch):
    left_ref, right_ref = tables
    tall_ref, wide_ref = scratch
    width = pairs[0][0].shape[0]
    for which, pair in enumerate(pairs):
        for at, part in enumerate(pair):
            high, low = split_halves(part)
            base = 3 * at * width
            tall_ref[which, base : base + width, :] = high
            tall_ref[which, base + width : base + 2 * width, :] = high
            tall_ref[which, base + 2 * width : base + 3 * width, :] = low
    results = []
    left_ref = left_ref()
    for which in range(len(pairs)):
        middle = jnp.dot(left_ref[...], tall_ref[which], preferred_element_type=jnp.float32)
        for at in range(2):
            high, low = split_halves(middle[at * width : (at + 1) * width])
            base = 3 * at * width
            wide_ref[which, :, base : base + width] = high
            wide_ref[which, :, base + width : base + 2 * width] = high
            wide_ref[which, :, base + 2 * width : base + 3 * width] = low
    right_ref = right_ref()
    for which in range(len(pairs)):
        done = jnp.dot(wide_ref[which], right_ref[...], preferred_element_type=jnp.float32)
        results.append((done[:, :width], done[:, width:]))
    return results


def rolled(value, row, col):
    return pltpu.roll(pltpu.roll(value, row, 0), col, 1)


def wrapped(own, below, right, diag, upper, nearer):
    return jnp.where(nearer, jnp.where(upper, own, below), jnp.where(upper, right, diag))


def masks(row, col, width):
    upper = lax.broadcasted_iota(jnp.int32, (width, width), 0) >= row
    nearer = lax.broadcasted_iota(jnp.int32, (width, width), 1) >= col
    return upper, nearer


def corner(positions_ref, slot, width):
    row = lax.rem(positions_ref[0, 0, slot, 0], width)
    col = lax.rem(positions_ref[0, 0, slot, 1], width)
    return row, col


def live_count(counts_ref):
    return counts_ref[0, lax.axis_index("col")]


class Incoming:
    def __init__(self, source, target, semaphore):
        self.target = target
        self.copy = pltpu.make_async_copy(source, target, semaphore)
        self.copy.start()
        self.waiting = True

    def __call__(self):
        if self.waiting:
            self.copy.wait()
            self.waiting = False
        return self.target


def incoming(sources, targets, semaphores):
    return [
        Incoming(source, target, semaphores.at[at])
        for at, (source, target) in enumerate(zip(sources, targets))
    ]


def outgoing(sources, targets, semaphores, first=0):
    sent = [
        pltpu.make_async_copy(source, target, semaphores.at[first + at])
        for at, (source, target) in enumerate(zip(sources, targets))
    ]
    for copy in sent:
        copy.start()
    return sent


def gradient_kernel(
    positions_ref,
    counts_ref,
    own_any,
    below_any,
    right_any,
    diag_any,
    probe_any,
    measured_any,
    left_any,
    right_table_any,
    own_grad_any,
    below_grad_any,
    right_grad_any,
    diag_grad_any,
    probe_grad_any,
    patch_any,
    moved_any,
    far_any,
    tiles_ref,
    probe_ref,
    measured_ref,
    left_ref,
    right_ref,
    grads_ref,
    probe_sum_ref,
    patch_ref,
    moved_ref,
    far_ref,
    tall_ref,
    wide_ref,
    in_sems,
    out_sems,
):
    width = probe_ref.shape[-1]
    live = live_count(counts_ref)
    *ready, left, measured, right = incoming(
        [own_any, below_any, right_any, diag_any, probe_any]
        + [left_any, measured_any.at[0, 0], right_table_any],
        [tiles_ref.at[at] for at in range(4)] + [probe_ref, left_ref, measured_ref, right_ref],
        in_sems,
    )
    for arrival in ready:
        arrival()

    def both(first):
        slots = (first, first + 1)
        spots = [corner(positions_ref, slot, width) for slot in slots]
        waves = []
        for slot, (row, col) in zip(slots, spots):
            upper, nearer = masks(row, col, width)
            for part in range(2):
                patch_ref[slot, part] = wrapped(
                    *[tiles_ref[at, part] for at in range(4)], upper, nearer
                )
                moved_ref[slot, part] = rolled(probe_ref[part], row, col)
            patch_r, patch_i = patch_ref[slot, 0], patch_ref[slot, 1]
            probe_r, probe_i = moved_ref[slot, 0], moved_ref[slot, 1]
            kept = slot < live
            waves.append(
                (
                    jnp.where(kept, probe_r * patch_r - probe_i * patch_i, 0.0),
                    jnp.where(kept, probe_r * patch_i + probe_i * patch_r, 0.0),
                )
            )
        span = pl.ds(first, 2)
        sent = outgoing(
            [patch_ref.at[span], moved_ref.at[span]],
            [patch_any.at[span], moved_any.at[span]],
            out_sems,
            5 + 3 * (first // 2),
        )
        fars = dft_pairs(waves, (left, right), (tall_ref, wide_ref))
        turned = []
        measured()
        for slot, (far_r, far_i) in zip(slots, fars):
            far_ref[slot, 0] = far_r
            far_ref[slot, 1] = far_i
            residue = far_r * far_r + far_i * far_i - measured_ref[slot].astype(jnp.float32)
            turned.append((residue * far_i, residue * far_r))
        sent += outgoing(
            [far_ref.at[span]], [far_any.at[span]], out_sems, 7 + 3 * (first // 2)
        )
        backs = dft_pairs(turned, (left, right), (tall_ref, wide_ref))
        pieces = []
        for slot, (row, col), (back_i, back_r) in zip(slots, spots, backs):
            patch_r, patch_i = patch_ref[slot, 0], patch_ref[slot, 1]
            back_row = lax.rem(width - row, width)
            back_col = lax.rem(width - col, width)
            pieces.append(
                (
                    rolled(patch_r * back_r + patch_i * back_i, back_row, back_col),
                    rolled(patch_r * back_i - patch_i * back_r, back_row, back_col),
                )
            )
        for part in range(2):
            total = pieces[0][part] + pieces[1][part]
            for half in range(2):
                rows = pl.ds((2 * part + half) * width, width)
                side = total[:, half * (width // 2) : (half + 1) * (width // 2)]
                probe_sum_ref[rows, :] = side if first == 0 else probe_sum_ref[rows, :] + side
        for part in range(2):
            sums = [0.0, 0.0, 0.0, 0.0]
            for slot, (row, col), (back_i, back_r) in zip(slots, spots, backs):
                upper, nearer = masks(row, col, width)
                probe_r, probe_i = moved_ref[slot, 0], moved_ref[slot, 1]
                if part == 0:
                    term = probe_r * back_r + probe_i * back_i
                else:
                    term = probe_r * back_i - probe_i * back_r
                close = jnp.where(nearer, term, 0.0)
                beyond = term - close
                for at, side in enumerate((close, beyond)):
                    top = jnp.where(upper, side, 0.0)
                    sums[2 * at] = sums[2 * at] + top
                    sums[2 * at + 1] = sums[2 * at + 1] + (side - top)
            for at, total in enumerate(sums):
                grads_ref[at, part] = total if first == 0 else grads_ref[at, part] + total
        for copy in sent:
            copy.wait()

    both(0)
    pl.when(live > 2)(lambda: both(2))
    outs = [own_grad_any, below_grad_any, right_grad_any, diag_grad_any, probe_grad_any]
    made = [grads_ref.at[at] for at in range(4)] + [probe_sum_ref]
    for copy in outgoing(made, outs, out_sems):
        copy.wait()


def linear_frames(positions_ref, live, tiles, change, kept, tables, scratch, finish):
    own_ref, below_ref, right_ref, diag_ref = [tile() for tile in tiles]
    change_ref = change()
    width = own_ref.shape[-1]

    def both(first, patches, moves, fars):
        slots = (first, first + 1)
        patch_ref, moved_ref = patches(), moves()
        waves = []
        for at, slot in enumerate(slots):
            row, col = corner(positions_ref, slot, width)
            upper, nearer = masks(row, col, width)
            step_r, step_i = [
                wrapped(own_ref[part], below_ref[part], right_ref[part], diag_ref[part], upper, nearer)
                for part in range(2)
            ]
            patch_r, patch_i = patch_ref[at, 0], patch_ref[at, 1]
            probe_r, probe_i = moved_ref[at, 0], moved_ref[at, 1]
            change_r = rolled(change_ref[0], row, col)
            change_i = rolled(change_ref[1], row, col)
            waves.append(
                (
                    probe_r * step_r - probe_i * step_i + change_r * patch_r - change_i * patch_i,
                    probe_r * step_i + probe_i * step_r + change_r * patch_i + change_i * patch_r,
                )
            )
        steps = dft_pairs(waves, tables, scratch)
        far_ref = fars()
        quads = [
            2.0 * (far_ref[at, 0] * step_r + far_ref[at, 1] * step_i)
            for at, (step_r, step_i) in enumerate(steps)
        ]
        finish(slots, quads)

    both(0, *kept[0])
    for arrival in kept[1]:
        arrival()
    pl.when(live > 2)(lambda: both(2, *kept[1]))


def halves(array, ref):
    return [(array.at[pl.ds(first, 2)], ref.at[pl.ds(first, 2)]) for first in (0, 2)]


def fold_kernel(
    own_any,
    left_any,
    above_any,
    corner_any,
    prev_any,
    grad_any,
    products_ref,
    held_ref,
    grad_ref,
    in_sems,
    out_sem,
):
    sources = [own_any, left_any, above_any, corner_any, prev_any]
    targets = [held_ref.at[at] for at in range(5)]
    own, left, above, diag, prev = incoming(sources, targets, in_sems)
    grad_ref[...] = own()[...] + left()[...] + above()[...] + diag()[...]
    copy = pltpu.make_async_copy(grad_ref, grad_any, out_sem)
    copy.start()
    square = jnp.sum(grad_ref[...] * grad_ref[...])
    along = jnp.sum(grad_ref[...] * prev()[...])
    lanes = lax.broadcasted_iota(jnp.int32, products_ref.shape, 1)
    products_ref[...] = jnp.where(lanes == 0, square, jnp.where(lanes == 1, along, 0.0))
    copy.wait()


def payload_kernel(pieces_any, products_ref, payload_ref, pieces_ref, in_sem):
    (pieces,) = incoming([pieces_any], [pieces_ref], in_sem)
    piece = jnp.sum(pieces()[...], axis=0)
    depth = piece.shape[0]
    for at in range(payload_ref.shape[0]):
        payload_ref[at, :depth] = piece
        payload_ref[at, depth:] = products_ref[...]


def curvature_kernel(
    positions_ref,
    counts_ref,
    prev_norm_ref,
    own_any,
    below_any,
    right_any,
    diag_any,
    prev_own_any,
    prev_below_any,
    prev_right_any,
    prev_diag_any,
    total_any,
    patch_any,
    moved_any,
    far_any,
    left_any,
    right_table_any,
    prev_probe_any,
    direction_any,
    probe_direction_any,
    sums_ref,
    tiles_ref,
    prev_tiles_ref,
    total_ref,
    change_ref,
    patch_ref,
    moved_ref,
    far_ref,
    left_ref,
    right_ref,
    prev_probe_ref,
    tall_ref,
    wide_ref,
    in_sems,
    out_sems,
    *,
    probe_scale,
    pieces,
):
    live = live_count(counts_ref)
    width = change_ref.shape[-1]
    kept = [
        halves(patch_any, patch_ref),
        halves(moved_any, moved_ref),
        halves(far_any, far_ref),
    ]
    moves = [(total_any, total_ref), (prev_probe_any, prev_probe_ref)]
    for group, target in (
        ((own_any, below_any, right_any, diag_any), tiles_ref),
        ((prev_own_any, prev_below_any, prev_right_any, prev_diag_any), prev_tiles_ref),
    ):
        moves += [(tile, target.at[at]) for at, tile in enumerate(group)]
    moves += [kept[0][0], kept[1][0], (left_any, left_ref), (right_table_any, right_ref), kept[2][0]]
    moves += [kept[0][1], kept[1][1], kept[2][1]]
    total, prev_probe, *arrivals = incoming(*zip(*moves), in_sems)
    tiles, prev_tiles = arrivals[:4], arrivals[4:8]
    (patch, moved, left, right, far), later = arrivals[8:13], arrivals[13:]

    total()
    depth = 4 * width // pieces
    products = jnp.zeros((1, total_ref.shape[-1]), jnp.float32)
    for piece in range(pieces):
        base = piece * (depth + 1)
        part, rest = divmod(piece * depth, 2 * width)
        half, first = divmod(rest, width)
        lanes = slice(half * (width // 2), (half + 1) * (width // 2))
        change_ref[part, first : first + depth, lanes] = (
            total_ref[base : base + depth, :] * probe_scale
        )
        products = products + total_ref[base + depth : base + depth + 1, :]
    lane = lax.broadcasted_iota(jnp.int32, (1, 128), 1)
    probe_grad = change_ref[...]
    prev_probe()
    grad_norm = jnp.sum(jnp.where(lane == 0, products, 0.0)) + jnp.sum(probe_grad * probe_grad)
    along_prev = jnp.sum(jnp.where(lane == 1, products, 0.0))
    along_prev = along_prev + jnp.sum(probe_grad * prev_probe_ref[...])
    ratio = grad_norm / prev_norm_ref[0]
    descent = grad_norm - ratio * along_prev
    change_ref[...] = ratio * prev_probe_ref[...] - change_ref[...]
    for at, (tile, prev) in enumerate(zip(tiles, prev_tiles)):
        tile()
        prev()
        tiles_ref[at] = ratio * prev_tiles_ref[at] - tiles_ref[at]
    sent = outgoing(
        [tiles_ref.at[0], change_ref], [direction_any, probe_direction_any], out_sems
    )
    row = jnp.where(lane == 5, grad_norm, jnp.where(lane == 6, descent, 0.0))
    sums_ref[...] = row

    def finish(slots, quads):
        row = sums_ref[...]
        for slot, quad in zip(slots, quads):
            square = jnp.sum(quad * quad)
            row = row + jnp.where((lane == 0) | (lane == 1 + slot), square, 0.0)
        sums_ref[...] = row

    linear_frames(
        positions_ref,
        live,
        [(lambda at=at: tiles_ref.at[at]) for at in range(4)],
        lambda: change_ref,
        ((patch, moved, far), later),
        (left, right),
        (tall_ref, wide_ref),
        finish,
    )
    for copy in sent:
        copy.wait()


def update_kernel(
    gathered_ref,
    sums_ref,
    object_any,
    direction_any,
    probe_any,
    probe_direction_any,
    object_new_any,
    probe_new_any,
    norm_ref,
    frames_ref,
    held_ref,
    in_sems,
    out_sems,
):
    sources = [object_any, direction_any, probe_any, probe_direction_any]
    arrivals = incoming(sources, [held_ref.at[at] for at in range(4)], in_sems)
    total = jnp.sum(gathered_ref[...], axis=0)
    local = sums_ref[...]
    lane = lax.broadcasted_iota(jnp.int32, (1, 128), 1)

    def pick(row, at):
        return jnp.sum(jnp.where(lane == at, row, 0.0))

    curvature = pick(total, 0)
    step_size = pick(local, 6) / (0.5 * curvature + 1e-06)
    outs = [object_new_any, probe_new_any]
    sent = []
    for which in range(2):
        field, direction = [arrival() for arrival in arrivals[2 * which : 2 * which + 2]]
        field[...] = field[...] + step_size * direction[...]
        sent += outgoing([field], [outs[which]], out_sems, which)
    norm_ref[0, 0] = pick(local, 5)
    pixels = held_ref.shape[-1] * held_ref.shape[-2]
    for slot in range(frames_ref.shape[-1]):
        frames_ref[0, 0, slot] = pick(local, 1 + slot) / pixels
    for copy in sent:
        copy.wait()


def shaped(*dims):
    return jax.ShapeDtypeStruct(dims, jnp.float32)


def buffer(*dims, dtype=jnp.float32):
    return pltpu.VMEM(dims, dtype)


def arrivals_of(count):
    return pltpu.SemaphoreType.DMA((count,))


def anywhere(count):
    return [pl.BlockSpec(memory_space=pl.ANY)] * count


def in_hbm(count):
    return [pl.BlockSpec(memory_space=pltpu.HBM)] * count


def in_vmem(count):
    return [pl.BlockSpec(memory_space=pltpu.VMEM)] * count


def in_smem(count):
    return [pl.BlockSpec(memory_space=pltpu.SMEM)] * count


def table_buffers(width):
    return [
        buffer(2 * width, 6 * width, dtype=jnp.bfloat16),
        buffer(6 * width, 2 * width, dtype=jnp.bfloat16),
    ]


def dft_scratch(width):
    return [
        buffer(2, 6 * width, width, dtype=jnp.bfloat16),
        buffer(2, width, 6 * width, dtype=jnp.bfloat16),
    ]


def costing(flops):
    return {
        "compiler_params": pltpu.CompilerParams(vmem_limit_bytes=VMEM_BYTES),
        "cost_estimate": pl.CostEstimate(flops=flops, bytes_accessed=10**7, transcendentals=0),
    }


def gradient_call(positions, counts, tiles, probe, measured, tables):
    width = probe.shape[-1]
    slots = measured.shape[2]
    frames = buffer(slots, 2, width, width)
    return pl.pallas_call(
        gradient_kernel,
        out_shape=(shaped(2, width, width),) * 4
        + (shaped(4 * width, width // 2),)
        + (shaped(slots, 2, width, width),) * 3,
        in_specs=in_smem(2) + anywhere(4) + in_hbm(4),
        out_specs=(*anywhere(5), *in_hbm(3)),
        scratch_shapes=[
            buffer(4, 2, width, width),
            buffer(2, width, width),
            buffer(slots, width, width, dtype=measured.dtype),
            *table_buffers(width),
            buffer(4, 2, width, width),
            buffer(4 * width, width // 2),
            frames,
            frames,
            frames,
            *dft_scratch(width),
            arrivals_of(8),
            arrivals_of(11),
        ],
        name="gradient_frames",
        **costing(10**10),
    )(positions, counts, *tiles, probe, measured, *tables)


def fold_call(parts, prev):
    shape = prev.shape
    return pl.pallas_call(
        fold_kernel,
        out_shape=(shaped(*shape), shaped(1, 128)),
        in_specs=anywhere(5),
        out_specs=(*anywhere(1), *in_vmem(1)),
        scratch_shapes=[
            buffer(5, *shape),
            buffer(*shape),
            arrivals_of(5),
            pltpu.SemaphoreType.DMA,
        ],
        name="fold",
        **costing(FOLD_FLOPS),
    )(*parts, prev)


def payload_call(pieces, products, targets):
    return pl.pallas_call(
        payload_kernel,
        out_shape=shaped(targets, pieces.shape[1] + 1, pieces.shape[2]),
        in_specs=anywhere(1) + in_vmem(1),
        out_specs=in_vmem(1)[0],
        scratch_shapes=[buffer(*pieces.shape), arrivals_of(1)],
        name="payload",
        **costing(10**6),
    )(pieces, products)


def curvature_call(positions, counts, prev_norm, tiles, total, pieces, kept, tables, probe_prev, scale):
    width = tiles[0].shape[-1]
    slots = kept[0].shape[0]
    frames = buffer(slots, 2, width, width)
    return pl.pallas_call(
        functools.partial(curvature_kernel, probe_scale=scale, pieces=pieces),
        out_shape=(shaped(2, width, width), shaped(2, width, width), shaped(1, 128)),
        in_specs=in_smem(3) + anywhere(9) + in_hbm(6),
        out_specs=(*in_hbm(2), *in_vmem(1)),
        scratch_shapes=[
            buffer(4, 2, width, width),
            buffer(4, 2, width, width),
            buffer(*total.shape),
            buffer(2, width, width),
            frames,
            frames,
            frames,
            *table_buffers(width),
            buffer(2, width, width),
            *dft_scratch(width),
            arrivals_of(18),
            arrivals_of(2),
        ],
        name="curvature_frames",
        **costing(5 * 10**9),
    )(positions, counts, prev_norm, *tiles, total, *kept, *tables, probe_prev)


def update_call(gathered, sums, arrays, slots):
    shape = arrays[0].shape
    return pl.pallas_call(
        update_kernel,
        out_shape=(shaped(*shape),) * 2 + (shaped(1, 1), shaped(1, 1, slots)),
        in_specs=in_vmem(2) + in_hbm(4),
        out_specs=(*in_hbm(2), *in_smem(2)),
        scratch_shapes=[buffer(4, *shape), arrivals_of(4), arrivals_of(2)],
        name="update",
        **costing(10**6),
    )(gathered, sums, *arrays)


def passed_along(shard, axis, by):
    count = lax.axis_size(axis)
    pairs = [(i, i + by) for i in range(count) if 0 <= i + by < count]
    return lax.ppermute(shard, axis, pairs)


def passed_across(shard, by):
    rows, cols = lax.axis_size("row"), lax.axis_size("col")
    pairs = [
        (row * cols + col, (row + by) * cols + col + by)
        for row in range(rows)
        for col in range(cols)
        if 0 <= row + by < rows and 0 <= col + by < cols
    ]
    return lax.ppermute(shard, ("row", "col"), pairs)


def device_groups(block):
    rows, cols = lax.axis_size("row"), lax.axis_size("col")
    near = [
        [row * cols + first + at for row in range(rows) for at in range(block)]
        for first in range(0, cols, block)
    ]
    return near, [list(members) for members in zip(*near)]


def exchanged(pieces, groups):
    return lax.all_to_all(pieces, ("row", "col"), 0, 0, axis_index_groups=groups)


def copies(piece, groups):
    return jnp.broadcast_to(piece[None], (len(groups[0]),) + piece.shape)


def held(value, *others):
    return lax.optimization_barrier((value,) + others)[0]


def per_device(
    object_field,
    probe_field,
    object_dir_prev,
    probe_dir_prev,
    prev_norm,
    intensities,
    positions,
    counts,
):
    width = probe_field.shape[-1]
    slots = positions.shape[2]
    tables = dft_blocks(width)
    probe_scale = 1.0 / math.sqrt(slots * lax.axis_size("row") * lax.axis_size("col"))
    near, apart = device_groups(4)

    right = passed_along(object_field, "col", -1)
    below = passed_along(object_field, "row", -1)
    diag = passed_along(below, "col", -1)
    prev = held(object_dir_prev, below)
    prev_below = passed_along(prev, "row", -1)
    prev_right = passed_along(prev, "col", -1)
    prev_diag = passed_across(prev, -1)

    own_grad, below_grad, right_grad, diag_grad, probe_part, *kept = gradient_call(
        positions,
        counts,
        (object_field, below, right, diag),
        probe_field,
        intensities,
        tables,
    )
    probe_part, prev_below, prev_right, prev_diag = lax.optimization_barrier(
        (probe_part, prev_below, prev_right, prev_diag)
    )
    corner_part = passed_across(diag_grad, 1)
    from_above = passed_along(below_grad, "row", 1)
    from_left = passed_along(right_grad, "col", 1)
    pieces = exchanged(probe_part.reshape((len(near[0]), -1, width // 2)), near)
    object_grad, products = fold_call(
        (own_grad, from_left, from_above, corner_part), object_dir_prev
    )
    payload = payload_call(pieces, products, len(apart[0]))
    grad_below = passed_along(object_grad, "row", -1)
    grad_right = passed_along(object_grad, "col", -1)
    grad_diag = passed_across(object_grad, -1)
    payload, grad_below, grad_right, grad_diag = lax.optimization_barrier(
        (exchanged(payload, apart), grad_below, grad_right, grad_diag)
    )
    payload = jnp.sum(payload, axis=0)[:, None, :]
    total = exchanged(copies(payload, near), near)
    object_direction, probe_direction, sums = curvature_call(
        positions,
        counts,
        prev_norm.reshape(1),
        (object_grad, grad_below, grad_right, grad_diag)
        + (object_dir_prev, prev_below, prev_right, prev_diag),
        total.reshape(-1, width // 2),
        len(near[0]),
        kept,
        tables,
        probe_dir_prev,
        probe_scale,
    )
    near, apart = device_groups(2)
    across = jnp.sum(exchanged(copies(sums, near), near), axis=0)
    across = exchanged(copies(across, apart), apart)
    object_new, probe_new, norm, frame_curvature = update_call(
        across, sums, (object_field, object_direction, probe_field, probe_direction), slots
    )
    return (
        object_new,
        probe_new,
        object_direction,
        probe_direction,
        norm.reshape(()),
        frame_curvature,
    )


def solution(mesh):
    return jax.shard_map(
        per_device,
        mesh=mesh,
        in_specs=(
            P(None, "row", "col"),
            P(),
            P(None, "row", "col"),
            P(),
            P(),
            P("row", "col", None, None, None),
            P("row", "col", None, None),
            P("row", None),
        ),
        out_specs=(
            P(None, "row", "col"),
            P(),
            P(None, "row", "col"),
            P(),
            P(),
            P("row", "col", None),
        ),
        check_vma=False,
    )
```

```python
import functools
import math

import jax
import jax.numpy as jnp
import numpy as np
from jax import lax
from jax.experimental import pallas as pl
from jax.experimental.pallas import tpu as pltpu
from jax.sharding import PartitionSpec as P

VMEM_BYTES = 60 * 1024 * 1024


def dft_blocks(width):
    at = np.arange(width)
    angle = (np.outer(at, at) % width) * (2.0 * math.pi / width)
    cosine = (np.cos(angle) / math.sqrt(width)).astype(np.float32)
    sine = (np.sin(angle) / math.sqrt(width)).astype(np.float32)

    def thrice(table):
        high = table.astype(jnp.bfloat16)
        low = (table - high.astype(np.float32)).astype(jnp.bfloat16)
        return np.concatenate([high, low, high], axis=1)

    left = np.stack([thrice(cosine), thrice(cosine - sine), thrice(cosine + sine)])
    return left, np.ascontiguousarray(left.transpose(0, 2, 1))


def split_halves(value):
    high = value.astype(jnp.bfloat16)
    low = (value - high.astype(jnp.float32)).astype(jnp.bfloat16)
    return high, low


def three_of(pair):
    return (pair[0] + pair[1], pair[1], pair[0])


def product(left, right):
    return jnp.dot(left, right, preferred_element_type=jnp.float32)


def dft_pairs(pairs, tables, scratch):
    left_ref, right_ref = tables
    tall_ref, wide_ref = scratch
    width = pairs[0][0].shape[0]
    for which, pair in enumerate(pairs):
        for at, part in enumerate(three_of(pair)):
            high, low = split_halves(part)
            tall_ref[which, at, :width] = high
            tall_ref[which, at, width : 2 * width] = high
            tall_ref[which, at, 2 * width :] = low
    results = []
    left_ref = left_ref()
    for which in range(len(pairs)):
        both, second, first = [product(left_ref[at], tall_ref[which, at]) for at in range(3)]
        for at, part in enumerate(three_of((both - second, both - first))):
            high, low = split_halves(part)
            wide_ref[which, at, :, :width] = high
            wide_ref[which, at, :, width : 2 * width] = high
            wide_ref[which, at, :, 2 * width :] = low
    right_ref = right_ref()
    for which in range(len(pairs)):
        both, second, first = [product(wide_ref[which, at], right_ref[at]) for at in range(3)]
        results.append((both - second, both - first))
    return results


def rolled(value, row, col):
    return pltpu.roll(pltpu.roll(value, row, 0), col, 1)


def wrapped(own, below, right, diag, upper, nearer):
    return jnp.where(nearer, jnp.where(upper, own, below), jnp.where(upper, right, diag))


def masks(row, col, width):
    upper = lax.broadcasted_iota(jnp.int32, (width, width), 0) >= row
    nearer = lax.broadcasted_iota(jnp.int32, (width, width), 1) >= col
    return upper, nearer


def corner(positions_ref, slot, width):
    row = lax.rem(positions_ref[0, 0, slot, 0], width)
    col = lax.rem(positions_ref[0, 0, slot, 1], width)
    return row, col


def live_count(counts_ref):
    return counts_ref[0, lax.axis_index("col")]


class Incoming:
    def __init__(self, source, target, semaphore):
        self.target = target
        self.copy = pltpu.make_async_copy(source, target, semaphore)
        self.copy.start()
        self.waiting = True

    def __call__(self):
        if self.waiting:
            self.copy.wait()
            self.waiting = False
        return self.target


def incoming(sources, targets, semaphores):
    return [
        Incoming(source, target, semaphores.at[at])
        for at, (source, target) in enumerate(zip(sources, targets))
    ]


def outgoing(sources, targets, semaphores, first=0):
    sent = [
        pltpu.make_async_copy(source, target, semaphores.at[first + at])
        for at, (source, target) in enumerate(zip(sources, targets))
    ]
    for copy in sent:
        copy.start()
    return sent


def gradient_kernel(
    positions_ref,
    counts_ref,
    own_any,
    below_any,
    right_any,
    diag_any,
    probe_any,
    measured_any,
    left_any,
    right_table_any,
    own_grad_any,
    below_grad_any,
    right_grad_any,
    diag_grad_any,
    probe_grad_any,
    patch_any,
    moved_any,
    far_any,
    tiles_ref,
    probe_ref,
    measured_ref,
    left_ref,
    right_ref,
    grads_ref,
    probe_sum_ref,
    patch_ref,
    moved_ref,
    far_ref,
    tall_ref,
    wide_ref,
    in_sems,
    out_sems,
):
    width = probe_ref.shape[-1]
    live = live_count(counts_ref)
    *ready, left, measured, right = incoming(
        [own_any, below_any, right_any, diag_any, probe_any]
        + [left_any, measured_any.at[0, 0], right_table_any],
        [tiles_ref.at[at] for at in range(4)] + [probe_ref, left_ref, measured_ref, right_ref],
        in_sems,
    )
    for arrival in ready:
        arrival()

    def both(first):
        slots = (first, first + 1)
        spots = [corner(positions_ref, slot, width) for slot in slots]
        waves = []
        for slot, (row, col) in zip(slots, spots):
            upper, nearer = masks(row, col, width)
            for part in range(2):
                patch_ref[slot, part] = wrapped(
                    *[tiles_ref[at, part] for at in range(4)], upper, nearer
                )
                moved_ref[slot, part] = rolled(probe_ref[part], row, col)
            patch_r, patch_i = patch_ref[slot, 0], patch_ref[slot, 1]
            probe_r, probe_i = moved_ref[slot, 0], moved_ref[slot, 1]
            kept = slot < live
            waves.append(
                (
                    jnp.where(kept, probe_r * patch_r - probe_i * patch_i, 0.0),
                    jnp.where(kept, probe_r * patch_i + probe_i * patch_r, 0.0),
                )
            )
        span = pl.ds(first, 2)
        sent = outgoing(
            [patch_ref.at[span], moved_ref.at[span]],
            [patch_any.at[span], moved_any.at[span]],
            out_sems,
            5 + 3 * (first // 2),
        )
        fars = dft_pairs(waves, (left, right), (tall_ref, wide_ref))
        turned = []
        measured()
        for slot, (far_r, far_i) in zip(slots, fars):
            far_ref[slot, 0] = far_r
            far_ref[slot, 1] = far_i
            residue = far_r * far_r + far_i * far_i - measured_ref[slot].astype(jnp.float32)
            turned.append((residue * far_i, residue * far_r))
        sent += outgoing(
            [far_ref.at[span]], [far_any.at[span]], out_sems, 7 + 3 * (first // 2)
        )
        backs = dft_pairs(turned, (left, right), (tall_ref, wide_ref))
        pieces = []
        for slot, (row, col), (back_i, back_r) in zip(slots, spots, backs):
            patch_r, patch_i = patch_ref[slot, 0], patch_ref[slot, 1]
            back_row = lax.rem(width - row, width)
            back_col = lax.rem(width - col, width)
            pieces.append(
                (
                    rolled(patch_r * back_r + patch_i * back_i, back_row, back_col),
                    rolled(patch_r * back_i - patch_i * back_r, back_row, back_col),
                )
            )
        for part in range(2):
            total = pieces[0][part] + pieces[1][part]
            for half in range(2):
                rows = pl.ds((2 * part + half) * width, width)
                side = total[:, half * (width // 2) : (half + 1) * (width // 2)]
                probe_sum_ref[rows, :] = side if first == 0 else probe_sum_ref[rows, :] + side
        for part in range(2):
            sums = [0.0, 0.0, 0.0, 0.0]
            for slot, (row, col), (back_i, back_r) in zip(slots, spots, backs):
                upper, nearer = masks(row, col, width)
                probe_r, probe_i = moved_ref[slot, 0], moved_ref[slot, 1]
                if part == 0:
                    term = probe_r * back_r + probe_i * back_i
                else:
                    term = probe_r * back_i - probe_i * back_r
                close = jnp.where(nearer, term, 0.0)
                beyond = term - close
                for at, side in enumerate((close, beyond)):
                    top = jnp.where(upper, side, 0.0)
                    sums[2 * at] = sums[2 * at] + top
                    sums[2 * at + 1] = sums[2 * at + 1] + (side - top)
            for at, total in enumerate(sums):
                grads_ref[at, part] = total if first == 0 else grads_ref[at, part] + total
        for copy in sent:
            copy.wait()

    both(0)
    pl.when(live > 2)(lambda: both(2))
    outs = [own_grad_any, below_grad_any, right_grad_any, diag_grad_any, probe_grad_any]
    made = [grads_ref.at[at] for at in range(4)] + [probe_sum_ref]
    for copy in outgoing(made, outs, out_sems):
        copy.wait()


def linear_frames(positions_ref, live, tiles, change, kept, tables, scratch, finish):
    own_ref, below_ref, right_ref, diag_ref = [tile() for tile in tiles]
    change_ref = change()
    width = own_ref.shape[-1]

    def both(first, patches, moves, fars):
        slots = (first, first + 1)
        patch_ref, moved_ref = patches(), moves()
        waves = []
        for at, slot in enumerate(slots):
            row, col = corner(positions_ref, slot, width)
            upper, nearer = masks(row, col, width)
            step_r, step_i = [
                wrapped(own_ref[part], below_ref[part], right_ref[part], diag_ref[part], upper, nearer)
                for part in range(2)
            ]
            patch_r, patch_i = patch_ref[at, 0], patch_ref[at, 1]
            probe_r, probe_i = moved_ref[at, 0], moved_ref[at, 1]
            change_r = rolled(change_ref[0], row, col)
            change_i = rolled(change_ref[1], row, col)
            waves.append(
                (
                    probe_r * step_r - probe_i * step_i + change_r * patch_r - change_i * patch_i,
                    probe_r * step_i + probe_i * step_r + change_r * patch_i + change_i * patch_r,
                )
            )
        steps = dft_pairs(waves, tables, scratch)
        far_ref = fars()
        quads = [
            2.0 * (far_ref[at, 0] * step_r + far_ref[at, 1] * step_i)
            for at, (step_r, step_i) in enumerate(steps)
        ]
        finish(slots, quads)

    both(0, *kept[0])
    for arrival in kept[1]:
        arrival()
    pl.when(live > 2)(lambda: both(2, *kept[1]))


def halves(array, ref):
    return [(array.at[pl.ds(first, 2)], ref.at[pl.ds(first, 2)]) for first in (0, 2)]


def curvature_kernel(
    positions_ref,
    counts_ref,
    prev_norm_ref,
    own_any,
    below_any,
    right_any,
    diag_any,
    prev_own_any,
    prev_below_any,
    prev_right_any,
    prev_diag_any,
    total_any,
    patch_any,
    moved_any,
    far_any,
    left_any,
    right_table_any,
    prev_probe_any,
    direction_any,
    probe_direction_any,
    sums_ref,
    tiles_ref,
    prev_tiles_ref,
    total_ref,
    change_ref,
    patch_ref,
    moved_ref,
    far_ref,
    left_ref,
    right_ref,
    prev_probe_ref,
    tall_ref,
    wide_ref,
    in_sems,
    out_sems,
    *,
    probe_scale,
    pieces,
):
    live = live_count(counts_ref)
    width = change_ref.shape[-1]
    kept = [
        halves(patch_any, patch_ref),
        halves(moved_any, moved_ref),
        halves(far_any, far_ref),
    ]
    moves = [(total_any, total_ref), (prev_probe_any, prev_probe_ref)]
    for group, target in (
        ((own_any, below_any, right_any, diag_any), tiles_ref),
        ((prev_own_any, prev_below_any, prev_right_any, prev_diag_any), prev_tiles_ref),
    ):
        moves += [(tile, target.at[at]) for at, tile in enumerate(group)]
    moves += [kept[0][0], kept[1][0], (left_any, left_ref), (right_table_any, right_ref), kept[2][0]]
    moves += [kept[0][1], kept[1][1], kept[2][1]]
    total, prev_probe, *arrivals = incoming(*zip(*moves), in_sems)
    tiles, prev_tiles = arrivals[:4], arrivals[4:8]
    (patch, moved, left, right, far), later = arrivals[8:13], arrivals[13:]

    total()
    depth = 4 * width // pieces
    products = jnp.zeros((2, total_ref.shape[-1]), jnp.float32)
    for piece in range(pieces):
        base = piece * (depth + 2)
        part, rest = divmod(piece * depth, 2 * width)
        half, first = divmod(rest, width)
        lanes = slice(half * (width // 2), (half + 1) * (width // 2))
        change_ref[part, first : first + depth, lanes] = (
            total_ref[base : base + depth, :] * probe_scale
        )
        products = products + total_ref[base + depth : base + depth + 2, :]
    lane = lax.broadcasted_iota(jnp.int32, (1, 128), 1)
    probe_grad = change_ref[...]
    prev_probe()
    grad_norm = whole_sum(products[:1]) + whole_sum(probe_grad * probe_grad)
    along_prev = whole_sum(products[1:]) + whole_sum(probe_grad * prev_probe_ref[...])
    ratio = grad_norm / prev_norm_ref[0]
    descent = grad_norm - ratio * along_prev
    change_ref[...] = ratio * prev_probe_ref[...] - change_ref[...]
    for at, (tile, prev) in enumerate(zip(tiles, prev_tiles)):
        tile()
        prev()
        tiles_ref[at] = ratio * prev_tiles_ref[at] - tiles_ref[at]
    sent = outgoing(
        [tiles_ref.at[0], change_ref], [direction_any, probe_direction_any], out_sems
    )
    row = jnp.where(lane == 5, grad_norm, jnp.where(lane == 6, descent, 0.0))
    sums_ref[...] = row

    def finish(slots, quads):
        row = sums_ref[...]
        for slot, quad in zip(slots, quads):
            square = whole_sum(quad * quad)
            row = row + jnp.where((lane == 0) | (lane == 1 + slot), square, 0.0)
        sums_ref[...] = row

    linear_frames(
        positions_ref,
        live,
        [(lambda at=at: tiles_ref.at[at]) for at in range(4)],
        lambda: change_ref,
        ((patch, moved, far), later),
        (left, right),
        (tall_ref, wide_ref),
        finish,
    )
    for copy in sent:
        copy.wait()


def update_kernel(
    gathered_ref,
    sums_ref,
    object_any,
    direction_any,
    probe_any,
    probe_direction_any,
    object_new_any,
    probe_new_any,
    norm_ref,
    frames_ref,
    held_ref,
    in_sems,
    out_sems,
):
    sources = [object_any, direction_any, probe_any, probe_direction_any]
    arrivals = incoming(sources, [held_ref.at[at] for at in range(4)], in_sems)
    total = jnp.sum(gathered_ref[...], axis=0)
    local = sums_ref[...]
    lane = lax.broadcasted_iota(jnp.int32, (1, 128), 1)

    def pick(row, at):
        return jnp.sum(jnp.where(lane == at, row, 0.0), axis=1, keepdims=True)

    curvature = pick(total, 0)
    step_size = pick(local, 6) / (0.5 * curvature + 1e-06)
    outs = [object_new_any, probe_new_any]
    sent = []
    for which in range(2):
        field, direction = [arrival() for arrival in arrivals[2 * which : 2 * which + 2]]
        field[...] = field[...] + step_size * direction[...]
        sent += outgoing([field], [outs[which]], out_sems, which)
    norm_ref[...] = pick(local, 5)
    pixels = held_ref.shape[-1] * held_ref.shape[-2]
    frames_ref[0] = local[:, 1 : 1 + frames_ref.shape[-1]] / pixels
    for copy in sent:
        copy.wait()


def whole_sum(value):
    return jnp.sum(jnp.sum(value, axis=tuple(range(value.ndim - 1)))[None], axis=1, keepdims=True)


def shaped(*dims):
    return jax.ShapeDtypeStruct(dims, jnp.float32)


def buffer(*dims, dtype=jnp.float32):
    return pltpu.VMEM(dims, dtype)


def arrivals_of(count):
    return pltpu.SemaphoreType.DMA((count,))


def anywhere(count):
    return [pl.BlockSpec(memory_space=pl.ANY)] * count


def in_hbm(count):
    return [pl.BlockSpec(memory_space=pltpu.HBM)] * count


def in_vmem(count):
    return [pl.BlockSpec(memory_space=pltpu.VMEM)] * count


def in_smem(count):
    return [pl.BlockSpec(memory_space=pltpu.SMEM)] * count


def table_buffers(width):
    return [
        buffer(3, width, 3 * width, dtype=jnp.bfloat16),
        buffer(3, 3 * width, width, dtype=jnp.bfloat16),
    ]


def dft_scratch(width):
    return [
        buffer(2, 3, 3 * width, width, dtype=jnp.bfloat16),
        buffer(2, 3, width, 3 * width, dtype=jnp.bfloat16),
    ]


def costing(flops):
    return {
        "compiler_params": pltpu.CompilerParams(vmem_limit_bytes=VMEM_BYTES),
        "cost_estimate": pl.CostEstimate(flops=flops, bytes_accessed=10**7, transcendentals=0),
    }


def gradient_call(positions, counts, tiles, probe, measured, tables):
    width = probe.shape[-1]
    slots = measured.shape[2]
    frames = buffer(slots, 2, width, width)
    return pl.pallas_call(
        gradient_kernel,
        out_shape=(shaped(2, width, width),) * 4
        + (shaped(4 * width, width // 2),)
        + (shaped(slots, 2, width, width),) * 3,
        in_specs=in_smem(2) + anywhere(4) + in_hbm(4),
        out_specs=(*anywhere(5), *in_hbm(3)),
        scratch_shapes=[
            buffer(4, 2, width, width),
            buffer(2, width, width),
            buffer(slots, width, width, dtype=measured.dtype),
            *table_buffers(width),
            buffer(4, 2, width, width),
            buffer(4 * width, width // 2),
            frames,
            frames,
            frames,
            *dft_scratch(width),
            arrivals_of(8),
            arrivals_of(11),
        ],
        name="gradient_frames",
        **costing(10**10),
    )(positions, counts, *tiles, probe, measured, *tables)


def curvature_call(positions, counts, prev_norm, tiles, total, pieces, kept, tables, probe_prev, scale):
    width = tiles[0].shape[-1]
    slots = kept[0].shape[0]
    frames = buffer(slots, 2, width, width)
    return pl.pallas_call(
        functools.partial(curvature_kernel, probe_scale=scale, pieces=pieces),
        out_shape=(shaped(2, width, width), shaped(2, width, width), shaped(1, 128)),
        in_specs=in_smem(3) + anywhere(9) + in_hbm(6),
        out_specs=(*in_hbm(2), *in_vmem(1)),
        scratch_shapes=[
            buffer(4, 2, width, width),
            buffer(4, 2, width, width),
            buffer(*total.shape),
            buffer(2, width, width),
            frames,
            frames,
            frames,
            *table_buffers(width),
            buffer(2, width, width),
            *dft_scratch(width),
            arrivals_of(18),
            arrivals_of(2),
        ],
        name="curvature_frames",
        **costing(5 * 10**9),
    )(positions, counts, prev_norm, *tiles, total, *kept, *tables, probe_prev)


def update_call(gathered, sums, arrays, slots):
    shape = arrays[0].shape
    return pl.pallas_call(
        update_kernel,
        out_shape=(shaped(*shape),) * 2 + (shaped(1, 1), shaped(1, 1, slots)),
        in_specs=in_vmem(2) + in_hbm(4),
        out_specs=(*in_hbm(2), *in_vmem(2)),
        scratch_shapes=[buffer(4, *shape), arrivals_of(4), arrivals_of(2)],
        name="update",
        **costing(10**6),
    )(gathered, sums, *arrays)


def passed_along(shard, axis, by):
    count = lax.axis_size(axis)
    pairs = [(i, i + by) for i in range(count) if 0 <= i + by < count]
    return lax.ppermute(shard, axis, pairs)


def passed_across(shard, by):
    rows, cols = lax.axis_size("row"), lax.axis_size("col")
    pairs = [
        (row * cols + col, (row + by) * cols + col + by)
        for row in range(rows)
        for col in range(cols)
        if 0 <= row + by < rows and 0 <= col + by < cols
    ]
    return lax.ppermute(shard, ("row", "col"), pairs)


def device_groups(block):
    rows, cols = lax.axis_size("row"), lax.axis_size("col")
    near = [
        [row * cols + first + at for row in range(rows) for at in range(block)]
        for first in range(0, cols, block)
    ]
    return near, [list(members) for members in zip(*near)]


def exchanged(pieces, groups):
    return lax.all_to_all(pieces, ("row", "col"), 0, 0, axis_index_groups=groups)


def copies(piece, groups):
    return jnp.broadcast_to(piece[None], (len(groups[0]),) + piece.shape)


def held(value, *others):
    return lax.optimization_barrier((value,) + others)[0]


def per_device(
    object_field,
    probe_field,
    object_dir_prev,
    probe_dir_prev,
    prev_norm,
    intensities,
    positions,
    counts,
):
    width = probe_field.shape[-1]
    slots = positions.shape[2]
    tables = dft_blocks(width)
    probe_scale = 1.0 / math.sqrt(slots * lax.axis_size("row") * lax.axis_size("col"))
    near, apart = device_groups(4)

    right = passed_along(object_field, "col", -1)
    below = passed_along(object_field, "row", -1)
    diag = passed_along(below, "col", -1)
    prev = held(object_dir_prev, below)
    prev_below = passed_along(prev, "row", -1)
    prev_right = passed_along(prev, "col", -1)
    prev_diag = passed_across(prev, -1)

    own_grad, below_grad, right_grad, diag_grad, probe_part, *kept = gradient_call(
        positions,
        counts,
        (object_field, below, right, diag),
        probe_field,
        intensities,
        tables,
    )
    probe_part, prev_below, prev_right, prev_diag = lax.optimization_barrier(
        (probe_part, prev_below, prev_right, prev_diag)
    )
    corner_part = passed_across(diag_grad, 1)
    from_above = passed_along(below_grad, "row", 1)
    from_left = passed_along(right_grad, "col", 1)
    pieces = exchanged(probe_part.reshape((len(near[0]), -1, width // 2)), near)
    object_grad = own_grad + from_left + from_above + corner_part
    sums = [
        jnp.sum(jnp.sum(object_grad * other, axis=(0, 1)).reshape(2, -1), axis=0, keepdims=True)
        for other in (object_grad, object_dir_prev)
    ]
    payload = copies(jnp.concatenate([jnp.sum(pieces, axis=0), *sums], axis=0), apart)
    grad_below = passed_along(object_grad, "row", -1)
    grad_right = passed_along(object_grad, "col", -1)
    grad_diag = passed_across(object_grad, -1)
    payload, grad_below, grad_right, grad_diag = lax.optimization_barrier(
        (exchanged(payload, apart), grad_below, grad_right, grad_diag)
    )
    payload = jnp.sum(payload, axis=0)[:, None, :]
    total = exchanged(copies(payload, near), near)
    object_direction, probe_direction, sums = curvature_call(
        positions,
        counts,
        prev_norm.reshape(1),
        (object_grad, grad_below, grad_right, grad_diag)
        + (object_dir_prev, prev_below, prev_right, prev_diag),
        total.reshape(-1, width // 2),
        len(near[0]),
        kept,
        tables,
        probe_dir_prev,
        probe_scale,
    )
    near, apart = device_groups(2)
    across = jnp.sum(exchanged(copies(sums, near), near), axis=0)
    across = exchanged(copies(across, apart), apart)
    object_new, probe_new, norm, frame_curvature = update_call(
        across, sums, (object_field, object_direction, probe_field, probe_direction), slots
    )
    return (
        object_new,
        probe_new,
        object_direction,
        probe_direction,
        norm.reshape(()),
        frame_curvature,
    )


def solution(mesh):
    return jax.shard_map(
        per_device,
        mesh=mesh,
        in_specs=(
            P(None, "row", "col"),
            P(),
            P(None, "row", "col"),
            P(),
            P(),
            P("row", "col", None, None, None),
            P("row", "col", None, None),
            P("row", None),
        ),
        out_specs=(
            P(None, "row", "col"),
            P(),
            P(None, "row", "col"),
            P(),
            P(),
            P("row", "col", None),
        ),
        check_vma=False,
    )
```

```python
import functools
import math

import jax
import jax.numpy as jnp
import numpy as np
from jax import lax
from jax.experimental import pallas as pl
from jax.experimental.pallas import tpu as pltpu
from jax.sharding import PartitionSpec as P

VMEM_BYTES = 60 * 1024 * 1024


def dft_blocks(width):
    at = np.arange(width)
    angle = (np.outer(at, at) % width) * (2.0 * math.pi / width)
    cosine = (np.cos(angle) / math.sqrt(width)).astype(np.float32)
    sine = (np.sin(angle) / math.sqrt(width)).astype(np.float32)

    def thrice(table):
        high = table.astype(jnp.bfloat16)
        low = (table - high.astype(np.float32)).astype(jnp.bfloat16)
        return np.concatenate([high, low, high], axis=1)

    left = np.stack([thrice(cosine), thrice(cosine - sine), thrice(cosine + sine)])
    return left, np.ascontiguousarray(left.transpose(0, 2, 1))


def split_halves(value):
    high = value.astype(jnp.bfloat16)
    low = (value - high.astype(jnp.float32)).astype(jnp.bfloat16)
    return high, low


def three_of(pair):
    return (pair[0] + pair[1], pair[1], pair[0])


def product(left, right):
    return jnp.dot(left, right, preferred_element_type=jnp.float32)


def dft_pairs(pairs, tables, scratch):
    left_ref, right_ref = tables
    tall_ref, wide_ref = scratch
    width = pairs[0][0].shape[0]
    for which, pair in enumerate(pairs):
        for at, part in enumerate(three_of(pair)):
            high, low = split_halves(part)
            tall_ref[which, at, :width] = high
            tall_ref[which, at, width : 2 * width] = high
            tall_ref[which, at, 2 * width :] = low
    results = []
    left_ref = left_ref()
    for which in range(len(pairs)):
        both, second, first = [product(left_ref[at], tall_ref[which, at]) for at in range(3)]
        for at, part in enumerate(three_of((both - second, both - first))):
            high, low = split_halves(part)
            wide_ref[which, at, :, :width] = high
            wide_ref[which, at, :, width : 2 * width] = high
            wide_ref[which, at, :, 2 * width :] = low
    right_ref = right_ref()
    for which in range(len(pairs)):
        both, second, first = [product(wide_ref[which, at], right_ref[at]) for at in range(3)]
        results.append((both - second, both - first))
    return results


def rolled(value, row, col):
    return pltpu.roll(pltpu.roll(value, row, 0), col, 1)


def wrapped(own, below, right, diag, upper, nearer):
    return jnp.where(nearer, jnp.where(upper, own, below), jnp.where(upper, right, diag))


def masks(row, col, width):
    upper = lax.broadcasted_iota(jnp.int32, (width, width), 0) >= row
    nearer = lax.broadcasted_iota(jnp.int32, (width, width), 1) >= col
    return upper, nearer


def corner(positions_ref, slot, width):
    row = lax.rem(positions_ref[0, 0, slot, 0], width)
    col = lax.rem(positions_ref[0, 0, slot, 1], width)
    return row, col


def live_count(counts_ref):
    return counts_ref[0, lax.axis_index("col")]


class Incoming:
    def __init__(self, source, target, semaphore):
        self.target = target
        self.copy = pltpu.make_async_copy(source, target, semaphore)
        self.copy.start()
        self.waiting = True

    def __call__(self):
        if self.waiting:
            self.copy.wait()
            self.waiting = False
        return self.target


def incoming(sources, targets, semaphores):
    return [
        Incoming(source, target, semaphores.at[at])
        for at, (source, target) in enumerate(zip(sources, targets))
    ]


def outgoing(sources, targets, semaphores, first=0):
    sent = [
        pltpu.make_async_copy(source, target, semaphores.at[first + at])
        for at, (source, target) in enumerate(zip(sources, targets))
    ]
    for copy in sent:
        copy.start()
    return sent


def gradient_kernel(
    positions_ref,
    counts_ref,
    own_any,
    below_any,
    right_any,
    diag_any,
    probe_any,
    measured_any,
    left_any,
    right_table_any,
    own_grad_any,
    below_grad_any,
    right_grad_any,
    diag_grad_any,
    probe_grad_any,
    patch_any,
    moved_any,
    far_any,
    tiles_ref,
    probe_ref,
    measured_ref,
    left_ref,
    right_ref,
    grads_ref,
    probe_sum_ref,
    patch_ref,
    moved_ref,
    far_ref,
    tall_ref,
    wide_ref,
    in_sems,
    out_sems,
):
    width = probe_ref.shape[-1]
    live = live_count(counts_ref)
    *ready, left, measured, right = incoming(
        [own_any, below_any, right_any, diag_any, probe_any]
        + [left_any, measured_any.at[0, 0], right_table_any],
        [tiles_ref.at[at] for at in range(4)] + [probe_ref, left_ref, measured_ref, right_ref],
        in_sems,
    )
    for arrival in ready:
        arrival()

    def both(first):
        slots = (first, first + 1)
        spots = [corner(positions_ref, slot, width) for slot in slots]
        waves = []
        for slot, (row, col) in zip(slots, spots):
            upper, nearer = masks(row, col, width)
            for part in range(2):
                patch_ref[slot, part] = wrapped(
                    *[tiles_ref[at, part] for at in range(4)], upper, nearer
                )
                moved_ref[slot, part] = rolled(probe_ref[part], row, col)
            patch_r, patch_i = patch_ref[slot, 0], patch_ref[slot, 1]
            probe_r, probe_i = moved_ref[slot, 0], moved_ref[slot, 1]
            kept = slot < live
            waves.append(
                (
                    jnp.where(kept, probe_r * patch_r - probe_i * patch_i, 0.0),
                    jnp.where(kept, probe_r * patch_i + probe_i * patch_r, 0.0),
                )
            )
        span = pl.ds(first, 2)
        sent = outgoing(
            [patch_ref.at[span], moved_ref.at[span]],
            [patch_any.at[span], moved_any.at[span]],
            out_sems,
            5 + 3 * (first // 2),
        )
        fars = dft_pairs(waves, (left, right), (tall_ref, wide_ref))
        turned = []
        measured()
        for slot, (far_r, far_i) in zip(slots, fars):
            far_ref[slot, 0] = far_r
            far_ref[slot, 1] = far_i
            residue = far_r * far_r + far_i * far_i - measured_ref[slot].astype(jnp.float32)
            turned.append((residue * far_i, residue * far_r))
        sent += outgoing(
            [far_ref.at[span]], [far_any.at[span]], out_sems, 7 + 3 * (first // 2)
        )
        backs = dft_pairs(turned, (left, right), (tall_ref, wide_ref))
        pieces = []
        for slot, (row, col), (back_i, back_r) in zip(slots, spots, backs):
            patch_r, patch_i = patch_ref[slot, 0], patch_ref[slot, 1]
            back_row = lax.rem(width - row, width)
            back_col = lax.rem(width - col, width)
            pieces.append(
                (
                    rolled(patch_r * back_r + patch_i * back_i, back_row, back_col),
                    rolled(patch_r * back_i - patch_i * back_r, back_row, back_col),
                )
            )
        for part in range(2):
            total = pieces[0][part] + pieces[1][part]
            for half in range(2):
                rows = pl.ds((2 * part + half) * width, width)
                side = total[:, half * (width // 2) : (half + 1) * (width // 2)]
                probe_sum_ref[rows, :] = side if first == 0 else probe_sum_ref[rows, :] + side
        for part in range(2):
            sums = [0.0, 0.0, 0.0, 0.0]
            for slot, (row, col), (back_i, back_r) in zip(slots, spots, backs):
                upper, nearer = masks(row, col, width)
                probe_r, probe_i = moved_ref[slot, 0], moved_ref[slot, 1]
                if part == 0:
                    term = probe_r * back_r + probe_i * back_i
                else:
                    term = probe_r * back_i - probe_i * back_r
                close = jnp.where(nearer, term, 0.0)
                beyond = term - close
                for at, side in enumerate((close, beyond)):
                    top = jnp.where(upper, side, 0.0)
                    sums[2 * at] = sums[2 * at] + top
                    sums[2 * at + 1] = sums[2 * at + 1] + (side - top)
            for at, total in enumerate(sums):
                grads_ref[at, part] = total if first == 0 else grads_ref[at, part] + total
        for copy in sent:
            copy.wait()

    both(0)
    pl.when(live > 2)(lambda: both(2))
    outs = [own_grad_any, below_grad_any, right_grad_any, diag_grad_any, probe_grad_any]
    made = [grads_ref.at[at] for at in range(4)] + [probe_sum_ref]
    for copy in outgoing(made, outs, out_sems):
        copy.wait()


def linear_frames(positions_ref, live, tiles, change, kept, tables, scratch, finish):
    own_ref, below_ref, right_ref, diag_ref = [tile() for tile in tiles]
    change_ref = change()
    width = own_ref.shape[-1]

    def both(first, patches, moves, fars):
        slots = (first, first + 1)
        patch_ref, moved_ref = patches(), moves()
        waves = []
        for at, slot in enumerate(slots):
            row, col = corner(positions_ref, slot, width)
            upper, nearer = masks(row, col, width)
            step_r, step_i = [
                wrapped(own_ref[part], below_ref[part], right_ref[part], diag_ref[part], upper, nearer)
                for part in range(2)
            ]
            patch_r, patch_i = patch_ref[at, 0], patch_ref[at, 1]
            probe_r, probe_i = moved_ref[at, 0], moved_ref[at, 1]
            change_r = rolled(change_ref[0], row, col)
            change_i = rolled(change_ref[1], row, col)
            waves.append(
                (
                    probe_r * step_r - probe_i * step_i + change_r * patch_r - change_i * patch_i,
                    probe_r * step_i + probe_i * step_r + change_r * patch_i + change_i * patch_r,
                )
            )
        steps = dft_pairs(waves, tables, scratch)
        far_ref = fars()
        quads = [
            2.0 * (far_ref[at, 0] * step_r + far_ref[at, 1] * step_i)
            for at, (step_r, step_i) in enumerate(steps)
        ]
        finish(slots, quads)

    both(0, *kept[0])
    for arrival in kept[1]:
        arrival()
    pl.when(live > 2)(lambda: both(2, *kept[1]))


def halves(array, ref):
    return [(array.at[pl.ds(first, 2)], ref.at[pl.ds(first, 2)]) for first in (0, 2)]


def joined_kernel(*refs):
    *sources, out_any, held_ref, in_sems, out_sem = refs
    count = len(sources)
    arrivals = incoming(sources, [held_ref.at[at] for at in range(count)], in_sems)
    for arrival in arrivals:
        arrival()
    if count > 1:
        held_ref[0] = sum((held_ref[at] for at in range(1, count)), held_ref[0])
    copy = pltpu.make_async_copy(held_ref.at[0], out_any, out_sem)
    copy.start()
    copy.wait()


def curvature_kernel(
    positions_ref,
    counts_ref,
    prev_norm_ref,
    own_any,
    below_any,
    right_any,
    diag_any,
    prev_own_any,
    prev_below_any,
    prev_right_any,
    prev_diag_any,
    total_any,
    patch_any,
    moved_any,
    far_any,
    left_any,
    right_table_any,
    prev_probe_any,
    direction_any,
    probe_direction_any,
    sums_ref,
    tiles_ref,
    prev_tiles_ref,
    total_ref,
    change_ref,
    patch_ref,
    moved_ref,
    far_ref,
    left_ref,
    right_ref,
    prev_probe_ref,
    tall_ref,
    wide_ref,
    in_sems,
    out_sems,
    *,
    probe_scale,
    pieces,
):
    live = live_count(counts_ref)
    width = change_ref.shape[-1]
    kept = [
        halves(patch_any, patch_ref),
        halves(moved_any, moved_ref),
        halves(far_any, far_ref),
    ]
    moves = [(total_any, total_ref), (prev_probe_any, prev_probe_ref)]
    for group, target in (
        ((own_any, below_any, right_any, diag_any), tiles_ref),
        ((prev_own_any, prev_below_any, prev_right_any, prev_diag_any), prev_tiles_ref),
    ):
        moves += [(tile, target.at[at]) for at, tile in enumerate(group)]
    moves += [kept[0][0], kept[1][0], (left_any, left_ref), (right_table_any, right_ref), kept[2][0]]
    moves += [kept[0][1], kept[1][1], kept[2][1]]
    total, prev_probe, *arrivals = incoming(*zip(*moves), in_sems)
    tiles, prev_tiles = arrivals[:4], arrivals[4:8]
    (patch, moved, left, right, far), later = arrivals[8:13], arrivals[13:]

    total()
    depth = 4 * width // pieces
    products = jnp.zeros((2, total_ref.shape[-1]), jnp.float32)
    for piece in range(pieces):
        base = piece * (depth + 2)
        part, rest = divmod(piece * depth, 2 * width)
        half, first = divmod(rest, width)
        lanes = slice(half * (width // 2), (half + 1) * (width // 2))
        change_ref[part, first : first + depth, lanes] = (
            total_ref[base : base + depth, :] * probe_scale
        )
        products = products + total_ref[base + depth : base + depth + 2, :]
    lane = lax.broadcasted_iota(jnp.int32, (1, 128), 1)
    probe_grad = change_ref[...]
    prev_probe()
    grad_norm = whole_sum(products[:1]) + whole_sum(probe_grad * probe_grad)
    along_prev = whole_sum(products[1:]) + whole_sum(probe_grad * prev_probe_ref[...])
    ratio = grad_norm / prev_norm_ref[0]
    descent = grad_norm - ratio * along_prev
    change_ref[...] = ratio * prev_probe_ref[...] - change_ref[...]
    for at, (tile, prev) in enumerate(zip(tiles, prev_tiles)):
        tile()
        prev()
        tiles_ref[at] = ratio * prev_tiles_ref[at] - tiles_ref[at]
    sent = outgoing(
        [tiles_ref.at[0], change_ref], [direction_any, probe_direction_any], out_sems
    )
    row = jnp.where(lane == 5, grad_norm, jnp.where(lane == 6, descent, 0.0))
    sums_ref[...] = row

    def finish(slots, quads):
        row = sums_ref[...]
        for slot, quad in zip(slots, quads):
            square = whole_sum(quad * quad)
            row = row + jnp.where((lane == 0) | (lane == 1 + slot), square, 0.0)
        sums_ref[...] = row

    linear_frames(
        positions_ref,
        live,
        [(lambda at=at: tiles_ref.at[at]) for at in range(4)],
        lambda: change_ref,
        ((patch, moved, far), later),
        (left, right),
        (tall_ref, wide_ref),
        finish,
    )
    for copy in sent:
        copy.wait()


def update_kernel(
    gathered_any,
    sums_any,
    object_any,
    direction_any,
    probe_any,
    probe_direction_any,
    object_new_any,
    probe_new_any,
    norm_ref,
    frames_ref,
    gathered_ref,
    sums_ref,
    held_ref,
    in_sems,
    out_sems,
):
    sources = [gathered_any, sums_any, object_any, direction_any, probe_any, probe_direction_any]
    targets = [gathered_ref, sums_ref] + [held_ref.at[at] for at in range(4)]
    gathered, sums, *arrivals = incoming(sources, targets, in_sems)
    total = jnp.sum(gathered()[...], axis=0)
    local = sums()[...]
    lane = lax.broadcasted_iota(jnp.int32, (1, 128), 1)

    def pick(row, at):
        return jnp.sum(jnp.where(lane == at, row, 0.0), axis=1, keepdims=True)

    curvature = pick(total, 0)
    step_size = pick(local, 6) / (0.5 * curvature + 1e-06)
    outs = [object_new_any, probe_new_any]
    sent = []
    for which in range(2):
        field, direction = [arrival() for arrival in arrivals[2 * which : 2 * which + 2]]
        field[...] = field[...] + step_size * direction[...]
        sent += outgoing([field], [outs[which]], out_sems, which)
    norm_ref[...] = pick(local, 5)
    pixels = held_ref.shape[-1] * held_ref.shape[-2]
    frames_ref[0] = local[:, 1 : 1 + frames_ref.shape[-1]] / pixels
    for copy in sent:
        copy.wait()


def whole_sum(value):
    return jnp.sum(jnp.sum(value, axis=tuple(range(value.ndim - 1)))[None], axis=1, keepdims=True)


def shaped(*dims):
    return jax.ShapeDtypeStruct(dims, jnp.float32)


def buffer(*dims, dtype=jnp.float32):
    return pltpu.VMEM(dims, dtype)


def arrivals_of(count):
    return pltpu.SemaphoreType.DMA((count,))


def anywhere(count):
    return [pl.BlockSpec(memory_space=pl.ANY)] * count


def in_hbm(count):
    return [pl.BlockSpec(memory_space=pltpu.HBM)] * count


def in_vmem(count):
    return [pl.BlockSpec(memory_space=pltpu.VMEM)] * count


def in_smem(count):
    return [pl.BlockSpec(memory_space=pltpu.SMEM)] * count


def table_buffers(width):
    return [
        buffer(3, width, 3 * width, dtype=jnp.bfloat16),
        buffer(3, 3 * width, width, dtype=jnp.bfloat16),
    ]


def dft_scratch(width):
    return [
        buffer(2, 3, 3 * width, width, dtype=jnp.bfloat16),
        buffer(2, 3, width, 3 * width, dtype=jnp.bfloat16),
    ]


def costing(flops):
    return {
        "compiler_params": pltpu.CompilerParams(vmem_limit_bytes=VMEM_BYTES),
        "cost_estimate": pl.CostEstimate(flops=flops, bytes_accessed=10**7, transcendentals=0),
    }


def gradient_call(positions, counts, tiles, probe, measured, tables):
    width = probe.shape[-1]
    slots = measured.shape[2]
    frames = buffer(slots, 2, width, width)
    return pl.pallas_call(
        gradient_kernel,
        out_shape=(shaped(2, width, width),) * 4
        + (shaped(4 * width, width // 2),)
        + (shaped(slots, 2, width, width),) * 3,
        in_specs=in_smem(2) + anywhere(4) + in_hbm(4),
        out_specs=(*anywhere(5), *in_hbm(3)),
        scratch_shapes=[
            buffer(4, 2, width, width),
            buffer(2, width, width),
            buffer(slots, width, width, dtype=measured.dtype),
            *table_buffers(width),
            buffer(4, 2, width, width),
            buffer(4 * width, width // 2),
            frames,
            frames,
            frames,
            *dft_scratch(width),
            arrivals_of(8),
            arrivals_of(11),
        ],
        name="gradient_frames",
        **costing(10**10),
    )(positions, counts, *tiles, probe, measured, *tables)


def joined_call(arrays, flops):
    shape = arrays[0].shape
    return pl.pallas_call(
        joined_kernel,
        out_shape=shaped(*shape),
        in_specs=anywhere(len(arrays)),
        out_specs=anywhere(1)[0],
        scratch_shapes=[
            buffer(len(arrays), *shape),
            arrivals_of(len(arrays)),
            pltpu.SemaphoreType.DMA,
        ],
        name="joined",
        **costing(flops),
    )(*arrays)


def curvature_call(positions, counts, prev_norm, tiles, total, pieces, kept, tables, probe_prev, scale):
    width = tiles[0].shape[-1]
    slots = kept[0].shape[0]
    frames = buffer(slots, 2, width, width)
    return pl.pallas_call(
        functools.partial(curvature_kernel, probe_scale=scale, pieces=pieces),
        out_shape=(shaped(2, width, width), shaped(2, width, width), shaped(1, 128)),
        in_specs=in_smem(3) + anywhere(9) + in_hbm(6),
        out_specs=(*in_hbm(2), *in_vmem(1)),
        scratch_shapes=[
            buffer(4, 2, width, width),
            buffer(4, 2, width, width),
            buffer(*total.shape),
            buffer(2, width, width),
            frames,
            frames,
            frames,
            *table_buffers(width),
            buffer(2, width, width),
            *dft_scratch(width),
            arrivals_of(18),
            arrivals_of(2),
        ],
        name="curvature_frames",
        **costing(5 * 10**9),
    )(positions, counts, prev_norm, *tiles, total, *kept, *tables, probe_prev)


def update_call(gathered, sums, arrays, slots):
    shape = arrays[0].shape
    return pl.pallas_call(
        update_kernel,
        out_shape=(shaped(*shape),) * 2 + (shaped(1, 1), shaped(1, 1, slots)),
        in_specs=anywhere(2) + in_hbm(4),
        out_specs=(*in_hbm(2), *in_vmem(2)),
        scratch_shapes=[
            buffer(*gathered.shape),
            buffer(*sums.shape),
            buffer(4, *shape),
            arrivals_of(6),
            arrivals_of(2),
        ],
        name="update",
        **costing(10**6),
    )(gathered, sums, *arrays)


def passed_along(shard, axis, by):
    count = lax.axis_size(axis)
    pairs = [(i, i + by) for i in range(count) if 0 <= i + by < count]
    return lax.ppermute(shard, axis, pairs)


def device_groups(block):
    rows, cols = lax.axis_size("row"), lax.axis_size("col")
    near = [
        [row * cols + first + at for row in range(rows) for at in range(block)]
        for first in range(0, cols, block)
    ]
    return near, [list(members) for members in zip(*near)]


def exchanged(pieces, groups):
    return lax.all_to_all(pieces, ("row", "col"), 0, 0, axis_index_groups=groups)


def copies(piece, groups):
    return jnp.broadcast_to(piece[None], (len(groups[0]),) + piece.shape)


def held(value, *others):
    return lax.optimization_barrier((value,) + others)[0]


def per_device(
    object_field,
    probe_field,
    object_dir_prev,
    probe_dir_prev,
    prev_norm,
    intensities,
    positions,
    counts,
):
    width = probe_field.shape[-1]
    slots = positions.shape[2]
    tables = dft_blocks(width)
    probe_scale = 1.0 / math.sqrt(slots * lax.axis_size("row") * lax.axis_size("col"))
    near, apart = device_groups(4)

    right = passed_along(object_field, "col", -1)
    below = passed_along(object_field, "row", -1)
    diag = passed_along(below, "col", -1)
    prev = held(object_dir_prev, below)
    prev_below = passed_along(prev, "row", -1)
    prev_right = passed_along(prev, "col", -1)

    own_grad, below_grad, right_grad, diag_grad, probe_part, *kept = gradient_call(
        positions,
        counts,
        (object_field, below, right, diag),
        probe_field,
        intensities,
        tables,
    )
    probe_part, prev_below, prev_right = lax.optimization_barrier(
        (probe_part, prev_below, prev_right)
    )
    from_left_corner = passed_along(diag_grad, "col", 1)
    pieces = exchanged(probe_part.reshape((len(near[0]), -1, width // 2)), near)
    from_above = passed_along(joined_call((below_grad, from_left_corner), 10**10), "row", 1)
    from_left = passed_along(right_grad, "col", 1)
    prev_diag = passed_along(held(prev_below, diag_grad), "col", -1)
    from_above = held(from_above, prev_diag)
    object_grad = own_grad + from_left + from_above
    sums = [
        jnp.sum(jnp.sum(object_grad * other, axis=(0, 1)).reshape(2, -1), axis=0, keepdims=True)
        for other in (object_grad, object_dir_prev)
    ]
    payload = copies(jnp.concatenate([jnp.sum(pieces, axis=0), *sums], axis=0), apart)
    grad_below = passed_along(object_grad, "row", -1)
    grad_right = passed_along(object_grad, "col", -1)
    payload, grad_below, grad_right = lax.optimization_barrier(
        (exchanged(payload, apart), grad_below, grad_right)
    )
    grad_diag = passed_along(grad_below, "col", -1)
    grad_diag = joined_call((grad_diag,), 2 * 10**10)
    payload = jnp.sum(payload, axis=0)[:, None, :]
    total = exchanged(copies(payload, near), near)
    object_direction, probe_direction, sums = curvature_call(
        positions,
        counts,
        prev_norm.reshape(1),
        (object_grad, grad_below, grad_right, grad_diag)
        + (object_dir_prev, prev_below, prev_right, prev_diag),
        total.reshape(-1, width // 2),
        len(near[0]),
        kept,
        tables,
        probe_dir_prev,
        probe_scale,
    )
    near, apart = device_groups(2)
    across = jnp.sum(exchanged(copies(sums, near), near), axis=0)
    across = exchanged(copies(across, apart), apart)
    object_new, probe_new, norm, frame_curvature = update_call(
        across, sums, (object_field, object_direction, probe_field, probe_direction), slots
    )
    return (
        object_new,
        probe_new,
        object_direction,
        probe_direction,
        norm.reshape(()),
        frame_curvature,
    )


def solution(mesh):
    return jax.shard_map(
        per_device,
        mesh=mesh,
        in_specs=(
            P(None, "row", "col"),
            P(),
            P(None, "row", "col"),
            P(),
            P(),
            P("row", "col", None, None, None),
            P("row", "col", None, None),
            P("row", None),
        ),
        out_specs=(
            P(None, "row", "col"),
            P(),
            P(None, "row", "col"),
            P(),
            P(),
            P("row", "col", None),
        ),
        check_vma=False,
    )
```

```python
import functools
import math

import jax
import jax.numpy as jnp
import numpy as np
from jax import lax
from jax.experimental import pallas as pl
from jax.experimental.pallas import tpu as pltpu
from jax.sharding import PartitionSpec as P


def dft_blocks(width):
    at = np.arange(width)
    angle = (np.outer(at, at) % width) * (2.0 * math.pi / width)
    cosine = (np.cos(angle) / math.sqrt(width)).astype(np.float32)
    sine = (np.sin(angle) / math.sqrt(width)).astype(np.float32)

    def thrice(table):
        high = table.astype(jnp.bfloat16)
        low = (table - high.astype(np.float32)).astype(jnp.bfloat16)
        return np.concatenate([high, low, high], axis=1)

    left = np.stack([thrice(cosine), thrice(cosine - sine), thrice(cosine + sine)])
    return left, np.ascontiguousarray(left.transpose(0, 2, 1))


def split_halves(value):
    high = value.astype(jnp.bfloat16)
    low = (value - high.astype(jnp.float32)).astype(jnp.bfloat16)
    return high, low


def three_of(pair):
    return (pair[0] + pair[1], pair[1], pair[0])


def product(left, right):
    return jnp.dot(left, right, preferred_element_type=jnp.float32)


def dft_pairs(pairs, tables, scratch):
    left_ref, right_ref = tables
    tall_ref, wide_ref = scratch
    width = pairs[0][0].shape[0]
    for which, pair in enumerate(pairs):
        for at, part in enumerate(three_of(pair)):
            high, low = split_halves(part)
            tall_ref[which, at, :width] = high
            tall_ref[which, at, width : 2 * width] = high
            tall_ref[which, at, 2 * width :] = low
    results = []
    left_ref = left_ref()
    for which in range(len(pairs)):
        both, second, first = [product(left_ref[at], tall_ref[which, at]) for at in range(3)]
        for at, part in enumerate(three_of((both - second, both - first))):
            high, low = split_halves(part)
            wide_ref[which, at, :, :width] = high
            wide_ref[which, at, :, width : 2 * width] = high
            wide_ref[which, at, :, 2 * width :] = low
    right_ref = right_ref()
    for which in range(len(pairs)):
        both, second, first = [product(wide_ref[which, at], right_ref[at]) for at in range(3)]
        results.append((both - second, both - first))
    return results


def rolled(value, row, col):
    return pltpu.roll(pltpu.roll(value, row, 0), col, 1)


def wrapped(own, below, right, diag, upper, nearer):
    return jnp.where(nearer, jnp.where(upper, own, below), jnp.where(upper, right, diag))


def masks(row, col, width):
    upper = lax.broadcasted_iota(jnp.int32, (width, width), 0) >= row
    nearer = lax.broadcasted_iota(jnp.int32, (width, width), 1) >= col
    return upper, nearer


def corner(positions_ref, slot, width):
    row = lax.rem(positions_ref[0, 0, slot, 0], width)
    col = lax.rem(positions_ref[0, 0, slot, 1], width)
    return row, col


def live_count(counts_ref):
    return counts_ref[0, lax.axis_index("col")]


class Incoming:
    def __init__(self, source, target, semaphore):
        self.target = target
        self.copy = pltpu.make_async_copy(source, target, semaphore)
        self.copy.start()
        self.waiting = True

    def __call__(self):
        if self.waiting:
            self.copy.wait()
            self.waiting = False
        return self.target


def incoming(sources, targets, semaphores):
    return [
        Incoming(source, target, semaphores.at[at])
        for at, (source, target) in enumerate(zip(sources, targets))
    ]


def outgoing(sources, targets, semaphores, first=0):
    sent = [
        pltpu.make_async_copy(source, target, semaphores.at[first + at])
        for at, (source, target) in enumerate(zip(sources, targets))
    ]
    for copy in sent:
        copy.start()
    return sent


def gradient_kernel(
    positions_ref,
    counts_ref,
    own_any,
    below_any,
    right_any,
    diag_any,
    probe_any,
    measured_any,
    left_any,
    right_table_any,
    own_grad_any,
    below_grad_any,
    right_grad_any,
    diag_grad_any,
    probe_grad_any,
    patch_any,
    moved_any,
    far_any,
    tiles_ref,
    probe_ref,
    measured_ref,
    left_ref,
    right_ref,
    grads_ref,
    probe_sum_ref,
    patch_ref,
    moved_ref,
    far_ref,
    tall_ref,
    wide_ref,
    in_sems,
    out_sems,
):
    width = probe_ref.shape[-1]
    live = live_count(counts_ref)
    *ready, left, measured, right = incoming(
        [own_any, below_any, right_any, diag_any, probe_any]
        + [left_any, measured_any.at[0, 0], right_table_any],
        [tiles_ref.at[at] for at in range(4)] + [probe_ref, left_ref, measured_ref, right_ref],
        in_sems,
    )
    for arrival in ready:
        arrival()

    def both(first):
        slots = (first, first + 1)
        spots = [corner(positions_ref, slot, width) for slot in slots]
        waves = []
        for slot, (row, col) in zip(slots, spots):
            upper, nearer = masks(row, col, width)
            for part in range(2):
                patch_ref[slot, part] = wrapped(
                    *[tiles_ref[at, part] for at in range(4)], upper, nearer
                )
                moved_ref[slot, part] = rolled(probe_ref[part], row, col)
            patch_r, patch_i = patch_ref[slot, 0], patch_ref[slot, 1]
            probe_r, probe_i = moved_ref[slot, 0], moved_ref[slot, 1]
            kept = slot < live
            waves.append(
                (
                    jnp.where(kept, probe_r * patch_r - probe_i * patch_i, 0.0),
                    jnp.where(kept, probe_r * patch_i + probe_i * patch_r, 0.0),
                )
            )
        span = pl.ds(first, 2)
        sent = outgoing(
            [patch_ref.at[span], moved_ref.at[span]],
            [patch_any.at[span], moved_any.at[span]],
            out_sems,
            5 + 3 * (first // 2),
        )
        fars = dft_pairs(waves, (left, right), (tall_ref, wide_ref))
        turned = []
        measured()
        for slot, (far_r, far_i) in zip(slots, fars):
            far_ref[slot, 0] = far_r
            far_ref[slot, 1] = far_i
            residue = far_r * far_r + far_i * far_i - measured_ref[slot].astype(jnp.float32)
            turned.append((residue * far_i, residue * far_r))
        sent += outgoing(
            [far_ref.at[span]], [far_any.at[span]], out_sems, 7 + 3 * (first // 2)
        )
        backs = dft_pairs(turned, (left, right), (tall_ref, wide_ref))
        pieces = []
        for slot, (row, col), (back_i, back_r) in zip(slots, spots, backs):
            patch_r, patch_i = patch_ref[slot, 0], patch_ref[slot, 1]
            back_row = lax.rem(width - row, width)
            back_col = lax.rem(width - col, width)
            pieces.append(
                (
                    rolled(patch_r * back_r + patch_i * back_i, back_row, back_col),
                    rolled(patch_r * back_i - patch_i * back_r, back_row, back_col),
                )
            )
        for part in range(2):
            total = pieces[0][part] + pieces[1][part]
            for half in range(2):
                rows = pl.ds((2 * part + half) * width, width)
                side = total[:, half * (width // 2) : (half + 1) * (width // 2)]
                probe_sum_ref[rows, :] = side if first == 0 else probe_sum_ref[rows, :] + side
        for part in range(2):
            sums = [0.0, 0.0, 0.0, 0.0]
            for slot, (row, col), (back_i, back_r) in zip(slots, spots, backs):
                upper, nearer = masks(row, col, width)
                probe_r, probe_i = moved_ref[slot, 0], moved_ref[slot, 1]
                if part == 0:
                    term = probe_r * back_r + probe_i * back_i
                else:
                    term = probe_r * back_i - probe_i * back_r
                close = jnp.where(nearer, term, 0.0)
                beyond = term - close
                for at, side in enumerate((close, beyond)):
                    top = jnp.where(upper, side, 0.0)
                    sums[2 * at] = sums[2 * at] + top
                    sums[2 * at + 1] = sums[2 * at + 1] + (side - top)
            for at, total in enumerate(sums):
                grads_ref[at, part] = total if first == 0 else grads_ref[at, part] + total
        for copy in sent:
            copy.wait()

    both(0)
    pl.when(live > 2)(lambda: both(2))
    outs = [own_grad_any, below_grad_any, right_grad_any, diag_grad_any, probe_grad_any]
    made = [grads_ref.at[at] for at in range(4)] + [probe_sum_ref]
    for copy in outgoing(made, outs, out_sems):
        copy.wait()


def linear_frames(positions_ref, live, tiles, change, kept, tables, scratch, finish):
    own_ref, below_ref, right_ref, diag_ref = [tile() for tile in tiles]
    change_ref = change()
    width = own_ref.shape[-1]

    def both(first, patches, moves, fars):
        slots = (first, first + 1)
        patch_ref, moved_ref = patches(), moves()
        waves = []
        for at, slot in enumerate(slots):
            row, col = corner(positions_ref, slot, width)
            upper, nearer = masks(row, col, width)
            step_r, step_i = [
                wrapped(own_ref[part], below_ref[part], right_ref[part], diag_ref[part], upper, nearer)
                for part in range(2)
            ]
            patch_r, patch_i = patch_ref[at, 0], patch_ref[at, 1]
            probe_r, probe_i = moved_ref[at, 0], moved_ref[at, 1]
            change_r = rolled(change_ref[0], row, col)
            change_i = rolled(change_ref[1], row, col)
            waves.append(
                (
                    probe_r * step_r - probe_i * step_i + change_r * patch_r - change_i * patch_i,
                    probe_r * step_i + probe_i * step_r + change_r * patch_i + change_i * patch_r,
                )
            )
        steps = dft_pairs(waves, tables, scratch)
        far_ref = fars()
        quads = [
            2.0 * (far_ref[at, 0] * step_r + far_ref[at, 1] * step_i)
            for at, (step_r, step_i) in enumerate(steps)
        ]
        finish(slots, quads)

    both(0, *kept[0])
    for arrival in kept[1]:
        arrival()
    pl.when(live > 2)(lambda: both(2, *kept[1]))


def halves(array, ref):
    return [(array.at[pl.ds(first, 2)], ref.at[pl.ds(first, 2)]) for first in (0, 2)]


def joined_kernel(*refs):
    *sources, out_any, held_ref, in_sems, out_sem = refs
    count = len(sources)
    arrivals = incoming(sources, [held_ref.at[at] for at in range(count)], in_sems)
    for arrival in arrivals:
        arrival()
    if count > 1:
        held_ref[0] = sum((held_ref[at] for at in range(1, count)), held_ref[0])
    copy = pltpu.make_async_copy(held_ref.at[0], out_any, out_sem)
    copy.start()
    copy.wait()


def curvature_kernel(
    positions_ref,
    counts_ref,
    prev_norm_ref,
    own_any,
    below_any,
    right_any,
    diag_any,
    prev_own_any,
    prev_below_any,
    prev_right_any,
    prev_diag_any,
    total_any,
    patch_any,
    moved_any,
    far_any,
    left_any,
    right_table_any,
    prev_probe_any,
    direction_any,
    probe_direction_any,
    sums_ref,
    tiles_ref,
    prev_tiles_ref,
    total_ref,
    change_ref,
    patch_ref,
    moved_ref,
    far_ref,
    left_ref,
    right_ref,
    prev_probe_ref,
    tall_ref,
    wide_ref,
    in_sems,
    out_sems,
    *,
    probe_scale,
    pieces,
):
    live = live_count(counts_ref)
    width = change_ref.shape[-1]
    kept = [
        halves(patch_any, patch_ref),
        halves(moved_any, moved_ref),
        halves(far_any, far_ref),
    ]
    moves = [(total_any, total_ref), (prev_probe_any, prev_probe_ref)]
    for group, target in (
        ((own_any, below_any, right_any, diag_any), tiles_ref),
        ((prev_own_any, prev_below_any, prev_right_any, prev_diag_any), prev_tiles_ref),
    ):
        moves += [(tile, target.at[at]) for at, tile in enumerate(group)]
    moves += [kept[0][0], kept[1][0], (left_any, left_ref), (right_table_any, right_ref), kept[2][0]]
    moves += [kept[0][1], kept[1][1], kept[2][1]]
    total, prev_probe, *arrivals = incoming(*zip(*moves), in_sems)
    tiles, prev_tiles = arrivals[:4], arrivals[4:8]
    (patch, moved, left, right, far), later = arrivals[8:13], arrivals[13:]

    total()
    depth = 4 * width // pieces
    products = jnp.zeros((2, total_ref.shape[-1]), jnp.float32)
    for piece in range(pieces):
        base = piece * (depth + 2)
        part, rest = divmod(piece * depth, 2 * width)
        half, first = divmod(rest, width)
        lanes = slice(half * (width // 2), (half + 1) * (width // 2))
        change_ref[part, first : first + depth, lanes] = (
            total_ref[base : base + depth, :] * probe_scale
        )
        products = products + total_ref[base + depth : base + depth + 2, :]
    lane = lax.broadcasted_iota(jnp.int32, (1, 128), 1)
    probe_grad = change_ref[...]
    prev_probe()
    grad_norm = whole_sum(products[:1]) + whole_sum(probe_grad * probe_grad)
    along_prev = whole_sum(products[1:]) + whole_sum(probe_grad * prev_probe_ref[...])
    ratio = grad_norm / prev_norm_ref[0]
    descent = grad_norm - ratio * along_prev
    change_ref[...] = ratio * prev_probe_ref[...] - change_ref[...]
    for at, (tile, prev) in enumerate(zip(tiles, prev_tiles)):
        tile()
        prev()
        tiles_ref[at] = ratio * prev_tiles_ref[at] - tiles_ref[at]
    sent = outgoing(
        [tiles_ref.at[0], change_ref], [direction_any, probe_direction_any], out_sems
    )
    row = jnp.where(lane == 5, grad_norm, jnp.where(lane == 6, descent, 0.0))
    sums_ref[...] = row

    def finish(slots, quads):
        row = sums_ref[...]
        for slot, quad in zip(slots, quads):
            square = whole_sum(quad * quad)
            row = row + jnp.where((lane == 0) | (lane == 1 + slot), square, 0.0)
        sums_ref[...] = row

    linear_frames(
        positions_ref,
        live,
        [(lambda at=at: tiles_ref.at[at]) for at in range(4)],
        lambda: change_ref,
        ((patch, moved, far), later),
        (left, right),
        (tall_ref, wide_ref),
        finish,
    )
    for copy in sent:
        copy.wait()


def update_kernel(
    gathered_any,
    sums_any,
    object_any,
    direction_any,
    probe_any,
    probe_direction_any,
    object_new_any,
    probe_new_any,
    norm_ref,
    frames_ref,
    gathered_ref,
    sums_ref,
    held_ref,
    in_sems,
    out_sems,
):
    sources = [gathered_any, sums_any, object_any, direction_any, probe_any, probe_direction_any]
    targets = [gathered_ref, sums_ref] + [held_ref.at[at] for at in range(4)]
    gathered, sums, *arrivals = incoming(sources, targets, in_sems)
    total = jnp.sum(gathered()[...], axis=0)
    local = sums()[...]
    lane = lax.broadcasted_iota(jnp.int32, (1, 128), 1)

    def pick(row, at):
        return jnp.sum(jnp.where(lane == at, row, 0.0), axis=1, keepdims=True)

    curvature = pick(total, 0)
    step_size = pick(local, 6) / (0.5 * curvature + 1e-06)
    outs = [object_new_any, probe_new_any]
    sent = []
    for which in range(2):
        field, direction = [arrival() for arrival in arrivals[2 * which : 2 * which + 2]]
        field[...] = field[...] + step_size * direction[...]
        sent += outgoing([field], [outs[which]], out_sems, which)
    norm_ref[...] = pick(local, 5)
    pixels = held_ref.shape[-1] * held_ref.shape[-2]
    frames_ref[0] = local[:, 1 : 1 + frames_ref.shape[-1]] / pixels
    for copy in sent:
        copy.wait()


def whole_sum(value):
    return jnp.sum(jnp.sum(value, axis=tuple(range(value.ndim - 1)))[None], axis=1, keepdims=True)


def shaped(*dims):
    return jax.ShapeDtypeStruct(dims, jnp.float32)


def buffer(*dims, dtype=jnp.float32):
    return pltpu.VMEM(dims, dtype)


def arrivals_of(count):
    return pltpu.SemaphoreType.DMA((count,))


def anywhere(count):
    return [pl.BlockSpec(memory_space=pl.ANY)] * count


def in_hbm(count):
    return [pl.BlockSpec(memory_space=pltpu.HBM)] * count


def in_vmem(count):
    return [pl.BlockSpec(memory_space=pltpu.VMEM)] * count


def in_smem(count):
    return [pl.BlockSpec(memory_space=pltpu.SMEM)] * count


def table_buffers(width):
    return [
        buffer(3, width, 3 * width, dtype=jnp.bfloat16),
        buffer(3, 3 * width, width, dtype=jnp.bfloat16),
    ]


def dft_scratch(width):
    return [
        buffer(2, 3, 3 * width, width, dtype=jnp.bfloat16),
        buffer(2, 3, width, 3 * width, dtype=jnp.bfloat16),
    ]


def costing(flops, mebibytes=60):
    return {
        "compiler_params": pltpu.CompilerParams(vmem_limit_bytes=mebibytes * 2**20),
        "cost_estimate": pl.CostEstimate(flops=flops, bytes_accessed=10**7, transcendentals=0),
    }


def gradient_call(positions, counts, tiles, probe, measured, tables):
    width = probe.shape[-1]
    slots = measured.shape[2]
    frames = buffer(slots, 2, width, width)
    return pl.pallas_call(
        gradient_kernel,
        out_shape=(shaped(2, width, width),) * 4
        + (shaped(4 * width, width // 2),)
        + (shaped(slots, 2, width, width),) * 3,
        in_specs=in_smem(2) + anywhere(4) + in_hbm(4),
        out_specs=(*anywhere(5), *in_hbm(3)),
        scratch_shapes=[
            buffer(4, 2, width, width),
            buffer(2, width, width),
            buffer(slots, width, width, dtype=measured.dtype),
            *table_buffers(width),
            buffer(4, 2, width, width),
            buffer(4 * width, width // 2),
            frames,
            frames,
            frames,
            *dft_scratch(width),
            arrivals_of(8),
            arrivals_of(11),
        ],
        name="gradient_frames",
        **costing(10**10, 60),
    )(positions, counts, *tiles, probe, measured, *tables)


def joined_call(arrays, flops):
    shape = arrays[0].shape
    return pl.pallas_call(
        joined_kernel,
        out_shape=shaped(*shape),
        in_specs=anywhere(len(arrays)),
        out_specs=anywhere(1)[0],
        scratch_shapes=[
            buffer(len(arrays), *shape),
            arrivals_of(len(arrays)),
            pltpu.SemaphoreType.DMA,
        ],
        name="joined",
        **costing(flops, 4),
    )(*arrays)


def curvature_call(positions, counts, prev_norm, tiles, total, pieces, kept, tables, probe_prev, scale):
    width = tiles[0].shape[-1]
    slots = kept[0].shape[0]
    frames = buffer(slots, 2, width, width)
    return pl.pallas_call(
        functools.partial(curvature_kernel, probe_scale=scale, pieces=pieces),
        out_shape=(shaped(2, width, width), shaped(2, width, width), shaped(1, 128)),
        in_specs=in_smem(3) + anywhere(9) + in_hbm(6),
        out_specs=(*in_hbm(2), *in_vmem(1)),
        scratch_shapes=[
            buffer(4, 2, width, width),
            buffer(4, 2, width, width),
            buffer(*total.shape),
            buffer(2, width, width),
            frames,
            frames,
            frames,
            *table_buffers(width),
            buffer(2, width, width),
            *dft_scratch(width),
            arrivals_of(18),
            arrivals_of(2),
        ],
        name="curvature_frames",
        **costing(5 * 10**9),
    )(positions, counts, prev_norm, *tiles, total, *kept, *tables, probe_prev)


def update_call(gathered, sums, arrays, slots):
    shape = arrays[0].shape
    return pl.pallas_call(
        update_kernel,
        out_shape=(shaped(*shape),) * 2 + (shaped(1, 1), shaped(1, 1, slots)),
        in_specs=anywhere(2) + in_hbm(4),
        out_specs=(*in_hbm(2), *in_vmem(2)),
        scratch_shapes=[
            buffer(*gathered.shape),
            buffer(*sums.shape),
            buffer(4, *shape),
            arrivals_of(6),
            arrivals_of(2),
        ],
        name="update",
        **costing(10**6),
    )(gathered, sums, *arrays)


def passed_along(shard, axis, by):
    count = lax.axis_size(axis)
    pairs = [(i, i + by) for i in range(count) if 0 <= i + by < count]
    return lax.ppermute(shard, axis, pairs)


def device_groups(block):
    rows, cols = lax.axis_size("row"), lax.axis_size("col")
    near = [
        [row * cols + first + at for row in range(rows) for at in range(block)]
        for first in range(0, cols, block)
    ]
    return near, [list(members) for members in zip(*near)]


def exchanged(pieces, groups):
    return lax.all_to_all(pieces, ("row", "col"), 0, 0, axis_index_groups=groups)


def copies(piece, groups):
    return jnp.broadcast_to(piece[None], (len(groups[0]),) + piece.shape)


def held(value, *others):
    return lax.optimization_barrier((value,) + others)[0]


def per_device(
    object_field,
    probe_field,
    object_dir_prev,
    probe_dir_prev,
    prev_norm,
    intensities,
    positions,
    counts,
):
    width = probe_field.shape[-1]
    slots = positions.shape[2]
    tables = dft_blocks(width)
    probe_scale = 1.0 / math.sqrt(slots * lax.axis_size("row") * lax.axis_size("col"))
    near, apart = device_groups(4)

    right = passed_along(object_field, "col", -1)
    below = passed_along(object_field, "row", -1)
    diag = passed_along(below, "col", -1)
    prev = held(object_dir_prev, below)
    prev_below = passed_along(prev, "row", -1)
    prev_right = passed_along(prev, "col", -1)

    own_grad, below_grad, right_grad, diag_grad, probe_part, *kept = gradient_call(
        positions,
        counts,
        (object_field, below, right, diag),
        probe_field,
        intensities,
        tables,
    )
    probe_part, prev_below, prev_right = lax.optimization_barrier(
        (probe_part, prev_below, prev_right)
    )
    from_left_corner = passed_along(diag_grad, "col", 1)
    pieces = exchanged(probe_part.reshape((len(near[0]), -1, width // 2)), near)
    below_sum = joined_call((below_grad, from_left_corner), 10**10)
    from_above = passed_along(below_sum, "row", 1)
    from_left = passed_along(held(right_grad, below_sum), "col", 1)
    prev_diag = passed_along(held(prev_below, diag_grad), "col", -1)
    prev_diag = joined_call((prev_diag,), 10**9)
    object_grad = own_grad + from_left + from_above
    sums = [
        jnp.sum(jnp.sum(object_grad * other, axis=(0, 1)).reshape(2, -1), axis=0, keepdims=True)
        for other in (object_grad, object_dir_prev)
    ]
    payload = copies(jnp.concatenate([jnp.sum(pieces, axis=0), *sums], axis=0), apart)
    grad_below = passed_along(object_grad, "row", -1)
    grad_right = passed_along(object_grad, "col", -1)
    payload, grad_below, grad_right = lax.optimization_barrier(
        (exchanged(payload, apart), grad_below, grad_right)
    )
    grad_diag = passed_along(grad_below, "col", -1)
    grad_diag = joined_call((grad_diag,), 2 * 10**10)
    payload = jnp.sum(payload, axis=0)[:, None, :]
    total = exchanged(copies(payload, near), near)
    object_direction, probe_direction, sums = curvature_call(
        positions,
        counts,
        prev_norm.reshape(1),
        (object_grad, grad_below, grad_right, grad_diag)
        + (object_dir_prev, prev_below, prev_right, prev_diag),
        total.reshape(-1, width // 2),
        len(near[0]),
        kept,
        tables,
        probe_dir_prev,
        probe_scale,
    )
    near, apart = device_groups(2)
    across = jnp.sum(exchanged(copies(sums, near), near), axis=0)
    across = exchanged(copies(across, apart), apart)
    object_new, probe_new, norm, frame_curvature = update_call(
        across, sums, (object_field, object_direction, probe_field, probe_direction), slots
    )
    return (
        object_new,
        probe_new,
        object_direction,
        probe_direction,
        norm.reshape(()),
        frame_curvature,
    )


def solution(mesh):
    return jax.shard_map(
        per_device,
        mesh=mesh,
        in_specs=(
            P(None, "row", "col"),
            P(),
            P(None, "row", "col"),
            P(),
            P(),
            P("row", "col", None, None, None),
            P("row", "col", None, None),
            P("row", None),
        ),
        out_specs=(
            P(None, "row", "col"),
            P(),
            P(None, "row", "col"),
            P(),
            P(),
            P("row", "col", None),
        ),
        check_vma=False,
    )
```

```python
import functools
import math

import jax
import jax.numpy as jnp
import numpy as np
from jax import lax
from jax.experimental import pallas as pl
from jax.experimental.pallas import tpu as pltpu
from jax.sharding import PartitionSpec as P


def dft_blocks(width):
    at = np.arange(width)
    angle = (np.outer(at, at) % width) * (2.0 * math.pi / width)
    cosine = (np.cos(angle) / math.sqrt(width)).astype(np.float32)
    sine = (np.sin(angle) / math.sqrt(width)).astype(np.float32)

    def thrice(table):
        high = table.astype(jnp.bfloat16)
        low = (table - high.astype(np.float32)).astype(jnp.bfloat16)
        return np.concatenate([high, low, high], axis=1)

    left = np.stack([thrice(cosine), thrice(cosine - sine), thrice(cosine + sine)])
    return left, np.ascontiguousarray(left.transpose(0, 2, 1))


def split_halves(value):
    high = value.astype(jnp.bfloat16)
    low = (value - high.astype(jnp.float32)).astype(jnp.bfloat16)
    return high, low


def three_of(pair):
    return (pair[0] + pair[1], pair[1], pair[0])


def product(left, right):
    return jnp.dot(left, right, preferred_element_type=jnp.float32)


def dft_pairs(pairs, tables, scratch):
    left_ref, right_ref = tables
    tall_ref, wide_ref = scratch
    width = pairs[0][0].shape[0]
    for which, pair in enumerate(pairs):
        for at, part in enumerate(three_of(pair)):
            high, low = split_halves(part)
            tall_ref[which, at, :width] = high
            tall_ref[which, at, width : 2 * width] = high
            tall_ref[which, at, 2 * width :] = low
    results = []
    left_ref = left_ref()
    for which in range(len(pairs)):
        both, second, first = [product(left_ref[at], tall_ref[which, at]) for at in range(3)]
        for at, part in enumerate(three_of((both - second, both - first))):
            high, low = split_halves(part)
            wide_ref[which, at, :, :width] = high
            wide_ref[which, at, :, width : 2 * width] = high
            wide_ref[which, at, :, 2 * width :] = low
    right_ref = right_ref()
    for which in range(len(pairs)):
        both, second, first = [product(wide_ref[which, at], right_ref[at]) for at in range(3)]
        results.append((both - second, both - first))
    return results


def rolled(value, row, col):
    return pltpu.roll(pltpu.roll(value, row, 0), col, 1)


def wrapped(own, below, right, diag, upper, nearer):
    return jnp.where(nearer, jnp.where(upper, own, below), jnp.where(upper, right, diag))


def masks(row, col, width):
    upper = lax.broadcasted_iota(jnp.int32, (width, width), 0) >= row
    nearer = lax.broadcasted_iota(jnp.int32, (width, width), 1) >= col
    return upper, nearer


def corner(positions_ref, slot, width):
    row = lax.rem(positions_ref[0, 0, slot, 0], width)
    col = lax.rem(positions_ref[0, 0, slot, 1], width)
    return row, col


def live_count(counts_ref):
    return counts_ref[0, lax.axis_index("col")]


class Incoming:
    def __init__(self, source, target, semaphore):
        self.target = target
        self.copy = pltpu.make_async_copy(source, target, semaphore)
        self.copy.start()
        self.waiting = True

    def __call__(self):
        if self.waiting:
            self.copy.wait()
            self.waiting = False
        return self.target


def incoming(sources, targets, semaphores):
    return [
        Incoming(source, target, semaphores.at[at])
        for at, (source, target) in enumerate(zip(sources, targets))
    ]


def outgoing(sources, targets, semaphores, first=0):
    sent = [
        pltpu.make_async_copy(source, target, semaphores.at[first + at])
        for at, (source, target) in enumerate(zip(sources, targets))
    ]
    for copy in sent:
        copy.start()
    return sent


def gradient_kernel(
    positions_ref,
    counts_ref,
    own_any,
    below_any,
    right_any,
    diag_any,
    probe_any,
    measured_any,
    left_any,
    right_table_any,
    own_grad_any,
    below_grad_any,
    side_grad_any,
    probe_grad_any,
    patch_any,
    moved_any,
    far_any,
    tiles_ref,
    probe_ref,
    measured_ref,
    left_ref,
    right_ref,
    grads_ref,
    probe_sum_ref,
    patch_ref,
    moved_ref,
    far_ref,
    tall_ref,
    wide_ref,
    in_sems,
    out_sems,
):
    width = probe_ref.shape[-1]
    live = live_count(counts_ref)
    *ready, left, measured, right = incoming(
        [own_any, below_any, right_any, diag_any, probe_any]
        + [left_any, measured_any.at[0, 0], right_table_any],
        [tiles_ref.at[at] for at in range(4)] + [probe_ref, left_ref, measured_ref, right_ref],
        in_sems,
    )
    for arrival in ready:
        arrival()

    def both(first):
        slots = (first, first + 1)
        spots = [corner(positions_ref, slot, width) for slot in slots]
        waves = []
        for slot, (row, col) in zip(slots, spots):
            upper, nearer = masks(row, col, width)
            for part in range(2):
                patch_ref[slot, part] = wrapped(
                    *[tiles_ref[at, part] for at in range(4)], upper, nearer
                )
                moved_ref[slot, part] = rolled(probe_ref[part], row, col)
            patch_r, patch_i = patch_ref[slot, 0], patch_ref[slot, 1]
            probe_r, probe_i = moved_ref[slot, 0], moved_ref[slot, 1]
            kept = slot < live
            waves.append(
                (
                    jnp.where(kept, probe_r * patch_r - probe_i * patch_i, 0.0),
                    jnp.where(kept, probe_r * patch_i + probe_i * patch_r, 0.0),
                )
            )
        span = pl.ds(first, 2)
        sent = outgoing(
            [patch_ref.at[span], moved_ref.at[span]],
            [patch_any.at[span], moved_any.at[span]],
            out_sems,
            5 + 3 * (first // 2),
        )
        fars = dft_pairs(waves, (left, right), (tall_ref, wide_ref))
        turned = []
        measured()
        for slot, (far_r, far_i) in zip(slots, fars):
            far_ref[slot, 0] = far_r
            far_ref[slot, 1] = far_i
            residue = far_r * far_r + far_i * far_i - measured_ref[slot].astype(jnp.float32)
            turned.append((residue * far_i, residue * far_r))
        sent += outgoing(
            [far_ref.at[span]], [far_any.at[span]], out_sems, 7 + 3 * (first // 2)
        )
        backs = dft_pairs(turned, (left, right), (tall_ref, wide_ref))
        pieces = []
        for slot, (row, col), (back_i, back_r) in zip(slots, spots, backs):
            patch_r, patch_i = patch_ref[slot, 0], patch_ref[slot, 1]
            back_row = lax.rem(width - row, width)
            back_col = lax.rem(width - col, width)
            pieces.append(
                (
                    rolled(patch_r * back_r + patch_i * back_i, back_row, back_col),
                    rolled(patch_r * back_i - patch_i * back_r, back_row, back_col),
                )
            )
        for part in range(2):
            total = pieces[0][part] + pieces[1][part]
            for half in range(2):
                rows = pl.ds((2 * part + half) * width, width)
                side = total[:, half * (width // 2) : (half + 1) * (width // 2)]
                probe_sum_ref[rows, :] = side if first == 0 else probe_sum_ref[rows, :] + side
        for part in range(2):
            sums = [0.0, 0.0, 0.0, 0.0]
            for slot, (row, col), (back_i, back_r) in zip(slots, spots, backs):
                upper, nearer = masks(row, col, width)
                probe_r, probe_i = moved_ref[slot, 0], moved_ref[slot, 1]
                if part == 0:
                    term = probe_r * back_r + probe_i * back_i
                else:
                    term = probe_r * back_i - probe_i * back_r
                close = jnp.where(nearer, term, 0.0)
                beyond = term - close
                for at, side in enumerate((close, beyond)):
                    top = jnp.where(upper, side, 0.0)
                    sums[2 * at] = sums[2 * at] + top
                    sums[2 * at + 1] = sums[2 * at + 1] + (side - top)
            for at, total in enumerate(sums):
                grads_ref[at, part] = total if first == 0 else grads_ref[at, part] + total
        for copy in sent:
            copy.wait()

    both(0)
    pl.when(live > 2)(lambda: both(2))
    sides = [side_grad_any.at[:, pl.ds(first, width)] for first in (0, width)]
    outs = [own_grad_any, below_grad_any, *sides, probe_grad_any]
    made = [grads_ref.at[at] for at in range(4)] + [probe_sum_ref]
    for copy in outgoing(made, outs, out_sems):
        copy.wait()


def linear_frames(positions_ref, live, tiles, change, kept, tables, scratch, finish):
    own_ref, below_ref, right_ref, diag_ref = [tile() for tile in tiles]
    change_ref = change()
    width = own_ref.shape[-1]

    def both(first, patches, moves, fars):
        slots = (first, first + 1)
        patch_ref, moved_ref = patches(), moves()
        waves = []
        for at, slot in enumerate(slots):
            row, col = corner(positions_ref, slot, width)
            upper, nearer = masks(row, col, width)
            step_r, step_i = [
                wrapped(own_ref[part], below_ref[part], right_ref[part], diag_ref[part], upper, nearer)
                for part in range(2)
            ]
            patch_r, patch_i = patch_ref[at, 0], patch_ref[at, 1]
            probe_r, probe_i = moved_ref[at, 0], moved_ref[at, 1]
            change_r = rolled(change_ref[0], row, col)
            change_i = rolled(change_ref[1], row, col)
            waves.append(
                (
                    probe_r * step_r - probe_i * step_i + change_r * patch_r - change_i * patch_i,
                    probe_r * step_i + probe_i * step_r + change_r * patch_i + change_i * patch_r,
                )
            )
        steps = dft_pairs(waves, tables, scratch)
        far_ref = fars()
        quads = [
            2.0 * (far_ref[at, 0] * step_r + far_ref[at, 1] * step_i)
            for at, (step_r, step_i) in enumerate(steps)
        ]
        finish(slots, quads)

    both(0, *kept[0])
    for arrival in kept[1]:
        arrival()
    pl.when(live > 2)(lambda: both(2, *kept[1]))


def halves(array, ref):
    return [(array.at[pl.ds(first, 2)], ref.at[pl.ds(first, 2)]) for first in (0, 2)]


def joined_kernel(*refs):
    *sources, out_any, held_ref, in_sems, out_sem = refs
    count = len(sources)
    width = held_ref.shape[-1]
    sources = [
        source if source.shape[1] == width else source.at[:, pl.ds(width, width)]
        for source in sources
    ]
    arrivals = incoming(sources, [held_ref.at[at] for at in range(count)], in_sems)
    for arrival in arrivals:
        arrival()
    if count > 1:
        held_ref[0] = sum((held_ref[at] for at in range(1, count)), held_ref[0])
    copy = pltpu.make_async_copy(held_ref.at[0], out_any, out_sem)
    copy.start()
    copy.wait()


def curvature_kernel(
    positions_ref,
    counts_ref,
    prev_norm_ref,
    own_any,
    below_any,
    right_any,
    diag_any,
    prev_own_any,
    prev_below_any,
    prev_right_any,
    prev_diag_any,
    total_any,
    patch_any,
    moved_any,
    far_any,
    left_any,
    right_table_any,
    prev_probe_any,
    direction_any,
    probe_direction_any,
    sums_ref,
    tiles_ref,
    prev_tiles_ref,
    total_ref,
    change_ref,
    patch_ref,
    moved_ref,
    far_ref,
    left_ref,
    right_ref,
    prev_probe_ref,
    tall_ref,
    wide_ref,
    in_sems,
    out_sems,
    *,
    probe_scale,
    pieces,
):
    live = live_count(counts_ref)
    width = change_ref.shape[-1]
    kept = [
        halves(patch_any, patch_ref),
        halves(moved_any, moved_ref),
        halves(far_any, far_ref),
    ]
    moves = [(total_any, total_ref), (prev_probe_any, prev_probe_ref)]
    for group, target in (
        ((own_any, below_any, right_any, diag_any), tiles_ref),
        ((prev_own_any, prev_below_any, prev_right_any, prev_diag_any), prev_tiles_ref),
    ):
        moves += [(tile, target.at[at]) for at, tile in enumerate(group)]
    moves += [kept[0][0], kept[1][0], (left_any, left_ref), (right_table_any, right_ref), kept[2][0]]
    moves += [kept[0][1], kept[1][1], kept[2][1]]
    total, prev_probe, *arrivals = incoming(*zip(*moves), in_sems)
    tiles, prev_tiles = arrivals[:4], arrivals[4:8]
    (patch, moved, left, right, far), later = arrivals[8:13], arrivals[13:]

    total()
    depth = 4 * width // pieces
    products = jnp.zeros((2, total_ref.shape[-1]), jnp.float32)
    for piece in range(pieces):
        base = piece * (depth + 2)
        part, rest = divmod(piece * depth, 2 * width)
        half, first = divmod(rest, width)
        lanes = slice(half * (width // 2), (half + 1) * (width // 2))
        change_ref[part, first : first + depth, lanes] = (
            total_ref[base : base + depth, :] * probe_scale
        )
        products = products + total_ref[base + depth : base + depth + 2, :]
    lane = lax.broadcasted_iota(jnp.int32, (1, 128), 1)
    probe_grad = change_ref[...]
    prev_probe()
    grad_norm = whole_sum(products[:1]) + whole_sum(probe_grad * probe_grad)
    along_prev = whole_sum(products[1:]) + whole_sum(probe_grad * prev_probe_ref[...])
    ratio = grad_norm / prev_norm_ref[0]
    descent = grad_norm - ratio * along_prev
    change_ref[...] = ratio * prev_probe_ref[...] - change_ref[...]
    for at, (tile, prev) in enumerate(zip(tiles, prev_tiles)):
        tile()
        prev()
        tiles_ref[at] = ratio * prev_tiles_ref[at] - tiles_ref[at]
    sent = outgoing(
        [tiles_ref.at[0], change_ref], [direction_any, probe_direction_any], out_sems
    )
    row = jnp.where(lane == 5, grad_norm, jnp.where(lane == 6, descent, 0.0))
    sums_ref[...] = row

    def finish(slots, quads):
        row = sums_ref[...]
        for slot, quad in zip(slots, quads):
            square = whole_sum(quad * quad)
            row = row + jnp.where((lane == 0) | (lane == 1 + slot), square, 0.0)
        sums_ref[...] = row

    linear_frames(
        positions_ref,
        live,
        [(lambda at=at: tiles_ref.at[at]) for at in range(4)],
        lambda: change_ref,
        ((patch, moved, far), later),
        (left, right),
        (tall_ref, wide_ref),
        finish,
    )
    for copy in sent:
        copy.wait()


def update_kernel(
    gathered_any,
    sums_any,
    object_any,
    direction_any,
    probe_any,
    probe_direction_any,
    object_new_any,
    probe_new_any,
    norm_ref,
    frames_ref,
    gathered_ref,
    sums_ref,
    held_ref,
    in_sems,
    out_sems,
):
    sources = [gathered_any, sums_any, object_any, direction_any, probe_any, probe_direction_any]
    targets = [gathered_ref, sums_ref] + [held_ref.at[at] for at in range(4)]
    gathered, sums, *arrivals = incoming(sources, targets, in_sems)
    total = jnp.sum(gathered()[...], axis=0)
    local = sums()[...]
    lane = lax.broadcasted_iota(jnp.int32, (1, 128), 1)

    def pick(row, at):
        return jnp.sum(jnp.where(lane == at, row, 0.0), axis=1, keepdims=True)

    curvature = pick(total, 0)
    step_size = pick(local, 6) / (0.5 * curvature + 1e-06)
    outs = [object_new_any, probe_new_any]
    sent = []
    for which in range(2):
        field, direction = [arrival() for arrival in arrivals[2 * which : 2 * which + 2]]
        field[...] = field[...] + step_size * direction[...]
        sent += outgoing([field], [outs[which]], out_sems, which)
    norm_ref[...] = pick(local, 5)
    pixels = held_ref.shape[-1] * held_ref.shape[-2]
    frames_ref[0] = local[:, 1 : 1 + frames_ref.shape[-1]] / pixels
    for copy in sent:
        copy.wait()


def whole_sum(value):
    return jnp.sum(jnp.sum(value, axis=tuple(range(value.ndim - 1)))[None], axis=1, keepdims=True)


def shaped(*dims):
    return jax.ShapeDtypeStruct(dims, jnp.float32)


def buffer(*dims, dtype=jnp.float32):
    return pltpu.VMEM(dims, dtype)


def arrivals_of(count):
    return pltpu.SemaphoreType.DMA((count,))


def anywhere(count):
    return [pl.BlockSpec(memory_space=pl.ANY)] * count


def in_hbm(count):
    return [pl.BlockSpec(memory_space=pltpu.HBM)] * count


def in_vmem(count):
    return [pl.BlockSpec(memory_space=pltpu.VMEM)] * count


def in_smem(count):
    return [pl.BlockSpec(memory_space=pltpu.SMEM)] * count


def table_buffers(width):
    return [
        buffer(3, width, 3 * width, dtype=jnp.bfloat16),
        buffer(3, 3 * width, width, dtype=jnp.bfloat16),
    ]


def dft_scratch(width):
    return [
        buffer(2, 3, 3 * width, width, dtype=jnp.bfloat16),
        buffer(2, 3, width, 3 * width, dtype=jnp.bfloat16),
    ]


def costing(flops, mebibytes=60):
    return {
        "compiler_params": pltpu.CompilerParams(vmem_limit_bytes=mebibytes * 2**20),
        "cost_estimate": pl.CostEstimate(flops=flops, bytes_accessed=10**7, transcendentals=0),
    }


def gradient_call(positions, counts, tiles, probe, measured, tables):
    width = probe.shape[-1]
    slots = measured.shape[2]
    frames = buffer(slots, 2, width, width)
    return pl.pallas_call(
        gradient_kernel,
        out_shape=(shaped(2, width, width),) * 2
        + (shaped(2, 2 * width, width), shaped(4 * width, width // 2))
        + (shaped(slots, 2, width, width),) * 3,
        in_specs=in_smem(2) + anywhere(4) + in_hbm(4),
        out_specs=(*anywhere(4), *in_hbm(3)),
        scratch_shapes=[
            buffer(4, 2, width, width),
            buffer(2, width, width),
            buffer(slots, width, width, dtype=measured.dtype),
            *table_buffers(width),
            buffer(4, 2, width, width),
            buffer(4 * width, width // 2),
            frames,
            frames,
            frames,
            *dft_scratch(width),
            arrivals_of(8),
            arrivals_of(11),
        ],
        name="gradient_frames",
        **costing(10**10, 60),
    )(positions, counts, *tiles, probe, measured, *tables)


def joined_call(arrays, flops):
    shape = arrays[0].shape
    return pl.pallas_call(
        joined_kernel,
        out_shape=shaped(*shape),
        in_specs=anywhere(len(arrays)),
        out_specs=anywhere(1)[0],
        scratch_shapes=[
            buffer(len(arrays), *shape),
            arrivals_of(len(arrays)),
            pltpu.SemaphoreType.DMA,
        ],
        name="joined",
        **costing(flops, 4),
    )(*arrays)


def curvature_call(positions, counts, prev_norm, tiles, total, pieces, kept, tables, probe_prev, scale):
    width = tiles[0].shape[-1]
    slots = kept[0].shape[0]
    frames = buffer(slots, 2, width, width)
    return pl.pallas_call(
        functools.partial(curvature_kernel, probe_scale=scale, pieces=pieces),
        out_shape=(shaped(2, width, width), shaped(2, width, width), shaped(1, 128)),
        in_specs=in_smem(3) + anywhere(9) + in_hbm(6),
        out_specs=(*in_hbm(2), *in_vmem(1)),
        scratch_shapes=[
            buffer(4, 2, width, width),
            buffer(4, 2, width, width),
            buffer(*total.shape),
            buffer(2, width, width),
            frames,
            frames,
            frames,
            *table_buffers(width),
            buffer(2, width, width),
            *dft_scratch(width),
            arrivals_of(18),
            arrivals_of(2),
        ],
        name="curvature_frames",
        **costing(5 * 10**9),
    )(positions, counts, prev_norm, *tiles, total, *kept, *tables, probe_prev)


def update_call(gathered, sums, arrays, slots):
    shape = arrays[0].shape
    return pl.pallas_call(
        update_kernel,
        out_shape=(shaped(*shape),) * 2 + (shaped(1, 1), shaped(1, 1, slots)),
        in_specs=anywhere(2) + in_hbm(4),
        out_specs=(*in_hbm(2), *in_vmem(2)),
        scratch_shapes=[
            buffer(*gathered.shape),
            buffer(*sums.shape),
            buffer(4, *shape),
            arrivals_of(6),
            arrivals_of(2),
        ],
        name="update",
        **costing(10**6),
    )(gathered, sums, *arrays)


def passed_along(shard, axis, by):
    count = lax.axis_size(axis)
    pairs = [(i, i + by) for i in range(count) if 0 <= i + by < count]
    return lax.ppermute(shard, axis, pairs)


def device_groups(block):
    rows, cols = lax.axis_size("row"), lax.axis_size("col")
    near = [
        [row * cols + first + at for row in range(rows) for at in range(block)]
        for first in range(0, cols, block)
    ]
    return near, [list(members) for members in zip(*near)]


def exchanged(pieces, groups):
    return lax.all_to_all(pieces, ("row", "col"), 0, 0, axis_index_groups=groups)


def copies(piece, groups):
    return jnp.broadcast_to(piece[None], (len(groups[0]),) + piece.shape)


def held(value, *others):
    return lax.optimization_barrier((value,) + others)[0]


def per_device(
    object_field,
    probe_field,
    object_dir_prev,
    probe_dir_prev,
    prev_norm,
    intensities,
    positions,
    counts,
):
    width = probe_field.shape[-1]
    slots = positions.shape[2]
    tables = dft_blocks(width)
    probe_scale = 1.0 / math.sqrt(slots * lax.axis_size("row") * lax.axis_size("col"))
    near, apart = device_groups(4)

    right = passed_along(object_field, "col", -1)
    below = passed_along(object_field, "row", -1)
    diag = passed_along(below, "col", -1)
    prev = held(object_dir_prev, below)
    prev_below = passed_along(prev, "row", -1)
    prev_right = passed_along(prev, "col", -1)

    own_grad, below_grad, side_grad, probe_part, *kept = gradient_call(
        positions,
        counts,
        (object_field, below, right, diag),
        probe_field,
        intensities,
        tables,
    )
    side_grad, probe_part, prev_below, prev_right = lax.optimization_barrier(
        (side_grad, probe_part, prev_below, prev_right)
    )
    from_left = passed_along(side_grad, "col", 1)
    pieces = exchanged(probe_part.reshape((len(near[0]), -1, width // 2)), near)
    below_sum = joined_call((below_grad, from_left), 10**10)
    from_above = passed_along(below_sum, "row", 1)
    prev_diag = passed_along(held(prev_below, side_grad), "col", -1)
    prev_diag = joined_call((prev_diag,), 10**9)
    object_grad = own_grad + from_left[:, :width] + from_above
    sums = [
        jnp.sum(jnp.sum(object_grad * other, axis=(0, 1)).reshape(2, -1), axis=0, keepdims=True)
        for other in (object_grad, object_dir_prev)
    ]
    payload = copies(jnp.concatenate([jnp.sum(pieces, axis=0), *sums], axis=0), apart)
    grad_below = passed_along(object_grad, "row", -1)
    grad_right = passed_along(object_grad, "col", -1)
    payload, grad_below = lax.optimization_barrier((exchanged(payload, apart), grad_below))
    grad_right = joined_call((grad_right,), 10**9)
    grad_diag = passed_along(grad_below, "col", -1)
    grad_diag = joined_call((grad_diag,), 2 * 10**10)
    payload = jnp.sum(payload, axis=0)[:, None, :]
    total = exchanged(copies(payload, near), near)
    object_direction, probe_direction, sums = curvature_call(
        positions,
        counts,
        prev_norm.reshape(1),
        (object_grad, grad_below, grad_right, grad_diag)
        + (object_dir_prev, prev_below, prev_right, prev_diag),
        total.reshape(-1, width // 2),
        len(near[0]),
        kept,
        tables,
        probe_dir_prev,
        probe_scale,
    )
    near, apart = device_groups(2)
    across = jnp.sum(exchanged(copies(sums, near), near), axis=0)
    across = exchanged(copies(across, apart), apart)
    object_new, probe_new, norm, frame_curvature = update_call(
        across, sums, (object_field, object_direction, probe_field, probe_direction), slots
    )
    return (
        object_new,
        probe_new,
        object_direction,
        probe_direction,
        norm.reshape(()),
        frame_curvature,
    )


def solution(mesh):
    return jax.shard_map(
        per_device,
        mesh=mesh,
        in_specs=(
            P(None, "row", "col"),
            P(),
            P(None, "row", "col"),
            P(),
            P(),
            P("row", "col", None, None, None),
            P("row", "col", None, None),
            P("row", None),
        ),
        out_specs=(
            P(None, "row", "col"),
            P(),
            P(None, "row", "col"),
            P(),
            P(),
            P("row", "col", None),
        ),
        check_vma=False,
    )
```

```python
import functools
import math

import jax
import jax.numpy as jnp
import numpy as np
from jax import lax
from jax.experimental import pallas as pl
from jax.experimental.pallas import tpu as pltpu
from jax.sharding import PartitionSpec as P


def dft_blocks(width):
    at = np.arange(width)
    angle = (np.outer(at, at) % width) * (2.0 * math.pi / width)
    cosine = (np.cos(angle) / math.sqrt(width)).astype(np.float32)
    sine = (np.sin(angle) / math.sqrt(width)).astype(np.float32)

    def thrice(table):
        high = table.astype(jnp.bfloat16)
        low = (table - high.astype(np.float32)).astype(jnp.bfloat16)
        return np.concatenate([high, low, high], axis=1)

    left = np.stack([thrice(cosine), thrice(cosine - sine), thrice(cosine + sine)])
    return left, np.ascontiguousarray(left.transpose(0, 2, 1))


def split_halves(value):
    high = value.astype(jnp.bfloat16)
    low = (value - high.astype(jnp.float32)).astype(jnp.bfloat16)
    return high, low


def three_of(pair):
    return (pair[0] + pair[1], pair[1], pair[0])


def product(left, right):
    return jnp.dot(left, right, preferred_element_type=jnp.float32)


def dft_pairs(pairs, tables, scratch):
    left_ref, right_ref = tables
    tall_ref, wide_ref = scratch
    width = pairs[0][0].shape[0]
    for which, pair in enumerate(pairs):
        for at, part in enumerate(three_of(pair)):
            high, low = split_halves(part)
            tall_ref[which, at, :width] = high
            tall_ref[which, at, width : 2 * width] = high
            tall_ref[which, at, 2 * width :] = low
    results = []
    left_ref = left_ref()
    for which in range(len(pairs)):
        both, second, first = [product(left_ref[at], tall_ref[which, at]) for at in range(3)]
        for at, part in enumerate(three_of((both - second, both - first))):
            high, low = split_halves(part)
            wide_ref[which, at, :, :width] = high
            wide_ref[which, at, :, width : 2 * width] = high
            wide_ref[which, at, :, 2 * width :] = low
    right_ref = right_ref()
    for which in range(len(pairs)):
        both, second, first = [product(wide_ref[which, at], right_ref[at]) for at in range(3)]
        results.append((both - second, both - first))
    return results


def rolled(value, row, col):
    return pltpu.roll(pltpu.roll(value, row, 0), col, 1)


def wrapped(own, below, right, diag, upper, nearer):
    return jnp.where(nearer, jnp.where(upper, own, below), jnp.where(upper, right, diag))


def masks(row, col, width):
    upper = lax.broadcasted_iota(jnp.int32, (width, width), 0) >= row
    nearer = lax.broadcasted_iota(jnp.int32, (width, width), 1) >= col
    return upper, nearer


def corner(positions_ref, slot, width):
    row = lax.rem(positions_ref[0, 0, slot, 0], width)
    col = lax.rem(positions_ref[0, 0, slot, 1], width)
    return row, col


def live_count(counts_ref):
    return counts_ref[0, lax.axis_index("col")]


class Incoming:
    def __init__(self, source, target, semaphore):
        self.target = target
        self.copy = pltpu.make_async_copy(source, target, semaphore)
        self.copy.start()
        self.waiting = True

    def __call__(self):
        if self.waiting:
            self.copy.wait()
            self.waiting = False
        return self.target


def incoming(sources, targets, semaphores):
    return [
        Incoming(source, target, semaphores.at[at])
        for at, (source, target) in enumerate(zip(sources, targets))
    ]


def outgoing(sources, targets, semaphores, first=0):
    sent = [
        pltpu.make_async_copy(source, target, semaphores.at[first + at])
        for at, (source, target) in enumerate(zip(sources, targets))
    ]
    for copy in sent:
        copy.start()
    return sent


def gradient_kernel(
    positions_ref,
    counts_ref,
    own_any,
    below_any,
    right_any,
    diag_any,
    probe_any,
    measured_any,
    left_any,
    right_table_any,
    own_grad_any,
    below_grad_any,
    side_grad_any,
    probe_grad_any,
    patch_any,
    moved_any,
    far_any,
    tiles_ref,
    probe_ref,
    measured_ref,
    left_ref,
    right_ref,
    grads_ref,
    probe_sum_ref,
    patch_ref,
    moved_ref,
    far_ref,
    tall_ref,
    wide_ref,
    in_sems,
    out_sems,
):
    width = probe_ref.shape[-1]
    live = live_count(counts_ref)
    *ready, left, measured, right = incoming(
        [own_any, below_any, right_any, diag_any, probe_any]
        + [left_any, measured_any.at[0, 0], right_table_any],
        [tiles_ref.at[at] for at in range(4)] + [probe_ref, left_ref, measured_ref, right_ref],
        in_sems,
    )
    for arrival in ready:
        arrival()

    def both(first):
        slots = (first, first + 1)
        spots = [corner(positions_ref, slot, width) for slot in slots]
        waves = []
        for slot, (row, col) in zip(slots, spots):
            upper, nearer = masks(row, col, width)
            for part in range(2):
                patch_ref[slot, part] = wrapped(
                    *[tiles_ref[at, part] for at in range(4)], upper, nearer
                )
                moved_ref[slot, part] = rolled(probe_ref[part], row, col)
            patch_r, patch_i = patch_ref[slot, 0], patch_ref[slot, 1]
            probe_r, probe_i = moved_ref[slot, 0], moved_ref[slot, 1]
            kept = slot < live
            waves.append(
                (
                    jnp.where(kept, probe_r * patch_r - probe_i * patch_i, 0.0),
                    jnp.where(kept, probe_r * patch_i + probe_i * patch_r, 0.0),
                )
            )
        span = pl.ds(first, 2)
        sent = outgoing(
            [patch_ref.at[span], moved_ref.at[span]],
            [patch_any.at[span], moved_any.at[span]],
            out_sems,
            5 + 3 * (first // 2),
        )
        fars = dft_pairs(waves, (left, right), (tall_ref, wide_ref))
        turned = []
        measured()
        for slot, (far_r, far_i) in zip(slots, fars):
            far_ref[slot, 0] = far_r
            far_ref[slot, 1] = far_i
            residue = far_r * far_r + far_i * far_i - measured_ref[slot].astype(jnp.float32)
            turned.append((residue * far_i, residue * far_r))
        sent += outgoing(
            [far_ref.at[span]], [far_any.at[span]], out_sems, 7 + 3 * (first // 2)
        )
        backs = dft_pairs(turned, (left, right), (tall_ref, wide_ref))
        pieces = []
        for slot, (row, col), (back_i, back_r) in zip(slots, spots, backs):
            patch_r, patch_i = patch_ref[slot, 0], patch_ref[slot, 1]
            back_row = lax.rem(width - row, width)
            back_col = lax.rem(width - col, width)
            pieces.append(
                (
                    rolled(patch_r * back_r + patch_i * back_i, back_row, back_col),
                    rolled(patch_r * back_i - patch_i * back_r, back_row, back_col),
                )
            )
        for part in range(2):
            total = pieces[0][part] + pieces[1][part]
            for half in range(2):
                rows = pl.ds((2 * part + half) * width, width)
                side = total[:, half * (width // 2) : (half + 1) * (width // 2)]
                probe_sum_ref[rows, :] = side if first == 0 else probe_sum_ref[rows, :] + side
        for part in range(2):
            sums = [0.0, 0.0, 0.0, 0.0]
            for slot, (row, col), (back_i, back_r) in zip(slots, spots, backs):
                upper, nearer = masks(row, col, width)
                probe_r, probe_i = moved_ref[slot, 0], moved_ref[slot, 1]
                if part == 0:
                    term = probe_r * back_r + probe_i * back_i
                else:
                    term = probe_r * back_i - probe_i * back_r
                close = jnp.where(nearer, term, 0.0)
                beyond = term - close
                for at, side in enumerate((close, beyond)):
                    top = jnp.where(upper, side, 0.0)
                    sums[2 * at] = sums[2 * at] + top
                    sums[2 * at + 1] = sums[2 * at + 1] + (side - top)
            for at, total in enumerate(sums):
                grads_ref[at, part] = total if first == 0 else grads_ref[at, part] + total
        for copy in sent:
            copy.wait()

    both(0)
    pl.when(live > 2)(lambda: both(2))
    sides = [side_grad_any.at[:, pl.ds(first, width)] for first in (0, width)]
    outs = [own_grad_any, below_grad_any, *sides, probe_grad_any]
    made = [grads_ref.at[at] for at in range(4)] + [probe_sum_ref]
    for copy in outgoing(made, outs, out_sems):
        copy.wait()


def linear_frames(positions_ref, live, tiles, change, kept, tables, scratch, finish):
    own_ref, below_ref, right_ref, diag_ref = [tile() for tile in tiles]
    change_ref = change()
    width = own_ref.shape[-1]

    def both(first, patches, moves, fars):
        slots = (first, first + 1)
        patch_ref, moved_ref = patches(), moves()
        waves = []
        for at, slot in enumerate(slots):
            row, col = corner(positions_ref, slot, width)
            upper, nearer = masks(row, col, width)
            step_r, step_i = [
                wrapped(own_ref[part], below_ref[part], right_ref[part], diag_ref[part], upper, nearer)
                for part in range(2)
            ]
            patch_r, patch_i = patch_ref[at, 0], patch_ref[at, 1]
            probe_r, probe_i = moved_ref[at, 0], moved_ref[at, 1]
            change_r = rolled(change_ref[0], row, col)
            change_i = rolled(change_ref[1], row, col)
            waves.append(
                (
                    probe_r * step_r - probe_i * step_i + change_r * patch_r - change_i * patch_i,
                    probe_r * step_i + probe_i * step_r + change_r * patch_i + change_i * patch_r,
                )
            )
        steps = dft_pairs(waves, tables, scratch)
        far_ref = fars()
        quads = [
            2.0 * (far_ref[at, 0] * step_r + far_ref[at, 1] * step_i)
            for at, (step_r, step_i) in enumerate(steps)
        ]
        finish(slots, quads)

    both(0, *kept[0])
    for arrival in kept[1]:
        arrival()
    pl.when(live > 2)(lambda: both(2, *kept[1]))


def halves(array, ref):
    return [(array.at[pl.ds(first, 2)], ref.at[pl.ds(first, 2)]) for first in (0, 2)]


def joined_kernel(*refs):
    *sources, out_any, held_ref, in_sems, out_sem = refs
    count = len(sources)
    width = held_ref.shape[-1]
    sources = [
        source if source.shape[1] == width else source.at[:, pl.ds(width, width)]
        for source in sources
    ]
    arrivals = incoming(sources, [held_ref.at[at] for at in range(count)], in_sems)
    for arrival in arrivals:
        arrival()
    if count > 1:
        held_ref[0] = sum((held_ref[at] for at in range(1, count)), held_ref[0])
    copy = pltpu.make_async_copy(held_ref.at[0], out_any, out_sem)
    copy.start()
    copy.wait()


def curvature_kernel(
    positions_ref,
    counts_ref,
    prev_norm_ref,
    own_any,
    below_any,
    right_any,
    diag_any,
    prev_own_any,
    prev_below_any,
    prev_right_any,
    prev_diag_any,
    total_any,
    patch_any,
    moved_any,
    far_any,
    left_any,
    right_table_any,
    prev_probe_any,
    direction_any,
    probe_direction_any,
    sums_ref,
    tiles_ref,
    prev_tiles_ref,
    total_ref,
    change_ref,
    patch_ref,
    moved_ref,
    far_ref,
    left_ref,
    right_ref,
    prev_probe_ref,
    tall_ref,
    wide_ref,
    in_sems,
    out_sems,
    *,
    probe_scale,
    pieces,
):
    live = live_count(counts_ref)
    width = change_ref.shape[-1]
    kept = [
        halves(patch_any, patch_ref),
        halves(moved_any, moved_ref),
        halves(far_any, far_ref),
    ]
    moves = [(total_any, total_ref), (prev_probe_any, prev_probe_ref)]
    for group, target in (
        ((own_any, below_any, right_any, diag_any), tiles_ref),
        ((prev_own_any, prev_below_any, prev_right_any, prev_diag_any), prev_tiles_ref),
    ):
        moves += [(tile, target.at[at]) for at, tile in enumerate(group)]
    moves += [kept[0][0], kept[1][0], (left_any, left_ref), (right_table_any, right_ref), kept[2][0]]
    moves += [kept[0][1], kept[1][1], kept[2][1]]
    total, prev_probe, *arrivals = incoming(*zip(*moves), in_sems)
    tiles, prev_tiles = arrivals[:4], arrivals[4:8]
    (patch, moved, left, right, far), later = arrivals[8:13], arrivals[13:]

    total()
    depth = 4 * width // pieces
    products = jnp.zeros((2, total_ref.shape[-1]), jnp.float32)
    for piece in range(pieces):
        base = piece * (depth + 2)
        part, rest = divmod(piece * depth, 2 * width)
        half, first = divmod(rest, width)
        lanes = slice(half * (width // 2), (half + 1) * (width // 2))
        change_ref[part, first : first + depth, lanes] = (
            total_ref[base : base + depth, :] * probe_scale
        )
        products = products + total_ref[base + depth : base + depth + 2, :]
    lane = lax.broadcasted_iota(jnp.int32, (1, 128), 1)
    probe_grad = change_ref[...]
    prev_probe()
    grad_norm = whole_sum(products[:1]) + whole_sum(probe_grad * probe_grad)
    along_prev = whole_sum(products[1:]) + whole_sum(probe_grad * prev_probe_ref[...])
    ratio = grad_norm / prev_norm_ref[0]
    descent = grad_norm - ratio * along_prev
    change_ref[...] = ratio * prev_probe_ref[...] - change_ref[...]
    for at, (tile, prev) in enumerate(zip(tiles, prev_tiles)):
        tile()
        prev()
        tiles_ref[at] = ratio * prev_tiles_ref[at] - tiles_ref[at]
    sent = outgoing(
        [tiles_ref.at[0], change_ref], [direction_any, probe_direction_any], out_sems
    )
    row = jnp.where(lane == 5, grad_norm, jnp.where(lane == 6, descent, 0.0))
    sums_ref[...] = row

    def finish(slots, quads):
        row = sums_ref[...]
        for slot, quad in zip(slots, quads):
            square = whole_sum(quad * quad)
            row = row + jnp.where((lane == 0) | (lane == 1 + slot), square, 0.0)
        sums_ref[...] = row

    linear_frames(
        positions_ref,
        live,
        [(lambda at=at: tiles_ref.at[at]) for at in range(4)],
        lambda: change_ref,
        ((patch, moved, far), later),
        (left, right),
        (tall_ref, wide_ref),
        finish,
    )
    for copy in sent:
        copy.wait()


def update_kernel(
    gathered_any,
    sums_any,
    object_any,
    direction_any,
    probe_any,
    probe_direction_any,
    object_new_any,
    probe_new_any,
    norm_ref,
    frames_ref,
    gathered_ref,
    sums_ref,
    held_ref,
    in_sems,
    out_sems,
):
    sources = [gathered_any, sums_any, object_any, direction_any, probe_any, probe_direction_any]
    targets = [gathered_ref, sums_ref] + [held_ref.at[at] for at in range(4)]
    gathered, sums, *arrivals = incoming(sources, targets, in_sems)
    total = jnp.sum(gathered()[...], axis=0)
    local = sums()[...]
    lane = lax.broadcasted_iota(jnp.int32, (1, 128), 1)

    def pick(row, at):
        return jnp.sum(jnp.where(lane == at, row, 0.0), axis=1, keepdims=True)

    curvature = pick(total, 0)
    step_size = pick(local, 6) / (0.5 * curvature + 1e-06)
    outs = [object_new_any, probe_new_any]
    sent = []
    for which in range(2):
        field, direction = [arrival() for arrival in arrivals[2 * which : 2 * which + 2]]
        field[...] = field[...] + step_size * direction[...]
        sent += outgoing([field], [outs[which]], out_sems, which)
    norm_ref[...] = pick(local, 5)
    pixels = held_ref.shape[-1] * held_ref.shape[-2]
    frames_ref[0] = local[:, 1 : 1 + frames_ref.shape[-1]] / pixels
    for copy in sent:
        copy.wait()


def whole_sum(value):
    return jnp.sum(jnp.sum(value, axis=tuple(range(value.ndim - 1)))[None], axis=1, keepdims=True)


def shaped(*dims):
    return jax.ShapeDtypeStruct(dims, jnp.float32)


def buffer(*dims, dtype=jnp.float32):
    return pltpu.VMEM(dims, dtype)


def arrivals_of(count):
    return pltpu.SemaphoreType.DMA((count,))


def anywhere(count):
    return [pl.BlockSpec(memory_space=pl.ANY)] * count


def in_hbm(count):
    return [pl.BlockSpec(memory_space=pltpu.HBM)] * count


def in_vmem(count):
    return [pl.BlockSpec(memory_space=pltpu.VMEM)] * count


def in_smem(count):
    return [pl.BlockSpec(memory_space=pltpu.SMEM)] * count


def table_buffers(width):
    return [
        buffer(3, width, 3 * width, dtype=jnp.bfloat16),
        buffer(3, 3 * width, width, dtype=jnp.bfloat16),
    ]


def dft_scratch(width):
    return [
        buffer(2, 3, 3 * width, width, dtype=jnp.bfloat16),
        buffer(2, 3, width, 3 * width, dtype=jnp.bfloat16),
    ]


def costing(flops, mebibytes=60):
    return {
        "compiler_params": pltpu.CompilerParams(vmem_limit_bytes=mebibytes * 2**20),
        "cost_estimate": pl.CostEstimate(flops=flops, bytes_accessed=10**7, transcendentals=0),
    }


def gradient_call(positions, counts, tiles, probe, measured, tables):
    width = probe.shape[-1]
    slots = measured.shape[2]
    frames = buffer(slots, 2, width, width)
    return pl.pallas_call(
        gradient_kernel,
        out_shape=(shaped(2, width, width),) * 2
        + (shaped(2, 2 * width, width), shaped(4 * width, width // 2))
        + (shaped(slots, 2, width, width),) * 3,
        in_specs=in_smem(2) + anywhere(4) + in_hbm(4),
        out_specs=(*anywhere(4), *in_hbm(3)),
        scratch_shapes=[
            buffer(4, 2, width, width),
            buffer(2, width, width),
            buffer(slots, width, width, dtype=measured.dtype),
            *table_buffers(width),
            buffer(4, 2, width, width),
            buffer(4 * width, width // 2),
            frames,
            frames,
            frames,
            *dft_scratch(width),
            arrivals_of(8),
            arrivals_of(11),
        ],
        name="gradient_frames",
        **costing(10**10, 60),
    )(positions, counts, *tiles, probe, measured, *tables)


def joined_call(arrays, flops):
    shape = arrays[0].shape
    return pl.pallas_call(
        joined_kernel,
        out_shape=shaped(*shape),
        in_specs=anywhere(len(arrays)),
        out_specs=anywhere(1)[0],
        scratch_shapes=[
            buffer(len(arrays), *shape),
            arrivals_of(len(arrays)),
            pltpu.SemaphoreType.DMA,
        ],
        name="joined",
        **costing(flops, 4),
    )(*arrays)


def curvature_call(positions, counts, prev_norm, tiles, total, pieces, kept, tables, probe_prev, scale):
    width = tiles[0].shape[-1]
    slots = kept[0].shape[0]
    frames = buffer(slots, 2, width, width)
    return pl.pallas_call(
        functools.partial(curvature_kernel, probe_scale=scale, pieces=pieces),
        out_shape=(shaped(2, width, width), shaped(2, width, width), shaped(1, 128)),
        in_specs=in_smem(3) + anywhere(9) + in_hbm(6),
        out_specs=(*in_hbm(2), *in_vmem(1)),
        scratch_shapes=[
            buffer(4, 2, width, width),
            buffer(4, 2, width, width),
            buffer(*total.shape),
            buffer(2, width, width),
            frames,
            frames,
            frames,
            *table_buffers(width),
            buffer(2, width, width),
            *dft_scratch(width),
            arrivals_of(18),
            arrivals_of(2),
        ],
        name="curvature_frames",
        **costing(5 * 10**9),
    )(positions, counts, prev_norm, *tiles, total, *kept, *tables, probe_prev)


def update_call(gathered, sums, arrays, slots):
    shape = arrays[0].shape
    return pl.pallas_call(
        update_kernel,
        out_shape=(shaped(*shape),) * 2 + (shaped(1, 1), shaped(1, 1, slots)),
        in_specs=anywhere(2) + in_hbm(4),
        out_specs=(*in_hbm(2), *in_vmem(2)),
        scratch_shapes=[
            buffer(*gathered.shape),
            buffer(*sums.shape),
            buffer(4, *shape),
            arrivals_of(6),
            arrivals_of(2),
        ],
        name="update",
        **costing(10**6),
    )(gathered, sums, *arrays)


def passed_along(shard, axis, by):
    count = lax.axis_size(axis)
    pairs = [(i, i + by) for i in range(count) if 0 <= i + by < count]
    return lax.ppermute(shard, axis, pairs)


def device_groups(block):
    rows, cols = lax.axis_size("row"), lax.axis_size("col")
    near = [
        [row * cols + first + at for row in range(rows) for at in range(block)]
        for first in range(0, cols, block)
    ]
    return near, [list(members) for members in zip(*near)]


def exchanged(pieces, groups):
    return lax.all_to_all(pieces, ("row", "col"), 0, 0, axis_index_groups=groups)


def copies(piece, groups):
    return jnp.broadcast_to(piece[None], (len(groups[0]),) + piece.shape)


def held(value, *others):
    return lax.optimization_barrier((value,) + others)[0]


def per_device(
    object_field,
    probe_field,
    object_dir_prev,
    probe_dir_prev,
    prev_norm,
    intensities,
    positions,
    counts,
):
    width = probe_field.shape[-1]
    slots = positions.shape[2]
    tables = dft_blocks(width)
    probe_scale = 1.0 / math.sqrt(slots * lax.axis_size("row") * lax.axis_size("col"))
    near, apart = device_groups(4)

    right = passed_along(object_field, "col", -1)
    below = passed_along(object_field, "row", -1)
    diag = passed_along(below, "col", -1)
    prev = held(object_dir_prev, below)
    prev_below = passed_along(prev, "row", -1)
    prev_right = passed_along(prev, "col", -1)

    own_grad, below_grad, side_grad, probe_part, *kept = gradient_call(
        positions,
        counts,
        (object_field, below, right, diag),
        probe_field,
        intensities,
        tables,
    )
    side_grad, probe_part, prev_below, prev_right = lax.optimization_barrier(
        (side_grad, probe_part, prev_below, prev_right)
    )
    from_left = passed_along(side_grad, "col", 1)
    pieces = exchanged(probe_part.reshape((len(near[0]), -1, width // 2)), near)
    below_sum = joined_call((below_grad, from_left), 10**10)
    from_above = passed_along(below_sum, "row", 1)
    prev_diag = passed_along(held(prev_below, below_sum), "col", -1)
    object_grad = own_grad + from_left[:, :width] + from_above
    sums = [
        jnp.sum(jnp.sum(object_grad * other, axis=(0, 1)).reshape(2, -1), axis=0, keepdims=True)
        for other in (object_grad, object_dir_prev)
    ]
    payload = copies(jnp.concatenate([jnp.sum(pieces, axis=0), *sums], axis=0), apart)
    object_grad, prev_diag = lax.optimization_barrier((object_grad, prev_diag))
    grad_below = passed_along(object_grad, "row", -1)
    grad_right = passed_along(object_grad, "col", -1)
    payload, grad_below = lax.optimization_barrier((exchanged(payload, apart), grad_below))
    grad_right = joined_call((grad_right,), 10**9)
    grad_diag = passed_along(grad_below, "col", -1)
    grad_diag = joined_call((grad_diag,), 2 * 10**10)
    payload = jnp.sum(payload, axis=0)[:, None, :]
    total = exchanged(copies(payload, near), near)
    object_direction, probe_direction, sums = curvature_call(
        positions,
        counts,
        prev_norm.reshape(1),
        (object_grad, grad_below, grad_right, grad_diag)
        + (object_dir_prev, prev_below, prev_right, prev_diag),
        total.reshape(-1, width // 2),
        len(near[0]),
        kept,
        tables,
        probe_dir_prev,
        probe_scale,
    )
    near, apart = device_groups(2)
    across = jnp.sum(exchanged(copies(sums, near), near), axis=0)
    across = exchanged(copies(across, apart), apart)
    object_new, probe_new, norm, frame_curvature = update_call(
        across, sums, (object_field, object_direction, probe_field, probe_direction), slots
    )
    return (
        object_new,
        probe_new,
        object_direction,
        probe_direction,
        norm.reshape(()),
        frame_curvature,
    )


def solution(mesh):
    return jax.shard_map(
        per_device,
        mesh=mesh,
        in_specs=(
            P(None, "row", "col"),
            P(),
            P(None, "row", "col"),
            P(),
            P(),
            P("row", "col", None, None, None),
            P("row", "col", None, None),
            P("row", None),
        ),
        out_specs=(
            P(None, "row", "col"),
            P(),
            P(None, "row", "col"),
            P(),
            P(),
            P("row", "col", None),
        ),
        check_vma=False,
    )
```

```python
import functools
import math

import jax
import jax.numpy as jnp
import numpy as np
from jax import lax
from jax.experimental import pallas as pl
from jax.experimental.pallas import tpu as pltpu
from jax.sharding import PartitionSpec as P


def dft_blocks(width):
    at = np.arange(width)
    angle = (np.outer(at, at) % width) * (2.0 * math.pi / width)
    cosine = (np.cos(angle) / math.sqrt(width)).astype(np.float32)
    sine = (np.sin(angle) / math.sqrt(width)).astype(np.float32)

    def thrice(table):
        high = table.astype(jnp.bfloat16)
        low = (table - high.astype(np.float32)).astype(jnp.bfloat16)
        return np.concatenate([high, low, high], axis=1)

    left = np.stack([thrice(cosine), thrice(cosine - sine), thrice(cosine + sine)])
    return left, np.ascontiguousarray(left.transpose(0, 2, 1))


def split_halves(value):
    high = value.astype(jnp.bfloat16)
    low = (value - high.astype(jnp.float32)).astype(jnp.bfloat16)
    return high, low


def three_of(pair):
    return (pair[0] + pair[1], pair[1], pair[0])


def product(left, right):
    return jnp.dot(left, right, preferred_element_type=jnp.float32)


def dft_pairs(pairs, tables, scratch):
    left_ref, right_ref = tables
    tall_ref, wide_ref = scratch
    width = pairs[0][0].shape[0]
    for which, pair in enumerate(pairs):
        for at, part in enumerate(three_of(pair)):
            high, low = split_halves(part)
            tall_ref[which, at, :width] = high
            tall_ref[which, at, width : 2 * width] = high
            tall_ref[which, at, 2 * width :] = low
    results = []
    left_ref = left_ref()
    for which in range(len(pairs)):
        both, second, first = [product(left_ref[at], tall_ref[which, at]) for at in range(3)]
        for at, part in enumerate(three_of((both - second, both - first))):
            high, low = split_halves(part)
            wide_ref[which, at, :, :width] = high
            wide_ref[which, at, :, width : 2 * width] = high
            wide_ref[which, at, :, 2 * width :] = low
    right_ref = right_ref()
    for which in range(len(pairs)):
        both, second, first = [product(wide_ref[which, at], right_ref[at]) for at in range(3)]
        results.append((both - second, both - first))
    return results


def rolled(value, row, col):
    return pltpu.roll(pltpu.roll(value, row, 0), col, 1)


def wrapped(own, below, right, diag, upper, nearer):
    return jnp.where(nearer, jnp.where(upper, own, below), jnp.where(upper, right, diag))


def masks(row, col, width):
    upper = lax.broadcasted_iota(jnp.int32, (width, width), 0) >= row
    nearer = lax.broadcasted_iota(jnp.int32, (width, width), 1) >= col
    return upper, nearer


def corner(positions_ref, slot, width):
    row = lax.rem(positions_ref[0, 0, slot, 0], width)
    col = lax.rem(positions_ref[0, 0, slot, 1], width)
    return row, col


def live_count(counts_ref):
    return counts_ref[0, lax.axis_index("col")]


class Incoming:
    def __init__(self, source, target, semaphore):
        self.target = target
        self.copy = pltpu.make_async_copy(source, target, semaphore)
        self.copy.start()
        self.waiting = True

    def __call__(self):
        if self.waiting:
            self.copy.wait()
            self.waiting = False
        return self.target


def incoming(sources, targets, semaphores):
    return [
        Incoming(source, target, semaphores.at[at])
        for at, (source, target) in enumerate(zip(sources, targets))
    ]


def outgoing(sources, targets, semaphores, first=0):
    sent = [
        pltpu.make_async_copy(source, target, semaphores.at[first + at])
        for at, (source, target) in enumerate(zip(sources, targets))
    ]
    for copy in sent:
        copy.start()
    return sent


def gradient_kernel(
    positions_ref,
    counts_ref,
    own_any,
    below_any,
    right_any,
    diag_any,
    probe_any,
    measured_any,
    left_any,
    right_table_any,
    own_grad_any,
    below_grad_any,
    side_grad_any,
    probe_grad_any,
    patch_any,
    moved_any,
    far_any,
    tiles_ref,
    probe_ref,
    measured_ref,
    left_ref,
    right_ref,
    grads_ref,
    probe_sum_ref,
    patch_ref,
    moved_ref,
    far_ref,
    tall_ref,
    wide_ref,
    in_sems,
    out_sems,
):
    width = probe_ref.shape[-1]
    live = live_count(counts_ref)
    probe, *ready, left, measured, right = incoming(
        [probe_any, own_any, below_any, right_any, diag_any]
        + [left_any, measured_any.at[0, 0], right_table_any],
        [probe_ref] + [tiles_ref.at[at] for at in range(4)] + [left_ref, measured_ref, right_ref],
        in_sems,
    )
    probe()

    def both(first):
        slots = (first, first + 1)
        spots = [corner(positions_ref, slot, width) for slot in slots]
        for slot, (row, col) in zip(slots, spots):
            for part in range(2):
                moved_ref[slot, part] = rolled(probe_ref[part], row, col)
        for arrival in ready:
            arrival()
        waves = []
        for slot, (row, col) in zip(slots, spots):
            upper, nearer = masks(row, col, width)
            for part in range(2):
                patch_ref[slot, part] = wrapped(
                    *[tiles_ref[at, part] for at in range(4)], upper, nearer
                )
            patch_r, patch_i = patch_ref[slot, 0], patch_ref[slot, 1]
            probe_r, probe_i = moved_ref[slot, 0], moved_ref[slot, 1]
            kept = slot < live
            waves.append(
                (
                    jnp.where(kept, probe_r * patch_r - probe_i * patch_i, 0.0),
                    jnp.where(kept, probe_r * patch_i + probe_i * patch_r, 0.0),
                )
            )
        span = pl.ds(first, 2)
        sent = outgoing(
            [patch_ref.at[span], moved_ref.at[span]],
            [patch_any.at[span], moved_any.at[span]],
            out_sems,
            5 + 3 * (first // 2),
        )
        fars = dft_pairs(waves, (left, right), (tall_ref, wide_ref))
        turned = []
        measured()
        for slot, (far_r, far_i) in zip(slots, fars):
            far_ref[slot, 0] = far_r
            far_ref[slot, 1] = far_i
            residue = far_r * far_r + far_i * far_i - measured_ref[slot].astype(jnp.float32)
            turned.append((residue * far_i, residue * far_r))
        sent += outgoing(
            [far_ref.at[span]], [far_any.at[span]], out_sems, 7 + 3 * (first // 2)
        )
        backs = dft_pairs(turned, (left, right), (tall_ref, wide_ref))
        pieces = []
        for slot, (row, col), (back_i, back_r) in zip(slots, spots, backs):
            patch_r, patch_i = patch_ref[slot, 0], patch_ref[slot, 1]
            back_row = lax.rem(width - row, width)
            back_col = lax.rem(width - col, width)
            pieces.append(
                (
                    rolled(patch_r * back_r + patch_i * back_i, back_row, back_col),
                    rolled(patch_r * back_i - patch_i * back_r, back_row, back_col),
                )
            )
        for part in range(2):
            total = pieces[0][part] + pieces[1][part]
            for half in range(2):
                rows = pl.ds((2 * part + half) * width, width)
                side = total[:, half * (width // 2) : (half + 1) * (width // 2)]
                probe_sum_ref[rows, :] = side if first == 0 else probe_sum_ref[rows, :] + side
        for part in range(2):
            sums = [0.0, 0.0, 0.0, 0.0]
            for slot, (row, col), (back_i, back_r) in zip(slots, spots, backs):
                upper, nearer = masks(row, col, width)
                probe_r, probe_i = moved_ref[slot, 0], moved_ref[slot, 1]
                if part == 0:
                    term = probe_r * back_r + probe_i * back_i
                else:
                    term = probe_r * back_i - probe_i * back_r
                close = jnp.where(nearer, term, 0.0)
                beyond = term - close
                for at, side in enumerate((close, beyond)):
                    top = jnp.where(upper, side, 0.0)
                    sums[2 * at] = sums[2 * at] + top
                    sums[2 * at + 1] = sums[2 * at + 1] + (side - top)
            for at, total in enumerate(sums):
                grads_ref[at, part] = total if first == 0 else grads_ref[at, part] + total
        for copy in sent:
            copy.wait()

    both(0)
    pl.when(live > 2)(lambda: both(2))
    sides = [side_grad_any.at[:, pl.ds(first, width)] for first in (0, width)]
    outs = [own_grad_any, below_grad_any, *sides, probe_grad_any]
    made = [grads_ref.at[at] for at in range(4)] + [probe_sum_ref]
    for copy in outgoing(made, outs, out_sems):
        copy.wait()


def linear_frames(positions_ref, live, tiles, change, kept, tables, scratch, finish):
    own_ref, below_ref, right_ref, diag_ref = [tile() for tile in tiles]
    change_ref = change()
    width = own_ref.shape[-1]

    def both(first, patches, moves, fars):
        slots = (first, first + 1)
        patch_ref, moved_ref = patches(), moves()
        waves = []
        for at, slot in enumerate(slots):
            row, col = corner(positions_ref, slot, width)
            upper, nearer = masks(row, col, width)
            step_r, step_i = [
                wrapped(own_ref[part], below_ref[part], right_ref[part], diag_ref[part], upper, nearer)
                for part in range(2)
            ]
            patch_r, patch_i = patch_ref[at, 0], patch_ref[at, 1]
            probe_r, probe_i = moved_ref[at, 0], moved_ref[at, 1]
            change_r = rolled(change_ref[0], row, col)
            change_i = rolled(change_ref[1], row, col)
            waves.append(
                (
                    probe_r * step_r - probe_i * step_i + change_r * patch_r - change_i * patch_i,
                    probe_r * step_i + probe_i * step_r + change_r * patch_i + change_i * patch_r,
                )
            )
        steps = dft_pairs(waves, tables, scratch)
        far_ref = fars()
        quads = [
            2.0 * (far_ref[at, 0] * step_r + far_ref[at, 1] * step_i)
            for at, (step_r, step_i) in enumerate(steps)
        ]
        finish(slots, quads)

    both(0, *kept[0])
    for arrival in kept[1]:
        arrival()
    pl.when(live > 2)(lambda: both(2, *kept[1]))


def halves(array, ref):
    return [(array.at[pl.ds(first, 2)], ref.at[pl.ds(first, 2)]) for first in (0, 2)]


def joined_kernel(*refs):
    *sources, out_any, held_ref, in_sems, out_sem = refs
    count = len(sources)
    width = held_ref.shape[-1]
    sources = [
        source if source.shape[1] == width else source.at[:, pl.ds(width, width)]
        for source in sources
    ]
    arrivals = incoming(sources, [held_ref.at[at] for at in range(count)], in_sems)
    for arrival in arrivals:
        arrival()
    if count > 1:
        held_ref[0] = sum((held_ref[at] for at in range(1, count)), held_ref[0])
    copy = pltpu.make_async_copy(held_ref.at[0], out_any, out_sem)
    copy.start()
    copy.wait()


def curvature_kernel(
    positions_ref,
    counts_ref,
    prev_norm_ref,
    own_any,
    below_any,
    right_any,
    diag_any,
    prev_own_any,
    prev_below_any,
    prev_right_any,
    prev_diag_any,
    total_any,
    patch_any,
    moved_any,
    far_any,
    left_any,
    right_table_any,
    prev_probe_any,
    direction_any,
    probe_direction_any,
    sums_ref,
    tiles_ref,
    prev_tiles_ref,
    total_ref,
    change_ref,
    patch_ref,
    moved_ref,
    far_ref,
    left_ref,
    right_ref,
    prev_probe_ref,
    tall_ref,
    wide_ref,
    in_sems,
    out_sems,
    *,
    probe_scale,
    pieces,
):
    live = live_count(counts_ref)
    width = change_ref.shape[-1]
    kept = [
        halves(patch_any, patch_ref),
        halves(moved_any, moved_ref),
        halves(far_any, far_ref),
    ]
    moves = [(total_any, total_ref), (prev_probe_any, prev_probe_ref)]
    for group, target in (
        ((own_any, below_any, right_any, diag_any), tiles_ref),
        ((prev_own_any, prev_below_any, prev_right_any, prev_diag_any), prev_tiles_ref),
    ):
        moves += [(tile, target.at[at]) for at, tile in enumerate(group)]
    moves += [kept[0][0], kept[1][0], (left_any, left_ref), (right_table_any, right_ref), kept[2][0]]
    moves += [kept[0][1], kept[1][1], kept[2][1]]
    total, prev_probe, *arrivals = incoming(*zip(*moves), in_sems)
    tiles, prev_tiles = arrivals[:4], arrivals[4:8]
    (patch, moved, left, right, far), later = arrivals[8:13], arrivals[13:]

    total()
    depth = 4 * width // pieces
    products = jnp.zeros((2, total_ref.shape[-1]), jnp.float32)
    for piece in range(pieces):
        base = piece * (depth + 2)
        part, rest = divmod(piece * depth, 2 * width)
        half, first = divmod(rest, width)
        lanes = slice(half * (width // 2), (half + 1) * (width // 2))
        change_ref[part, first : first + depth, lanes] = (
            total_ref[base : base + depth, :] * probe_scale
        )
        products = products + total_ref[base + depth : base + depth + 2, :]
    lane = lax.broadcasted_iota(jnp.int32, (1, 128), 1)
    probe_grad = change_ref[...]
    prev_probe()
    grad_norm = whole_sum(products[:1]) + whole_sum(probe_grad * probe_grad)
    along_prev = whole_sum(products[1:]) + whole_sum(probe_grad * prev_probe_ref[...])
    ratio = grad_norm / prev_norm_ref[0]
    descent = grad_norm - ratio * along_prev
    change_ref[...] = ratio * prev_probe_ref[...] - change_ref[...]
    for at, (tile, prev) in enumerate(zip(tiles, prev_tiles)):
        tile()
        prev()
        tiles_ref[at] = ratio * prev_tiles_ref[at] - tiles_ref[at]
    sent = outgoing(
        [tiles_ref.at[0], change_ref], [direction_any, probe_direction_any], out_sems
    )
    row = jnp.where(lane == 5, grad_norm, jnp.where(lane == 6, descent, 0.0))
    sums_ref[...] = row

    def finish(slots, quads):
        row = sums_ref[...]
        for slot, quad in zip(slots, quads):
            square = whole_sum(quad * quad)
            row = row + jnp.where((lane == 0) | (lane == 1 + slot), square, 0.0)
        sums_ref[...] = row

    linear_frames(
        positions_ref,
        live,
        [(lambda at=at: tiles_ref.at[at]) for at in range(4)],
        lambda: change_ref,
        ((patch, moved, far), later),
        (left, right),
        (tall_ref, wide_ref),
        finish,
    )
    for copy in sent:
        copy.wait()


def update_kernel(
    gathered_any,
    sums_any,
    object_any,
    direction_any,
    probe_any,
    probe_direction_any,
    object_new_any,
    probe_new_any,
    norm_ref,
    frames_ref,
    gathered_ref,
    sums_ref,
    held_ref,
    in_sems,
    out_sems,
):
    sources = [gathered_any, sums_any, object_any, direction_any, probe_any, probe_direction_any]
    targets = [gathered_ref, sums_ref] + [held_ref.at[at] for at in range(4)]
    gathered, sums, *arrivals = incoming(sources, targets, in_sems)
    total = jnp.sum(gathered()[...], axis=0)
    local = sums()[...]
    lane = lax.broadcasted_iota(jnp.int32, (1, 128), 1)

    def pick(row, at):
        return jnp.sum(jnp.where(lane == at, row, 0.0), axis=1, keepdims=True)

    curvature = pick(total, 0)
    step_size = pick(local, 6) / (0.5 * curvature + 1e-06)
    outs = [object_new_any, probe_new_any]
    sent = []
    for which in range(2):
        field, direction = [arrival() for arrival in arrivals[2 * which : 2 * which + 2]]
        field[...] = field[...] + step_size * direction[...]
        sent += outgoing([field], [outs[which]], out_sems, which)
    norm_ref[...] = pick(local, 5)
    pixels = held_ref.shape[-1] * held_ref.shape[-2]
    frames_ref[0] = local[:, 1 : 1 + frames_ref.shape[-1]] / pixels
    for copy in sent:
        copy.wait()


def whole_sum(value):
    return jnp.sum(jnp.sum(value, axis=tuple(range(value.ndim - 1)))[None], axis=1, keepdims=True)


def shaped(*dims):
    return jax.ShapeDtypeStruct(dims, jnp.float32)


def buffer(*dims, dtype=jnp.float32):
    return pltpu.VMEM(dims, dtype)


def arrivals_of(count):
    return pltpu.SemaphoreType.DMA((count,))


def anywhere(count):
    return [pl.BlockSpec(memory_space=pl.ANY)] * count


def in_hbm(count):
    return [pl.BlockSpec(memory_space=pltpu.HBM)] * count


def in_vmem(count):
    return [pl.BlockSpec(memory_space=pltpu.VMEM)] * count


def in_smem(count):
    return [pl.BlockSpec(memory_space=pltpu.SMEM)] * count


def table_buffers(width):
    return [
        buffer(3, width, 3 * width, dtype=jnp.bfloat16),
        buffer(3, 3 * width, width, dtype=jnp.bfloat16),
    ]


def dft_scratch(width):
    return [
        buffer(2, 3, 3 * width, width, dtype=jnp.bfloat16),
        buffer(2, 3, width, 3 * width, dtype=jnp.bfloat16),
    ]


def costing(flops, mebibytes=60):
    return {
        "compiler_params": pltpu.CompilerParams(vmem_limit_bytes=mebibytes * 2**20),
        "cost_estimate": pl.CostEstimate(flops=flops, bytes_accessed=10**7, transcendentals=0),
    }


def gradient_call(positions, counts, tiles, probe, measured, tables):
    width = probe.shape[-1]
    slots = measured.shape[2]
    frames = buffer(slots, 2, width, width)
    return pl.pallas_call(
        gradient_kernel,
        out_shape=(shaped(2, width, width),) * 2
        + (shaped(2, 2 * width, width), shaped(4 * width, width // 2))
        + (shaped(slots, 2, width, width),) * 3,
        in_specs=in_smem(2) + anywhere(4) + in_hbm(4),
        out_specs=(*anywhere(4), *in_hbm(3)),
        scratch_shapes=[
            buffer(4, 2, width, width),
            buffer(2, width, width),
            buffer(slots, width, width, dtype=measured.dtype),
            *table_buffers(width),
            buffer(4, 2, width, width),
            buffer(4 * width, width // 2),
            frames,
            frames,
            frames,
            *dft_scratch(width),
            arrivals_of(8),
            arrivals_of(11),
        ],
        name="gradient_frames",
        **costing(10**10, 60),
    )(positions, counts, *tiles, probe, measured, *tables)


def joined_call(arrays, flops):
    shape = arrays[0].shape
    return pl.pallas_call(
        joined_kernel,
        out_shape=shaped(*shape),
        in_specs=anywhere(len(arrays)),
        out_specs=anywhere(1)[0],
        scratch_shapes=[
            buffer(len(arrays), *shape),
            arrivals_of(len(arrays)),
            pltpu.SemaphoreType.DMA,
        ],
        name="joined",
        **costing(flops, 4),
    )(*arrays)


def curvature_call(positions, counts, prev_norm, tiles, total, pieces, kept, tables, probe_prev, scale):
    width = tiles[0].shape[-1]
    slots = kept[0].shape[0]
    frames = buffer(slots, 2, width, width)
    return pl.pallas_call(
        functools.partial(curvature_kernel, probe_scale=scale, pieces=pieces),
        out_shape=(shaped(2, width, width), shaped(2, width, width), shaped(1, 128)),
        in_specs=in_smem(3) + anywhere(9) + in_hbm(6),
        out_specs=(*in_hbm(2), *in_vmem(1)),
        scratch_shapes=[
            buffer(4, 2, width, width),
            buffer(4, 2, width, width),
            buffer(*total.shape),
            buffer(2, width, width),
            frames,
            frames,
            frames,
            *table_buffers(width),
            buffer(2, width, width),
            *dft_scratch(width),
            arrivals_of(18),
            arrivals_of(2),
        ],
        name="curvature_frames",
        **costing(5 * 10**9),
    )(positions, counts, prev_norm, *tiles, total, *kept, *tables, probe_prev)


def update_call(gathered, sums, arrays, slots):
    shape = arrays[0].shape
    return pl.pallas_call(
        update_kernel,
        out_shape=(shaped(*shape),) * 2 + (shaped(1, 1), shaped(1, 1, slots)),
        in_specs=anywhere(2) + in_hbm(4),
        out_specs=(*in_hbm(2), *in_vmem(2)),
        scratch_shapes=[
            buffer(*gathered.shape),
            buffer(*sums.shape),
            buffer(4, *shape),
            arrivals_of(6),
            arrivals_of(2),
        ],
        name="update",
        **costing(10**6),
    )(gathered, sums, *arrays)


def passed_along(shard, axis, by):
    count = lax.axis_size(axis)
    pairs = [(i, i + by) for i in range(count) if 0 <= i + by < count]
    return lax.ppermute(shard, axis, pairs)


def device_groups(block):
    rows, cols = lax.axis_size("row"), lax.axis_size("col")
    near = [
        [row * cols + first + at for row in range(rows) for at in range(block)]
        for first in range(0, cols, block)
    ]
    return near, [list(members) for members in zip(*near)]


def exchanged(pieces, groups):
    return lax.all_to_all(pieces, ("row", "col"), 0, 0, axis_index_groups=groups)


def copies(piece, groups):
    return jnp.broadcast_to(piece[None], (len(groups[0]),) + piece.shape)


def held(value, *others):
    return lax.optimization_barrier((value,) + others)[0]


def per_device(
    object_field,
    probe_field,
    object_dir_prev,
    probe_dir_prev,
    prev_norm,
    intensities,
    positions,
    counts,
):
    width = probe_field.shape[-1]
    slots = positions.shape[2]
    tables = dft_blocks(width)
    probe_scale = 1.0 / math.sqrt(slots * lax.axis_size("row") * lax.axis_size("col"))
    near, apart = device_groups(4)

    right = passed_along(object_field, "col", -1)
    below = passed_along(object_field, "row", -1)
    diag = passed_along(below, "col", -1)
    prev = held(object_dir_prev, below)
    prev_below = passed_along(prev, "row", -1)
    prev_right = passed_along(prev, "col", -1)

    own_grad, below_grad, side_grad, probe_part, *kept = gradient_call(
        positions,
        counts,
        (object_field, below, right, diag),
        probe_field,
        intensities,
        tables,
    )
    side_grad, probe_part, prev_below, prev_right = lax.optimization_barrier(
        (side_grad, probe_part, prev_below, prev_right)
    )
    from_left = passed_along(side_grad, "col", 1)
    pieces = exchanged(probe_part.reshape((len(near[0]), -1, width // 2)), near)
    below_sum = joined_call((below_grad, from_left), 10**10)
    from_above = passed_along(below_sum, "row", 1)
    prev_diag = passed_along(held(prev_below, below_sum), "col", -1)
    object_grad = own_grad + from_left[:, :width] + from_above
    sums = [
        jnp.sum(jnp.sum(object_grad * other, axis=(0, 1)).reshape(2, -1), axis=0, keepdims=True)
        for other in (object_grad, object_dir_prev)
    ]
    payload = copies(jnp.concatenate([jnp.sum(pieces, axis=0), *sums], axis=0), apart)
    object_grad, prev_diag = lax.optimization_barrier((object_grad, prev_diag))
    grad_below = passed_along(object_grad, "row", -1)
    grad_right = passed_along(object_grad, "col", -1)
    payload, grad_below = lax.optimization_barrier((exchanged(payload, apart), grad_below))
    grad_right = joined_call((grad_right,), 10**9)
    grad_diag = passed_along(grad_below, "col", -1)
    grad_diag = joined_call((grad_diag,), 2 * 10**10)
    payload = jnp.sum(payload, axis=0)[:, None, :]
    total = exchanged(copies(payload, near), near)
    object_direction, probe_direction, sums = curvature_call(
        positions,
        counts,
        prev_norm.reshape(1),
        (object_grad, grad_below, grad_right, grad_diag)
        + (object_dir_prev, prev_below, prev_right, prev_diag),
        total.reshape(-1, width // 2),
        len(near[0]),
        kept,
        tables,
        probe_dir_prev,
        probe_scale,
    )
    near, apart = device_groups(2)
    across = jnp.sum(exchanged(copies(sums, near), near), axis=0)
    across = exchanged(copies(across, apart), apart)
    object_new, probe_new, norm, frame_curvature = update_call(
        across, sums, (object_field, object_direction, probe_field, probe_direction), slots
    )
    return (
        object_new,
        probe_new,
        object_direction,
        probe_direction,
        norm.reshape(()),
        frame_curvature,
    )


def solution(mesh):
    return jax.shard_map(
        per_device,
        mesh=mesh,
        in_specs=(
            P(None, "row", "col"),
            P(),
            P(None, "row", "col"),
            P(),
            P(),
            P("row", "col", None, None, None),
            P("row", "col", None, None),
            P("row", None),
        ),
        out_specs=(
            P(None, "row", "col"),
            P(),
            P(None, "row", "col"),
            P(),
            P(),
            P("row", "col", None),
        ),
        check_vma=False,
    )
```
